32 devices in a mesh: groups: 2 (over y), expert: 4 (over z), tensor: 4 (over x, core).
Axes of the slice: x: 2, y: 2, z: 4, core: 2. Of those that a mesh axis runs over, the one named last changes fastest.
Arguments:
- tokens: bfloat16 [512, 3072], P(('groups', 'expert'), 'tensor'), parts along dimension 0, may hold values from -6 to 6
- expert_ids: int32 [512, 2], P(('groups', 'expert')), parts along dimension 0, may hold values from 0 to 3, all different within a row; in each aligned block of 64 rows (0 to 63, 64 to 127, ...) at most 34 rows name the same one
- gate_probs: float32 [512, 2], P(('groups', 'expert')), parts along dimension 0, may hold values from 0.2 to 1
- out_grad: bfloat16 [512, 3072], P(('groups', 'expert'), 'tensor'), parts along dimension 0, may hold values from -1.5 to 1.5
- gate_weight: bfloat16 [4, 3072, 8192], P('expert', None, 'tensor'), may hold values from -0.109375 to 0.109375
- up_weight: bfloat16 [4, 3072, 8192], P('expert', None, 'tensor'), may hold values from -0.109375 to 0.109375
- down_weight: bfloat16 [4, 8192, 3072], P('expert', None, 'tensor'), may hold values from -0.0625 to 0.0625
Outputs:
- mixed: bfloat16 [512, 3072], P(('groups', 'expert'), 'tensor'), parts along dimension 0
- gate_grad: float32 [512, 2], P(('groups', 'expert')), parts along dimension 0
The draws below stay inside these ranges and needn't reach their ends.
There are 2 independent parts, one for each index of `groups`. The reference program is written for one: setup_inputs(seed, part) draws one part's arguments, and reference() takes and returns one part's arrays. A program takes and returns all parts, laid end to end along the dimension named above; an argument that names none is the same for every part. Nothing has to cross between parts.
Inputs may be any that keep to these rules, and one draw needn't show every extreme that they name: `expert_ids`: each token names 2 different experts; among the 64 rows of one device no expert is named by more than 34 rows.
All inputs are finite; a program needn't handle non-finite values.
Results may differ from the reference program's by a relative error of at most 0.005.
Values may be sent and summed in bfloat16 or wider, within the bound.
No kernel may reach another device: no remote copies, remote signals or barrier semaphores. Data moves between devices by JAX's collectives and lax.ppermute only.
A program may use at most 128 MiB of HBM per device.

```python
import math
import jax
import jax.numpy as jnp
import numpy as np

D = 3072
FF = 8192
EXPERTS = 4
TOPK = 2
TOK_DEV = 64
MOST = 34
SPAN = 1
TOKENS = 256


def block_scale(rng, shape, shards, low, high):
    loudness = 1.0
    for position, shards_of in shards:
        heights = jax.random.uniform(jax.random.fold_in(jax.random.fold_in(rng, 6), position), (shards_of,), jnp.float32, low / len(shards), high / len(shards))
        loudness = loudness * jnp.repeat(jnp.exp(heights), shape[position] // shards_of).reshape((-1,) + (1,) * (len(shape) - 1 - position))
    return loudness


def routed_block(own_key, own, number, rows, count, top, most, skew):
    sequence = jax.random.permutation(own_key, count)
    packed, usual = shares(count, rows * top, most, skew, True), shares(count, rows * top, most, skew, False)
    places = jnp.arange(count)

    def named(tallies, offset_by):
        used = int((tallies > 0).sum())
        fixed = max(1, used // 4)
        moved = fixed + (places - fixed + offset_by * (used - fixed)) % max(1, count - fixed)
        return jnp.zeros((count,), jnp.int32).at[sequence[jnp.where(places < fixed, places, moved)]].set(jnp.asarray(tallies, jnp.int32))

    tallies = jnp.where(number % 4 == 0, named(packed, number // 4), named(usual, number - number // 4 - 1))
    mixed = jax.random.permutation(jax.random.fold_in(own, 3), count)
    giver, sink = mixed[0:count // 2 * 2:2], mixed[1:count // 2 * 2:2]
    room = jnp.minimum(tallies[giver] - 1, most - tallies[sink]) // 2
    room = jnp.where((giver == sequence[0]) | (sink == sequence[0]) | (tallies[sink] == 0), 0, jnp.maximum(room, 0))
    moved = jax.random.randint(jax.random.fold_in(own, 4), (count // 2,), 0, 1 << 20) % (room + 1)
    tallies = tallies.at[giver].add(-moved).at[sink].add(moved)
    labels = jnp.searchsorted(jnp.cumsum(tallies), jnp.arange(rows * top), side="right").astype(jnp.int32)
    grid = labels.reshape(top, rows).T
    grid = grid[jax.random.permutation(jax.random.fold_in(own, 1), rows)]
    offset_by = jax.random.randint(jax.random.fold_in(own, 2), (rows, 1), 0, top)
    return jnp.take_along_axis(grid, (jnp.arange(top)[None, :] + offset_by) % top, axis=1)


def shares(number_of, total, reach, slope, full):
    loads = [(1 << 20) // math.isqrt(grade ** slope) + 1 for grade in range(1, number_of + 1)]
    largest = reach if full else min(reach, max(-(-total // number_of), total * loads[0] // sum(loads)))
    least = 1 if total - largest >= number_of - 1 else 0
    holding, rest = [largest] + [least] * (number_of - 1), total - largest - least * (number_of - 1)
    while rest > 0:
        movable = [i for i in range(1, number_of) if holding[i] < largest] or [i for i in range(1, number_of) if holding[i] < reach]
        whole, left = sum([loads[i] for i in movable]), rest
        for i in movable:
            more = min(reach - holding[i], max(1, left * loads[i] // whole), rest)
            holding[i] = holding[i] + more
            rest = rest - more
    return np.array(holding)


def normal_values(rng, dims, deviation, bound, split=(), held_as=jnp.bfloat16):
    factor_of = block_scale(rng, dims, split, -0.22, 0.18) if split else 1.0
    values = jax.random.normal(rng, dims, jnp.float32) * deviation * factor_of
    return jnp.minimum(jnp.maximum(values, -bound), bound).astype(held_as)


def setup_inputs(seed: int = 0, part: int = 0) -> dict:
    key_of = jax.random.split(jax.random.key(seed), 8)
    own_keys = jax.random.split(jax.random.fold_in(key_of[7], part), 8)
    tokens = normal_values(own_keys[0], (TOKENS, D), 1.0, 6.0, ((0, 4), (1, 4)))
    expert_ids_keys = jax.random.split(jax.random.fold_in(own_keys[1], 1), TOKENS // TOK_DEV)
    expert_ids_turns = jax.random.permutation(jax.random.fold_in(own_keys[1], 3), TOKENS // TOK_DEV)
    expert_ids = jax.vmap(lambda own, number: routed_block(jax.random.fold_in(own_keys[1], 2), own, number, TOK_DEV, EXPERTS, TOPK, MOST, 2))(expert_ids_keys, expert_ids_turns).reshape((TOKENS, TOPK))
    gate_probs = jnp.clip(0.2 + 0.8 * jax.random.uniform(own_keys[2], (TOKENS, TOPK), jnp.float32) ** block_scale(own_keys[2], (TOKENS, TOPK), ((0, 4),), -0.2, 0.2), 0.2, 1.0)
    out_grad = normal_values(own_keys[3], (TOKENS, D), 0.25, 1.5, ((0, 4), (1, 4)))
    gate_weight = normal_values(key_of[4], (EXPERTS * SPAN, D, FF // SPAN), D ** -0.5, 0.109375, ((0, 4), (2, 4)))
    up_weight = normal_values(key_of[5], (EXPERTS * SPAN, D, FF // SPAN), D ** -0.5, 0.109375, ((0, 4), (2, 4)))
    down_weight = normal_values(key_of[6], (EXPERTS * SPAN, FF // SPAN, D), FF ** -0.5, 0.0625, ((0, 4), (2, 4)))
    return {"tokens": tokens, "expert_ids": expert_ids, "gate_probs": gate_probs, "out_grad": out_grad, "gate_weight": gate_weight, "up_weight": up_weight, "down_weight": down_weight}


def reference(tokens, expert_ids, gate_probs, out_grad, gate_weight, up_weight, down_weight):
    span_count = gate_weight.shape[0] // EXPERTS
    slab = gate_weight.shape[2]
    w_gate = gate_weight.reshape(EXPERTS, span_count, D, slab).transpose(0, 2, 1, 3).reshape(EXPERTS, D, FF)
    w_up = up_weight.reshape(EXPERTS, span_count, D, slab).transpose(0, 2, 1, 3).reshape(EXPERTS, D, FF)
    w_down = down_weight.reshape(EXPERTS, FF, D)
    hit_float = (expert_ids[:, :, None] == jnp.arange(EXPERTS, dtype=jnp.int32)[None, None, :]).astype(jnp.float32)
    route_weight = jnp.sum(hit_float * gate_probs[:, :, None], axis=1)
    grad_float = out_grad.astype(jnp.float32)
    mixed = jnp.zeros((tokens.shape[0], D), jnp.float32)
    dot_list = []
    for expert in range(EXPERTS):
        gate_pre = jnp.dot(tokens, w_gate[expert], preferred_element_type=jnp.float32)
        up_pre = jnp.dot(tokens, w_up[expert], preferred_element_type=jnp.float32)
        sigmoid_gate = jax.nn.sigmoid(gate_pre)
        hidden = (gate_pre * sigmoid_gate * up_pre).astype(jnp.bfloat16)
        expert_out = jnp.dot(hidden, w_down[expert], preferred_element_type=jnp.float32)
        mixed = mixed + route_weight[:, expert:expert + 1] * expert_out
        dot_list.append(jnp.sum(grad_float * expert_out, axis=1))
    dots = jnp.stack(dot_list, axis=1)
    gate_grad = jnp.sum(hit_float * dots[:, None, :], axis=2)
    return mixed.astype(jnp.bfloat16), gate_grad
```

```python
import functools

import jax
import jax.numpy as jnp
from jax import lax
from jax.experimental import pallas as pl
from jax.experimental.pallas import tpu as pltpu
from jax.sharding import PartitionSpec as P

EXPERTS = 4
MOST = 34
BF = jnp.bfloat16
F32 = jnp.float32
VMEM_LIMIT = 24 * 1024 * 1024
FF_TILE = 256
K_TILE = 512


def swap(value, axis, bit):
    size = lax.axis_size(axis)
    return lax.ppermute(value, axis, [(i, i ^ bit) for i in range(size)])


def select_kernel(me_ref, ids_ref, tokens_ref, *out_refs):
    rows = tokens_ref.shape[0]
    upper = (
        lax.broadcasted_iota(jnp.int32, (rows, rows), 0)
        < lax.broadcasted_iota(jnp.int32, (rows, rows), 1)
    ).astype(BF)
    slot = lax.broadcasted_iota(jnp.int32, (MOST, rows), 0)
    for step, out_ref in enumerate(out_refs):
        expert = me_ref[0] ^ step
        member = jnp.max((ids_ref[...] == expert).astype(jnp.int32), axis=0, keepdims=True)
        before = jnp.dot(
            jnp.broadcast_to(member.astype(F32), (16, rows)).astype(BF), upper, preferred_element_type=F32
        )[:1]
        place = jnp.where(member > 0, before.astype(jnp.int32), -1)
        pick = (slot == place).astype(F32).astype(BF)
        out_ref[...] = jnp.dot(pick, tokens_ref[...], preferred_element_type=F32).astype(BF)


def select_rows(me, ids_t, tokens):
    width = tokens.shape[1]
    vmem = pl.BlockSpec(memory_space=pltpu.VMEM)
    return pl.pallas_call(
        select_kernel,
        out_shape=[jax.ShapeDtypeStruct((MOST, width), BF)] * EXPERTS,
        in_specs=[pl.BlockSpec(memory_space=pltpu.SMEM), vmem, vmem],
        out_specs=[vmem] * EXPERTS,
        name="select_rows",
    )(me, ids_t, tokens)


def hidden_kernel(parts, t_ref, *refs):
    x_refs = refs[:parts]
    gate_ref, up_ref, out_ref = refs[parts:]
    depth = x_refs[0].shape[1]
    gate = up = None
    for j in range(parts):
        at = pl.ds(pl.multiple_of((t_ref[0] ^ j) * depth, depth), depth)
        x = x_refs[j][...]
        g = jnp.dot(x, gate_ref[0, at, :], preferred_element_type=F32)
        u = jnp.dot(x, up_ref[0, at, :], preferred_element_type=F32)
        gate = g if gate is None else gate + g
        up = u if up is None else up + u
    out_ref[...] = (gate * jax.nn.sigmoid(gate) * up).astype(BF)


def hidden_part(t, xs, gate_weight, up_weight, start, size):
    rows = xs[0].shape[0]
    depth = gate_weight.shape[1]
    first = start // FF_TILE
    whole = lambda x: pl.BlockSpec(x.shape, lambda i, t_ref: (0, 0))
    weight = pl.BlockSpec((1, depth, FF_TILE), lambda i, t_ref: (0, 0, first + i))
    return pl.pallas_call(
        functools.partial(hidden_kernel, len(xs)),
        out_shape=jax.ShapeDtypeStruct((rows, size), BF),
        grid_spec=pltpu.PrefetchScalarGridSpec(
            num_scalar_prefetch=1,
            grid=(size // FF_TILE,),
            in_specs=[whole(x) for x in xs] + [weight, weight],
            out_specs=pl.BlockSpec((rows, FF_TILE), lambda i, t_ref: (0, i)),
        ),
        compiler_params=pltpu.CompilerParams(vmem_limit_bytes=VMEM_LIMIT),
        cost_estimate=pl.CostEstimate(
            flops=4 * rows * depth * size, bytes_accessed=4 * depth * size, transcendentals=rows * size
        ),
        name="hidden_part",
    )(t, *xs, gate_weight, up_weight)


def down_kernel(count, steps, has_sum, last, where_ref, *refs):
    pieces = refs[:count]
    weight_ref = refs[count]
    rest = refs[count + 1:]
    sum_ref = rest[0] if has_sum else None
    outs = rest[1:-1] if has_sum else rest[:-1]
    total = rest[-1]
    here = pl.program_id(0)
    for number, (piece, start) in enumerate(steps):
        @pl.when(here == number)
        def _():
            term = jnp.dot(
                pieces[piece][:, start:start + K_TILE], weight_ref[0], preferred_element_type=F32
            )
            if number > 0:
                total[...] += term
            elif has_sum:
                total[...] = sum_ref[...] + term
            else:
                total[...] = term
            if number == len(steps) - 1:
                if last:
                    value = total[...]
                    for k, out in enumerate(outs):
                        out[...] = value[k * MOST:(k + 1) * MOST].astype(BF)
                else:
                    outs[0][...] = total[...]


def down_part(pieces, where, weight, running, last):
    rows = pieces[0].shape[0]
    width = weight.shape[2]
    steps = [(n, s) for n, p in enumerate(pieces) for s in range(0, p.shape[1], K_TILE)]
    whole = lambda x: pl.BlockSpec(x.shape, lambda i, w: (0, 0))
    has_sum = running is not None
    if last:
        out_shape = [jax.ShapeDtypeStruct((MOST, width), BF)] * EXPERTS
    else:
        out_shape = [jax.ShapeDtypeStruct((rows, width), F32)]
    return pl.pallas_call(
        functools.partial(down_kernel, len(pieces), steps, has_sum, last),
        out_shape=out_shape,
        grid_spec=pltpu.PrefetchScalarGridSpec(
            num_scalar_prefetch=1,
            grid=(len(steps),),
            in_specs=[whole(p) for p in pieces]
            + [pl.BlockSpec((1, K_TILE, width), lambda i, w: (0, w[i], 0))]
            + ([whole(running)] if has_sum else []),
            out_specs=[whole(o) for o in out_shape],
            scratch_shapes=[pltpu.VMEM((rows, width), F32)],
        ),
        compiler_params=pltpu.CompilerParams(vmem_limit_bytes=VMEM_LIMIT),
        cost_estimate=pl.CostEstimate(
            flops=2 * rows * width * K_TILE * len(steps),
            bytes_accessed=2 * width * K_TILE * len(steps),
            transcendentals=0,
        ),
        name="down_part",
    )(jnp.stack(where).astype(jnp.int32), *pieces, weight, *([running] if has_sum else []))


def combine_kernel(place_ref, route_ref, grad_ref, *refs):
    back_refs = refs[:EXPERTS]
    mixed_ref, dots_ref = refs[EXPERTS:]
    rows = grad_ref.shape[0]
    grad = grad_ref[...].astype(F32)
    slot = lax.broadcasted_iota(jnp.int32, (rows, MOST), 1)
    column = lax.broadcasted_iota(jnp.int32, (rows, EXPERTS), 1)
    mixed = None
    dots = jnp.zeros((rows, EXPERTS), F32)
    for k in range(EXPERTS):
        pick = (place_ref[:, k:k + 1] == slot).astype(F32).astype(BF)
        out = jnp.dot(pick, back_refs[k][...], preferred_element_type=F32)
        term = route_ref[:, k:k + 1] * out
        mixed = term if mixed is None else mixed + term
        dots = jnp.where(column == k, jnp.sum(grad * out, axis=1, keepdims=True), dots)
    mixed_ref[...] = mixed.astype(BF)
    dots_ref[...] = dots


def combine(place, route, out_grad, back):
    vmem = pl.BlockSpec(memory_space=pltpu.VMEM)
    rows = out_grad.shape[0]
    return pl.pallas_call(
        combine_kernel,
        out_shape=[
            jax.ShapeDtypeStruct(out_grad.shape, BF),
            jax.ShapeDtypeStruct((rows, EXPERTS), F32),
        ],
        in_specs=[vmem] * (3 + EXPERTS),
        out_specs=[vmem] * 2,
        name="combine",
    )(place, route, out_grad, *back)


CHUNKS = (512, 512, 512, 512)


def per_device(tokens, expert_ids, gate_probs, out_grad, gate_weight, up_weight, down_weight):
    me = lax.axis_index("expert")
    t = lax.axis_index("tensor")
    t_index = t.astype(jnp.int32).reshape(1)
    slab = gate_weight.shape[2]

    rows = select_rows(me.astype(jnp.int32).reshape(1), expert_ids.T, tokens)
    arrived = [rows[0]] + [swap(rows[k], "expert", k) for k in (1, 2, 3)]
    own = jnp.concatenate(arrived, axis=0)
    across = swap(own, "tensor", 2)
    xs = [own, swap(own, "tensor", 1), across, swap(across, "tensor", 1)]

    order = me ^ jnp.arange(EXPERTS, dtype=jnp.int32)
    hits = expert_ids[:, :, None] == order[None, None, :]
    member = jnp.sum(hits.astype(jnp.int32), axis=1)
    place = jnp.where(member > 0, jnp.cumsum(member, axis=0) - member, -1)
    route = jnp.sum(hits.astype(F32) * gate_probs[:, :, None], axis=1)

    starts = [sum(CHUNKS[:i]) for i in range(len(CHUNKS))]
    piece = {}
    for start, size in zip(starts, CHUNKS):
        h = hidden_part(t_index, xs, gate_weight, up_weight, start, size)
        far = swap(h, "tensor", 2)
        piece[start] = [h, swap(h, "tensor", 1), far, swap(far, "tensor", 1)]

    def rows_of(start, size, j):
        return [((t ^ j) * slab + start) // K_TILE + i for i in range(size // K_TILE)]

    near, near_at = [], []
    for start, size in zip(starts, CHUNKS):
        for j in (0, 1):
            near.append(piece[start][j])
            near_at += rows_of(start, size, j)
    running = down_part(near, near_at, down_weight, None, False)[0]
    for start, size in zip(starts, CHUNKS):
        last = start == starts[-1]
        result = down_part(
            piece[start][2:], rows_of(start, size, 2) + rows_of(start, size, 3), down_weight, running, last
        )
        running = result[0]
    back = [result[0]] + [swap(result[k], "expert", k) for k in (1, 2, 3)]
    mixed, dots = combine(place, route, out_grad, back)
    dots = dots + swap(dots, "tensor", 2)
    dots = dots + swap(dots, "tensor", 1)
    gate_grad = jnp.sum(hits.astype(F32) * dots[:, None, :], axis=2)
    return mixed, gate_grad


def per_device_any(tokens, expert_ids, gate_probs, out_grad, gate_weight, up_weight, down_weight):
    span_count = lax.axis_size("expert") // EXPERTS
    hits = expert_ids[:, :, None] == jnp.arange(EXPERTS, dtype=jnp.int32)[None, None, :]
    hit_float = hits.astype(F32)
    member = jnp.sum(hits.astype(jnp.int32), axis=1)
    place = jnp.cumsum(member, axis=0) - member
    placed = (place[None, :, :] == jnp.arange(MOST, dtype=jnp.int32)[:, None, None]) & (member[None, :, :] == 1)
    select = jnp.transpose(placed, (2, 0, 1)).astype(F32)
    route = jnp.sum(hit_float * gate_probs[:, :, None], axis=1)
    rows = jnp.einsum("est,td->esd", select.astype(BF), tokens, preferred_element_type=F32).astype(BF)
    arrived = lax.all_to_all(
        jnp.repeat(rows, span_count, axis=0), "expert", split_axis=0, concat_axis=0, tiled=True
    )
    full = lax.all_gather(arrived, "tensor", axis=2, tiled=True)
    gate = jnp.einsum("smd,df->smf", full, gate_weight[0], preferred_element_type=F32)
    up = jnp.einsum("smd,df->smf", full, up_weight[0], preferred_element_type=F32)
    hidden = (gate * jax.nn.sigmoid(gate) * up).astype(BF)
    partial_out = jnp.einsum(
        "smf,fd->smd",
        lax.all_gather(hidden, "tensor", axis=2, tiled=True),
        down_weight[0],
        preferred_element_type=F32,
    )
    back = lax.all_to_all(partial_out, "expert", split_axis=0, concat_axis=0, tiled=True)
    expert_out = jnp.sum(back.reshape(EXPERTS, span_count, MOST, tokens.shape[1]), axis=1)
    token_out = jnp.einsum("est,esd->ted", select, expert_out, precision=lax.Precision.HIGHEST)
    mixed = jnp.sum(route[:, :, None] * token_out, axis=1).astype(BF)
    dots = lax.psum(jnp.sum(out_grad.astype(F32)[:, None, :] * token_out, axis=2), "tensor")
    return mixed, jnp.sum(hit_float * dots[:, None, :], axis=2)


def solution(mesh):
    in_specs = (
        P(("groups", "expert"), "tensor"),
        P(("groups", "expert"), None),
        P(("groups", "expert"), None),
        P(("groups", "expert"), "tensor"),
        P("expert", None, "tensor"),
        P("expert", None, "tensor"),
        P("expert", None, "tensor"),
    )
    out_specs = (P(("groups", "expert"), "tensor"), P(("groups", "expert"), None))
    direct = mesh.shape["expert"] == EXPERTS and mesh.shape["tensor"] == 4
    return jax.shard_map(
        per_device if direct else per_device_any,
        mesh=mesh, in_specs=in_specs, out_specs=out_specs, check_vma=False,
    )
```

```python
import functools

import jax
import jax.numpy as jnp
from jax import lax
from jax.experimental import pallas as pl
from jax.experimental.pallas import tpu as pltpu
from jax.sharding import PartitionSpec as P

EXPERTS = 4
MOST = 34
BF = jnp.bfloat16
F32 = jnp.float32
VMEM_LIMIT = 24 * 1024 * 1024
SMALL_LIMIT = 4 * 1024 * 1024
FF_TILE = 256
K_TILE = 512


def swap(value, axis, bit):
    size = lax.axis_size(axis)
    return lax.ppermute(value, axis, [(i, i ^ bit) for i in range(size)])


def select_kernel(me_ref, ids_ref, tokens_ref, *out_refs):
    rows = tokens_ref.shape[0]
    upper = (
        lax.broadcasted_iota(jnp.int32, (rows, rows), 0)
        < lax.broadcasted_iota(jnp.int32, (rows, rows), 1)
    ).astype(BF)
    slot = lax.broadcasted_iota(jnp.int32, (MOST, rows), 0)
    for step, out_ref in enumerate(out_refs):
        expert = me_ref[0] ^ step
        member = jnp.max((ids_ref[...] == expert).astype(jnp.int32), axis=0, keepdims=True)
        before = jnp.dot(
            jnp.broadcast_to(member.astype(F32), (16, rows)).astype(BF), upper, preferred_element_type=F32
        )[:1]
        place = jnp.where(member > 0, before.astype(jnp.int32), -1)
        pick = (slot == place).astype(F32).astype(BF)
        out_ref[...] = jnp.dot(pick, tokens_ref[...], preferred_element_type=F32).astype(BF)


def select_rows(me, ids_t, tokens):
    width = tokens.shape[1]
    vmem = pl.BlockSpec(memory_space=pltpu.VMEM)
    return pl.pallas_call(
        select_kernel,
        out_shape=[jax.ShapeDtypeStruct((MOST, width), BF)] * EXPERTS,
        in_specs=[pl.BlockSpec(memory_space=pltpu.SMEM), vmem, vmem],
        out_specs=[vmem] * EXPERTS,
        compiler_params=pltpu.CompilerParams(vmem_limit_bytes=SMALL_LIMIT),
        cost_estimate=pl.CostEstimate(flops=1000, bytes_accessed=1000, transcendentals=0),
        name="select_rows",
    )(me, ids_t, tokens)


def hidden_kernel(parts, t_ref, *refs):
    x_refs = refs[:parts]
    gate_ref, up_ref = refs[parts:parts + 2]
    out_ref = refs[-1]
    depth = x_refs[0].shape[1]
    gate = up = None
    for j in range(parts):
        at = pl.ds(pl.multiple_of((t_ref[0] ^ j) * depth, depth), depth)
        x = x_refs[j][...]
        g = jnp.dot(x, gate_ref[0, at, :], preferred_element_type=F32)
        u = jnp.dot(x, up_ref[0, at, :], preferred_element_type=F32)
        gate = g if gate is None else gate + g
        up = u if up is None else up + u
    out_ref[...] = (gate * jax.nn.sigmoid(gate) * up).astype(BF)


def hidden_part(t, xs, gate_weight, up_weight, start, size, after=()):
    rows = xs[0].shape[0]
    depth = gate_weight.shape[1]
    first = start // FF_TILE
    whole = lambda x: pl.BlockSpec(x.shape, lambda i, t_ref: (0, 0))
    weight = pl.BlockSpec((1, depth, FF_TILE), lambda i, t_ref: (0, 0, first + i))
    return pl.pallas_call(
        functools.partial(hidden_kernel, len(xs)),
        out_shape=jax.ShapeDtypeStruct((rows, size), BF),
        grid_spec=pltpu.PrefetchScalarGridSpec(
            num_scalar_prefetch=1,
            grid=(size // FF_TILE,),
            in_specs=[whole(x) for x in xs] + [weight, weight] + [pl.BlockSpec(memory_space=pl.ANY)] * len(after),
            out_specs=pl.BlockSpec((rows, FF_TILE), lambda i, t_ref: (0, i)),
        ),
        compiler_params=pltpu.CompilerParams(vmem_limit_bytes=VMEM_LIMIT),
        cost_estimate=pl.CostEstimate(flops=1000, bytes_accessed=1000, transcendentals=0),
        name="hidden_part",
    )(t, *xs, gate_weight, up_weight, *after)


def down_kernel(count, steps, has_sum, last, where_ref, *refs):
    pieces = refs[:count]
    weight_ref = refs[count]
    rest = refs[count + 1:]
    sum_ref = rest[0] if has_sum else None
    outs = rest[1:-1] if has_sum else rest[:-1]
    total = rest[-1]
    here = pl.program_id(0)
    for number, (piece, start) in enumerate(steps):
        @pl.when(here == number)
        def _():
            term = jnp.dot(
                pieces[piece][:, start:start + K_TILE], weight_ref[0], preferred_element_type=F32
            )
            if number > 0:
                total[...] += term
            elif has_sum:
                total[...] = sum_ref[...] + term
            else:
                total[...] = term
            if number == len(steps) - 1:
                if last:
                    value = total[...]
                    for k, out in enumerate(outs):
                        out[...] = value[k * MOST:(k + 1) * MOST].astype(BF)
                else:
                    outs[0][...] = total[...]


def down_part(t, slab, pieces, where, weight, running, last):
    rows = pieces[0].shape[0]
    width = weight.shape[2]
    steps = [(n, s) for n, p in enumerate(pieces) for s in range(0, p.shape[1], K_TILE)]
    at = [(where[n][0], (where[n][1] + s) // K_TILE) for n, s in steps]

    def weight_row(i, t_ref):
        row = jnp.int32(0)
        for number, (j, tile) in enumerate(at):
            row = jnp.where(i == number, (t_ref[0] ^ j) * (slab // K_TILE) + tile, row)
        return 0, row, 0

    whole = lambda x: pl.BlockSpec(x.shape, lambda i, w: (0, 0))
    has_sum = running is not None
    if last:
        out_shape = [jax.ShapeDtypeStruct((MOST, width), BF)] * EXPERTS
    else:
        out_shape = [jax.ShapeDtypeStruct((rows, width), F32)]
    return pl.pallas_call(
        functools.partial(down_kernel, len(pieces), steps, has_sum, last),
        out_shape=out_shape,
        grid_spec=pltpu.PrefetchScalarGridSpec(
            num_scalar_prefetch=1,
            grid=(len(steps),),
            in_specs=[whole(p) for p in pieces]
            + [pl.BlockSpec((1, K_TILE, width), weight_row)]
            + ([whole(running)] if has_sum else []),
            out_specs=[whole(o) for o in out_shape],
            scratch_shapes=[pltpu.VMEM((rows, width), F32)],
        ),
        compiler_params=pltpu.CompilerParams(vmem_limit_bytes=VMEM_LIMIT),
        cost_estimate=pl.CostEstimate(
            flops=4 * rows * width * K_TILE * len(steps),
            bytes_accessed=4 * width * K_TILE * len(steps),
            transcendentals=0,
        ),
        name="down_part",
    )(t, *pieces, weight, *([running] if has_sum else []))


def combine_kernel(place_ref, route_ref, grad_ref, *refs):
    back_refs = refs[:EXPERTS]
    mixed_ref, dots_ref = refs[EXPERTS:]
    rows = grad_ref.shape[0]
    grad = grad_ref[...].astype(F32)
    slot = lax.broadcasted_iota(jnp.int32, (rows, MOST), 1)
    column = lax.broadcasted_iota(jnp.int32, (rows, EXPERTS), 1)
    mixed = None
    dots = jnp.zeros((rows, EXPERTS), F32)
    for k in range(EXPERTS):
        pick = (place_ref[:, k:k + 1] == slot).astype(F32).astype(BF)
        out = jnp.dot(pick, back_refs[k][...], preferred_element_type=F32)
        term = route_ref[:, k:k + 1] * out
        mixed = term if mixed is None else mixed + term
        dots = jnp.where(column == k, jnp.sum(grad * out, axis=1, keepdims=True), dots)
    mixed_ref[...] = mixed.astype(BF)
    dots_ref[...] = dots


def combine(place, route, out_grad, back):
    vmem = pl.BlockSpec(memory_space=pltpu.VMEM)
    rows = out_grad.shape[0]
    return pl.pallas_call(
        combine_kernel,
        out_shape=[
            jax.ShapeDtypeStruct(out_grad.shape, BF),
            jax.ShapeDtypeStruct((rows, EXPERTS), F32),
        ],
        in_specs=[vmem] * (3 + EXPERTS),
        out_specs=[vmem] * 2,
        compiler_params=pltpu.CompilerParams(vmem_limit_bytes=SMALL_LIMIT),
        cost_estimate=pl.CostEstimate(flops=1000, bytes_accessed=1000, transcendentals=0),
        name="combine",
    )(place, route, out_grad, *back)


CHUNKS = (512, 512, 512, 512)


def per_device(tokens, expert_ids, gate_probs, out_grad, gate_weight, up_weight, down_weight):
    me = lax.axis_index("expert")
    t = lax.axis_index("tensor")
    t_index = t.astype(jnp.int32).reshape(1)
    slab = gate_weight.shape[2]
    gate_weight, up_weight, down_weight = (
        pltpu.with_memory_space_constraint(w, pltpu.HBM) for w in (gate_weight, up_weight, down_weight)
    )

    rows = select_rows(me.astype(jnp.int32).reshape(1), expert_ids.T, tokens)
    arrived = [rows[0]] + [swap(rows[k], "expert", k) for k in (1, 2, 3)]
    own = jnp.concatenate(arrived, axis=0)
    across = swap(own, "tensor", 2)
    xs = [own, swap(own, "tensor", 1), across, swap(across, "tensor", 1)]

    order = me ^ jnp.arange(EXPERTS, dtype=jnp.int32)
    hits = expert_ids[:, :, None] == order[None, None, :]
    member = jnp.sum(hits.astype(jnp.int32), axis=1)
    place = jnp.where(member > 0, jnp.cumsum(member, axis=0) - member, -1)
    route = jnp.sum(hits.astype(F32) * gate_probs[:, :, None], axis=1)

    starts = [sum(CHUNKS[:i]) for i in range(len(CHUNKS))]
    pieces = []
    for i, (start, size) in enumerate(zip(starts, CHUNKS)):
        after = [pieces[i - 2][2]] if i >= 2 else []
        h = hidden_part(t_index, xs, gate_weight, up_weight, start, size, after)
        far = swap(h, "tensor", 2)
        pieces.append([h, swap(h, "tensor", 1), far, swap(far, "tensor", 1)])
    running = None
    for i, start in enumerate(starts):
        use = [(i, 2), (i, 3)]
        if i == 0:
            use = [(0, 0), (0, 1)] + use
        if i + 1 < len(starts):
            use += [(i + 1, 0), (i + 1, 1)]
        result = down_part(
            t_index, slab, [pieces[n][j] for n, j in use], [(j, starts[n]) for n, j in use], down_weight, running,
            i + 1 == len(starts),
        )
        running = result[0]
    back = [result[0]] + [swap(result[k], "expert", k) for k in (1, 2, 3)]
    mixed, dots = combine(place, route, out_grad, back)
    dots = dots + swap(dots, "tensor", 2)
    dots = dots + swap(dots, "tensor", 1)
    gate_grad = jnp.sum(hits.astype(F32) * dots[:, None, :], axis=2)
    return mixed, gate_grad


def per_device_any(tokens, expert_ids, gate_probs, out_grad, gate_weight, up_weight, down_weight):
    span_count = lax.axis_size("expert") // EXPERTS
    hits = expert_ids[:, :, None] == jnp.arange(EXPERTS, dtype=jnp.int32)[None, None, :]
    hit_float = hits.astype(F32)
    member = jnp.sum(hits.astype(jnp.int32), axis=1)
    place = jnp.cumsum(member, axis=0) - member
    placed = (place[None, :, :] == jnp.arange(MOST, dtype=jnp.int32)[:, None, None]) & (member[None, :, :] == 1)
    select = jnp.transpose(placed, (2, 0, 1)).astype(F32)
    route = jnp.sum(hit_float * gate_probs[:, :, None], axis=1)
    rows = jnp.einsum("est,td->esd", select.astype(BF), tokens, preferred_element_type=F32).astype(BF)
    arrived = lax.all_to_all(
        jnp.repeat(rows, span_count, axis=0), "expert", split_axis=0, concat_axis=0, tiled=True
    )
    full = lax.all_gather(arrived, "tensor", axis=2, tiled=True)
    gate = jnp.einsum("smd,df->smf", full, gate_weight[0], preferred_element_type=F32)
    up = jnp.einsum("smd,df->smf", full, up_weight[0], preferred_element_type=F32)
    hidden = (gate * jax.nn.sigmoid(gate) * up).astype(BF)
    partial_out = jnp.einsum(
        "smf,fd->smd",
        lax.all_gather(hidden, "tensor", axis=2, tiled=True),
        down_weight[0],
        preferred_element_type=F32,
    )
    back = lax.all_to_all(partial_out, "expert", split_axis=0, concat_axis=0, tiled=True)
    expert_out = jnp.sum(back.reshape(EXPERTS, span_count, MOST, tokens.shape[1]), axis=1)
    token_out = jnp.einsum("est,esd->ted", select, expert_out, precision=lax.Precision.HIGHEST)
    mixed = jnp.sum(route[:, :, None] * token_out, axis=1).astype(BF)
    dots = lax.psum(jnp.sum(out_grad.astype(F32)[:, None, :] * token_out, axis=2), "tensor")
    return mixed, jnp.sum(hit_float * dots[:, None, :], axis=2)


def solution(mesh):
    in_specs = (
        P(("groups", "expert"), "tensor"),
        P(("groups", "expert"), None),
        P(("groups", "expert"), None),
        P(("groups", "expert"), "tensor"),
        P("expert", None, "tensor"),
        P("expert", None, "tensor"),
        P("expert", None, "tensor"),
    )
    out_specs = (P(("groups", "expert"), "tensor"), P(("groups", "expert"), None))
    direct = mesh.shape["expert"] == EXPERTS and mesh.shape["tensor"] == 4
    return jax.shard_map(
        per_device if direct else per_device_any,
        mesh=mesh, in_specs=in_specs, out_specs=out_specs, check_vma=False,
    )
```

```python
import functools

import jax
import jax.numpy as jnp
from jax import lax
from jax.experimental import pallas as pl
from jax.experimental.pallas import tpu as pltpu
from jax.sharding import PartitionSpec as P

EXPERTS = 4
MOST = 34
BF = jnp.bfloat16
F32 = jnp.float32
VMEM_LIMIT = 24 * 1024 * 1024
SMALL_LIMIT = 4 * 1024 * 1024
FF_TILE = 256
K_TILE = 512


def swap(value, axis, bit):
    size = lax.axis_size(axis)
    return lax.ppermute(value, axis, [(i, i ^ bit) for i in range(size)])


VMEM = pl.BlockSpec(memory_space=pltpu.VMEM)
SMEM = pl.BlockSpec(memory_space=pltpu.SMEM)
ANY = pl.BlockSpec(memory_space=pl.ANY)
SMALL = dict(
    compiler_params=pltpu.CompilerParams(vmem_limit_bytes=SMALL_LIMIT),
    cost_estimate=pl.CostEstimate(flops=1000, bytes_accessed=1000, transcendentals=0),
)


def routing(ids, me):
    rows = ids.shape[1]
    upper = (
        lax.broadcasted_iota(jnp.int32, (rows, rows), 0) < lax.broadcasted_iota(jnp.int32, (rows, rows), 1)
    ).astype(F32).astype(BF)
    slot = lax.broadcasted_iota(jnp.int32, (MOST, rows), 0)
    hits, picks = [], []
    for step in range(EXPERTS):
        hit = (ids == (me ^ step)).astype(F32)
        member = jnp.sum(hit, axis=0, keepdims=True)
        before = jnp.dot(
            jnp.broadcast_to(member, (16, rows)).astype(BF), upper, preferred_element_type=F32
        )[:1]
        place = jnp.where(member > 0.5, before.astype(jnp.int32), -1)
        hits.append(hit)
        picks.append((slot == place).astype(F32))
    return hits, picks


def select_kernel(me_ref, t_ref, ids_ref, tokens_ref, *out_refs):
    _, picks = routing(ids_ref[...], me_ref[0])
    for pick, out_ref in zip(picks, out_refs):
        out_ref[...] = jnp.dot(pick.astype(BF), tokens_ref[...], preferred_element_type=F32).astype(BF)


def select_rows(me, t, ids_t, tokens):
    width = tokens.shape[1]
    return pl.pallas_call(
        select_kernel,
        out_shape=[jax.ShapeDtypeStruct((MOST, width), BF)] * EXPERTS,
        in_specs=[SMEM, SMEM, VMEM, VMEM],
        out_specs=[VMEM] * EXPERTS,
        name="select_rows",
        **SMALL,
    )(me, t, ids_t, tokens)


def pack_kernel(*refs):
    blocks = refs[:EXPERTS]
    refs[-1][...] = jnp.concatenate([b[...].astype(F32) for b in blocks], axis=0).astype(BF)


def pack(blocks, after):
    return pl.pallas_call(
        pack_kernel,
        out_shape=jax.ShapeDtypeStruct((EXPERTS * MOST, blocks[0].shape[1]), BF),
        in_specs=[VMEM] * EXPERTS + [ANY] * len(after),
        out_specs=VMEM,
        name="pack",
        **SMALL,
    )(*blocks, *after)


def hold(value, after):
    return pl.pallas_call(
        lambda *refs: None,
        out_shape=jax.ShapeDtypeStruct(value.shape, value.dtype),
        in_specs=[ANY] * (1 + len(after)),
        out_specs=ANY,
        input_output_aliases={0: 0},
        name="hold",
        **SMALL,
    )(value, *after)


def load_kernel(runs, count, *refs):
    weight_refs = refs[:count]
    out_refs, sems = refs[-1 - len(runs) * count:-1], refs[-1]
    copies = []
    for n, (start, size) in enumerate(runs):
        for m, weight in enumerate(weight_refs):
            copies.append(
                pltpu.make_async_copy(
                    weight.at[0, :, pl.ds(start, size)], out_refs[n * count + m], sems.at[n * count + m]
                )
            )
    for copy in copies:
        copy.start()
    for copy in copies:
        copy.wait()


def load(weights, runs, after=()):
    depth = weights[0].shape[1]
    count = len(weights)
    moved = sum(2 * depth * size * count for _, size in runs)
    return pl.pallas_call(
        functools.partial(load_kernel, runs, count),
        out_shape=[pltpu.VMEM((depth, size), BF) for _, size in runs for _ in weights],
        in_specs=[ANY] * (count + len(after)),
        out_specs=[ANY] * (len(runs) * count),
        scratch_shapes=[pltpu.SemaphoreType.DMA((len(runs) * count,))],
        compiler_params=pltpu.CompilerParams(vmem_limit_bytes=SMALL_LIMIT),
        cost_estimate=pl.CostEstimate(flops=0, bytes_accessed=2 * moved, transcendentals=0),
        name="load",
    )(*weights, *after)


def hidden_kernel(parts, number, t_ref, *refs):
    x_refs = refs[:parts]
    gate_ref, up_ref, down_ref = refs[parts:parts + 3]
    out_ref, share_ref, sem = refs[-3:]
    slab = share_ref.shape[0]
    row = pl.multiple_of((t_ref[0] ^ number) * slab, slab)
    copy = pltpu.make_async_copy(down_ref.at[0, pl.ds(row, slab), :], share_ref, sem)
    copy.start()
    depth = x_refs[0].shape[1]
    for tile in range(0, out_ref.shape[1], FF_TILE):
        columns = slice(tile, tile + FF_TILE)
        gate = up = None
        for j in range(parts):
            at = pl.ds(pl.multiple_of((t_ref[0] ^ j) * depth, depth), depth)
            x = x_refs[j][...]
            g = jnp.dot(x, gate_ref[at, columns], preferred_element_type=F32)
            u = jnp.dot(x, up_ref[at, columns], preferred_element_type=F32)
            gate = g if gate is None else gate + g
            up = u if up is None else up + u
        out_ref[:, tile:tile + FF_TILE] = (gate * jax.nn.sigmoid(gate) * up).astype(BF)
    copy.wait()


def hidden_part(t, xs, gate_run, up_run, down_weight, number, slab, after=()):
    rows, size = xs[0].shape[0], gate_run.shape[1]
    width = down_weight.shape[2]
    return pl.pallas_call(
        functools.partial(hidden_kernel, len(xs), number),
        out_shape=[jax.ShapeDtypeStruct((rows, size), BF), pltpu.VMEM((slab, width), BF)],
        in_specs=[SMEM] + [VMEM] * (len(xs) + 2) + [ANY] * (1 + len(after)),
        out_specs=[VMEM, ANY],
        scratch_shapes=[pltpu.SemaphoreType.DMA],
        compiler_params=pltpu.CompilerParams(vmem_limit_bytes=SMALL_LIMIT),
        cost_estimate=pl.CostEstimate(flops=1000, bytes_accessed=1000, transcendentals=0),
        name="hidden_part",
    )(t, *xs, gate_run, up_run, down_weight, *after)


def down_kernel(count, where, has_sum, last, *refs):
    pieces = refs[:count]
    weight_refs = refs[count:count + EXPERTS]
    rest = refs[count + EXPERTS:]
    outs = rest[has_sum:]
    total = rest[0][...] if has_sum else None
    for piece, (j, first) in zip(pieces, where):
        size = piece.shape[1]
        term = jnp.dot(piece[...], weight_refs[j][first:first + size, :], preferred_element_type=F32)
        total = term if total is None else total + term
    if last:
        for k, out in enumerate(outs):
            out[...] = total[k * MOST:(k + 1) * MOST].astype(BF)
    else:
        outs[0][...] = total


def down_part(pieces, where, weights, running, last):
    rows = pieces[0].shape[0]
    width = weights[0].shape[1]
    has_sum = running is not None
    if last:
        out_shape = [jax.ShapeDtypeStruct((MOST, width), BF)] * EXPERTS
    else:
        out_shape = [jax.ShapeDtypeStruct((rows, width), F32)]
    return pl.pallas_call(
        functools.partial(down_kernel, len(pieces), where, has_sum, last),
        out_shape=out_shape,
        in_specs=[VMEM] * (len(pieces) + len(weights) + has_sum),
        out_specs=[VMEM] * len(out_shape),
        compiler_params=pltpu.CompilerParams(vmem_limit_bytes=SMALL_LIMIT),
        cost_estimate=pl.CostEstimate(
            flops=2 * rows * width * sum(p.shape[1] for p in pieces), bytes_accessed=1000, transcendentals=0
        ),
        name="down_part",
    )(*pieces, *weights, *([running] if has_sum else []))


def combine_kernel(me_ref, ids_ref, probs_ref, grad_ref, *refs):
    back_refs = refs[:EXPERTS]
    mixed_ref, gate_grad_ref = refs[EXPERTS:]
    rows = grad_ref.shape[0]
    hits, picks = routing(ids_ref[...], me_ref[0])
    grad = grad_ref[...].astype(F32)
    column = lax.broadcasted_iota(jnp.int32, (rows, 128), 1)
    dots = jnp.zeros((rows, 128), F32)
    routes = jnp.concatenate(
        [jnp.sum(h * probs_ref[...], axis=0, keepdims=True) for h in hits]
        + [jnp.zeros((128 - EXPERTS, rows), F32)],
        axis=0,
    )
    routes = jnp.concatenate([routes, jnp.zeros((128, 128 - rows), F32)], axis=1).T
    mixed = None
    for k in range(EXPERTS):
        out = lax.dot_general(
            picks[k].astype(BF), back_refs[k][...], (((0,), (0,)), ((), ())), preferred_element_type=F32
        )
        term = routes[:rows, k:k + 1] * out
        mixed = term if mixed is None else mixed + term
        dots = jnp.where(column == k, jnp.sum(grad * out, axis=1, keepdims=True), dots)
    mixed_ref[...] = mixed.astype(BF)
    turned = jnp.concatenate([dots, jnp.zeros((128 - rows, 128), F32)], axis=0).T
    gate_grad = None
    for k in range(EXPERTS):
        term = hits[k] * turned[k:k + 1, :rows]
        gate_grad = term if gate_grad is None else gate_grad + term
    gate_grad_ref[...] = gate_grad


def combine(me, ids_t, probs_t, out_grad, back):
    return pl.pallas_call(
        combine_kernel,
        out_shape=[
            jax.ShapeDtypeStruct(out_grad.shape, BF),
            jax.ShapeDtypeStruct(probs_t.shape, F32),
        ],
        in_specs=[SMEM] + [VMEM] * (3 + EXPERTS),
        out_specs=[VMEM] * 2,
        name="combine",
        **SMALL,
    )(me, ids_t, probs_t, out_grad, *back)


CHUNKS = (512, 512, 512, 512)


def per_device(tokens, expert_ids, gate_probs, out_grad, gate_weight, up_weight, down_weight):
    me = lax.axis_index("expert").astype(jnp.int32).reshape(1)
    t_index = lax.axis_index("tensor").astype(jnp.int32).reshape(1)
    slab = gate_weight.shape[2]
    ids_t, probs_t = expert_ids.T, gate_probs.T
    gate_weight, up_weight, down_weight = (
        pltpu.with_memory_space_constraint(w, pltpu.HBM) for w in (gate_weight, up_weight, down_weight)
    )

    rows = select_rows(me, t_index, ids_t, tokens)
    starts = [sum(CHUNKS[:i]) for i in range(len(CHUNKS))]
    runs = list(zip(starts, CHUNKS))
    half = len(runs) // 2
    loaded = list(load([gate_weight, up_weight], runs[:half], [rows[0]]))
    arrived = [rows[0]] + [swap(rows[k], "expert", k) for k in (1, 2, 3)]
    own = pack(arrived, loaded[:1])
    loaded += load([gate_weight, up_weight], runs[half:], [own])
    across = hold(swap(own, "tensor", 2), loaded[-1:])
    xs = [own, swap(own, "tensor", 1), across, swap(across, "tensor", 1)]

    pieces, shares = [], []
    for i in range(len(CHUNKS)):
        after = [pieces[i - 2][2]] if i >= 2 else loaded[2 * half:2 * half + 1]
        h, share = hidden_part(t_index, xs, loaded[2 * i], loaded[2 * i + 1], down_weight, i, slab, after)
        far = swap(h, "tensor", 2)
        pieces.append([h, swap(h, "tensor", 1), far, swap(far, "tensor", 1)])
        shares.append(share)
    running = None
    for i, start in enumerate(starts):
        use = [(i, 2), (i, 3)]
        if i == 0:
            use = [(0, 0), (0, 1)] + use
        if i + 1 < len(starts):
            use += [(i + 1, 0), (i + 1, 1)]
        result = down_part(
            [pieces[n][j] for n, j in use], [(j, starts[n]) for n, j in use], shares, running, i + 1 == len(starts)
        )
        running = result[0]
    back = [result[0]] + [swap(result[k], "expert", k) for k in (1, 2, 3)]
    mixed, gate_grad = combine(me, ids_t, probs_t, out_grad, back)
    gate_grad = gate_grad + swap(gate_grad, "tensor", 2)
    gate_grad = gate_grad + swap(gate_grad, "tensor", 1)
    return mixed, gate_grad.T


def per_device_any(tokens, expert_ids, gate_probs, out_grad, gate_weight, up_weight, down_weight):
    span_count = lax.axis_size("expert") // EXPERTS
    hits = expert_ids[:, :, None] == jnp.arange(EXPERTS, dtype=jnp.int32)[None, None, :]
    hit_float = hits.astype(F32)
    member = jnp.sum(hits.astype(jnp.int32), axis=1)
    place = jnp.cumsum(member, axis=0) - member
    placed = (place[None, :, :] == jnp.arange(MOST, dtype=jnp.int32)[:, None, None]) & (member[None, :, :] == 1)
    select = jnp.transpose(placed, (2, 0, 1)).astype(F32)
    route = jnp.sum(hit_float * gate_probs[:, :, None], axis=1)
    rows = jnp.einsum("est,td->esd", select.astype(BF), tokens, preferred_element_type=F32).astype(BF)
    arrived = lax.all_to_all(
        jnp.repeat(rows, span_count, axis=0), "expert", split_axis=0, concat_axis=0, tiled=True
    )
    full = lax.all_gather(arrived, "tensor", axis=2, tiled=True)
    gate = jnp.einsum("smd,df->smf", full, gate_weight[0], preferred_element_type=F32)
    up = jnp.einsum("smd,df->smf", full, up_weight[0], preferred_element_type=F32)
    hidden = (gate * jax.nn.sigmoid(gate) * up).astype(BF)
    partial_out = jnp.einsum(
        "smf,fd->smd",
        lax.all_gather(hidden, "tensor", axis=2, tiled=True),
        down_weight[0],
        preferred_element_type=F32,
    )
    back = lax.all_to_all(partial_out, "expert", split_axis=0, concat_axis=0, tiled=True)
    expert_out = jnp.sum(back.reshape(EXPERTS, span_count, MOST, tokens.shape[1]), axis=1)
    token_out = jnp.einsum("est,esd->ted", select, expert_out, precision=lax.Precision.HIGHEST)
    mixed = jnp.sum(route[:, :, None] * token_out, axis=1).astype(BF)
    dots = lax.psum(jnp.sum(out_grad.astype(F32)[:, None, :] * token_out, axis=2), "tensor")
    return mixed, jnp.sum(hit_float * dots[:, None, :], axis=2)


def solution(mesh):
    in_specs = (
        P(("groups", "expert"), "tensor"),
        P(("groups", "expert"), None),
        P(("groups", "expert"), None),
        P(("groups", "expert"), "tensor"),
        P("expert", None, "tensor"),
        P("expert", None, "tensor"),
        P("expert", None, "tensor"),
    )
    out_specs = (P(("groups", "expert"), "tensor"), P(("groups", "expert"), None))
    direct = mesh.shape["expert"] == EXPERTS and mesh.shape["tensor"] == 4
    return jax.shard_map(
        per_device if direct else per_device_any,
        mesh=mesh, in_specs=in_specs, out_specs=out_specs, check_vma=False,
    )
```

```python
import functools

import jax
import jax.numpy as jnp
from jax import lax
from jax.experimental import pallas as pl
from jax.experimental.pallas import tpu as pltpu
from jax.sharding import PartitionSpec as P

EXPERTS = 4
MOST = 34
BF = jnp.bfloat16
F32 = jnp.float32
VMEM_LIMIT = 24 * 1024 * 1024
SMALL_LIMIT = 4 * 1024 * 1024
FF_TILE = 256
K_TILE = 256


def swap(value, axis, bit):
    size = lax.axis_size(axis)
    return lax.ppermute(value, axis, [(i, i ^ bit) for i in range(size)])


VMEM = pl.BlockSpec(memory_space=pltpu.VMEM)
SMEM = pl.BlockSpec(memory_space=pltpu.SMEM)
ANY = pl.BlockSpec(memory_space=pl.ANY)
SMALL = dict(
    compiler_params=pltpu.CompilerParams(vmem_limit_bytes=SMALL_LIMIT),
    cost_estimate=pl.CostEstimate(flops=1000, bytes_accessed=1000, transcendentals=0),
)


def routing(ids, me):
    rows = ids.shape[1]
    upper = (
        lax.broadcasted_iota(jnp.int32, (rows, rows), 0) < lax.broadcasted_iota(jnp.int32, (rows, rows), 1)
    ).astype(F32).astype(BF)
    slot = lax.broadcasted_iota(jnp.int32, (MOST, rows), 0)
    hits, picks = [], []
    for step in range(EXPERTS):
        hit = (ids == (me ^ step)).astype(F32)
        member = jnp.sum(hit, axis=0, keepdims=True)
        before = jnp.dot(
            jnp.broadcast_to(member, (16, rows)).astype(BF), upper, preferred_element_type=F32
        )[:1]
        place = jnp.where(member > 0.5, before.astype(jnp.int32), -1)
        hits.append(hit)
        picks.append((slot == place).astype(F32))
    return hits, picks


def select_kernel(me_ref, t_ref, ids_hbm, tokens_hbm, *refs):
    out_refs = refs[:EXPERTS]
    ids_ref, tokens_ref, sems = refs[EXPERTS:]
    ids_copy = pltpu.make_async_copy(ids_hbm, ids_ref, sems.at[0])
    tokens_copy = pltpu.make_async_copy(tokens_hbm, tokens_ref, sems.at[1])
    ids_copy.start()
    tokens_copy.start()
    ids_copy.wait()
    _, picks = routing(ids_ref[...], me_ref[0])
    tokens_copy.wait()
    for pick, out_ref in zip(picks, out_refs):
        out_ref[...] = jnp.dot(pick.astype(BF), tokens_ref[...], preferred_element_type=F32).astype(BF)


def select_rows(me, t, ids_t, tokens):
    width = tokens.shape[1]
    return pl.pallas_call(
        select_kernel,
        out_shape=[jax.ShapeDtypeStruct((MOST, width), BF)] * EXPERTS,
        in_specs=[SMEM, SMEM, ANY, ANY],
        out_specs=[VMEM] * EXPERTS,
        scratch_shapes=[
            pltpu.VMEM(ids_t.shape, ids_t.dtype),
            pltpu.VMEM(tokens.shape, tokens.dtype),
            pltpu.SemaphoreType.DMA((2,)),
        ],
        name="select_rows",
        **SMALL,
    )(me, t, *(pltpu.with_memory_space_constraint(v, pltpu.HBM) for v in (ids_t, tokens)))


def pack_kernel(*refs):
    blocks = refs[:EXPERTS]
    refs[-1][...] = jnp.concatenate([b[...].astype(F32) for b in blocks], axis=0).astype(BF)


def pack(blocks, after):
    return pl.pallas_call(
        pack_kernel,
        out_shape=jax.ShapeDtypeStruct((EXPERTS * MOST, blocks[0].shape[1]), BF),
        in_specs=[VMEM] * EXPERTS + [ANY] * len(after),
        out_specs=VMEM,
        name="pack",
        **SMALL,
    )(*blocks, *after)


def hold(value, after):
    return pl.pallas_call(
        lambda *refs: None,
        out_shape=jax.ShapeDtypeStruct(value.shape, value.dtype),
        in_specs=[ANY] * (1 + len(after)),
        out_specs=ANY,
        input_output_aliases={0: 0},
        name="hold",
        **SMALL,
    )(value, *after)


def load_kernel(runs, count, *refs):
    weight_refs = refs[:count]
    out_refs, sems = refs[-1 - len(runs) * count:-1], refs[-1]
    copies = []
    for n, (start, size) in enumerate(runs):
        for m, weight in enumerate(weight_refs):
            copies.append(
                pltpu.make_async_copy(
                    weight.at[0, :, pl.ds(start, size)], out_refs[n * count + m], sems.at[n * count + m]
                )
            )
    for copy in copies:
        copy.start()
    for copy in copies:
        copy.wait()


def load(weights, runs, after=()):
    depth = weights[0].shape[1]
    count = len(weights)
    moved = sum(2 * depth * size * count for _, size in runs)
    return pl.pallas_call(
        functools.partial(load_kernel, runs, count),
        out_shape=[pltpu.VMEM((depth, size), BF) for _, size in runs for _ in weights],
        in_specs=[ANY] * (count + len(after)),
        out_specs=[ANY] * (len(runs) * count),
        scratch_shapes=[pltpu.SemaphoreType.DMA((len(runs) * count,))],
        compiler_params=pltpu.CompilerParams(vmem_limit_bytes=SMALL_LIMIT),
        cost_estimate=pl.CostEstimate(flops=0, bytes_accessed=2 * moved, transcendentals=0),
        name="load",
    )(*weights, *after)


def hidden_kernel(parts, t_ref, *refs):
    x_refs = refs[:parts]
    gate_ref, up_ref = refs[parts:parts + 2]
    out_ref = refs[-1]
    depth = x_refs[0].shape[1]
    for tile in range(0, out_ref.shape[1], FF_TILE):
        columns = slice(tile, tile + FF_TILE)
        gate = up = None
        for j in range(parts):
            at = pl.ds(pl.multiple_of((t_ref[0] ^ j) * depth, depth), depth)
            x = x_refs[j][...]
            g = jnp.dot(x, gate_ref[at, columns], preferred_element_type=F32)
            u = jnp.dot(x, up_ref[at, columns], preferred_element_type=F32)
            gate = g if gate is None else gate + g
            up = u if up is None else up + u
        out_ref[:, tile:tile + FF_TILE] = (gate * jax.nn.sigmoid(gate) * up).astype(BF)


def hidden_part(t, xs, gate_run, up_run, after=()):
    rows, size = xs[0].shape[0], gate_run.shape[1]
    return pl.pallas_call(
        functools.partial(hidden_kernel, len(xs)),
        out_shape=jax.ShapeDtypeStruct((rows, size), BF),
        in_specs=[SMEM] + [VMEM] * (len(xs) + 2) + [ANY] * len(after),
        out_specs=VMEM,
        compiler_params=pltpu.CompilerParams(vmem_limit_bytes=SMALL_LIMIT),
        cost_estimate=pl.CostEstimate(flops=1000, bytes_accessed=1000, transcendentals=0),
        name="hidden_part",
    )(t, *xs, gate_run, up_run, *after)


def down_kernel(count, where, slab, has_sum, last, t_ref, *refs):
    pieces = refs[:count]
    weight_ref = refs[count]
    rest = refs[count + 1:]
    outs = rest[has_sum:]
    total = rest[0][...] if has_sum else None
    for piece, (j, first) in zip(pieces, where):
        size = piece.shape[1]
        row = pl.multiple_of((t_ref[0] ^ j) * slab + first, K_TILE)
        term = jnp.dot(piece[...], weight_ref[0, pl.ds(row, size), :], preferred_element_type=F32)
        total = term if total is None else total + term
    if last:
        for k, out in enumerate(outs):
            out[...] = total[k * MOST:(k + 1) * MOST].astype(BF)
    else:
        outs[0][...] = total


def down_part(t, slab, pieces, where, weight, running, last):
    rows = pieces[0].shape[0]
    width = weight.shape[2]
    has_sum = running is not None
    if last:
        out_shape = [jax.ShapeDtypeStruct((MOST, width), BF)] * EXPERTS
    else:
        out_shape = [jax.ShapeDtypeStruct((rows, width), F32)]
    return pl.pallas_call(
        functools.partial(down_kernel, len(pieces), where, slab, has_sum, last),
        out_shape=out_shape,
        in_specs=[SMEM] + [VMEM] * (len(pieces) + 1 + has_sum),
        out_specs=[VMEM] * len(out_shape),
        compiler_params=pltpu.CompilerParams(vmem_limit_bytes=SMALL_LIMIT),
        cost_estimate=pl.CostEstimate(
            flops=2 * rows * width * sum(p.shape[1] for p in pieces), bytes_accessed=1000, transcendentals=0
        ),
        name="down_part",
    )(t, *pieces, weight, *([running] if has_sum else []))


def combine_kernel(me_ref, ids_ref, probs_ref, grad_ref, *refs):
    back_refs = refs[:EXPERTS]
    mixed_ref, gate_grad_ref = refs[EXPERTS:]
    rows = grad_ref.shape[0]
    hits, picks = routing(ids_ref[...], me_ref[0])
    grad = grad_ref[...].astype(F32)
    column = lax.broadcasted_iota(jnp.int32, (rows, 128), 1)
    dots = jnp.zeros((rows, 128), F32)
    routes = jnp.concatenate(
        [jnp.sum(h * probs_ref[...], axis=0, keepdims=True) for h in hits]
        + [jnp.zeros((128 - EXPERTS, rows), F32)],
        axis=0,
    )
    routes = jnp.concatenate([routes, jnp.zeros((128, 128 - rows), F32)], axis=1).T
    mixed = None
    for k in range(EXPERTS):
        out = lax.dot_general(
            picks[k].astype(BF), back_refs[k][...], (((0,), (0,)), ((), ())), preferred_element_type=F32
        )
        term = routes[:rows, k:k + 1] * out
        mixed = term if mixed is None else mixed + term
        dots = jnp.where(column == k, jnp.sum(grad * out, axis=1, keepdims=True), dots)
    mixed_ref[...] = mixed.astype(BF)
    turned = jnp.concatenate([dots, jnp.zeros((128 - rows, 128), F32)], axis=0).T
    gate_grad = None
    for k in range(EXPERTS):
        term = hits[k] * turned[k:k + 1, :rows]
        gate_grad = term if gate_grad is None else gate_grad + term
    gate_grad_ref[...] = gate_grad


def combine(me, ids_t, probs_t, out_grad, back):
    return pl.pallas_call(
        combine_kernel,
        out_shape=[
            jax.ShapeDtypeStruct(out_grad.shape, BF),
            jax.ShapeDtypeStruct(probs_t.shape, F32),
        ],
        in_specs=[SMEM] + [VMEM] * (3 + EXPERTS),
        out_specs=[VMEM] * 2,
        name="combine",
        **SMALL,
    )(me, ids_t, probs_t, out_grad, *back)


CHUNKS = (512, 512, 512, 512)


def per_device(tokens, expert_ids, gate_probs, out_grad, gate_weight, up_weight, down_weight):
    me = lax.axis_index("expert").astype(jnp.int32).reshape(1)
    t_index = lax.axis_index("tensor").astype(jnp.int32).reshape(1)
    slab = gate_weight.shape[2]
    ids_t, probs_t = expert_ids.T, gate_probs.T
    gate_weight, up_weight = (
        pltpu.with_memory_space_constraint(w, pltpu.HBM) for w in (gate_weight, up_weight)
    )

    rows = select_rows(me, t_index, ids_t, tokens)
    starts = [sum(CHUNKS[:i]) for i in range(len(CHUNKS))]
    runs = list(zip(starts, CHUNKS))
    half = len(runs) // 2
    loaded = list(load([gate_weight, up_weight], runs[:half], [rows[0]]))
    arrived = [rows[0]] + [swap(rows[k], "expert", k) for k in (1, 2, 3)]
    own = pack(arrived, loaded[:1])
    loaded += load([gate_weight, up_weight], runs[half:], [own])
    across = hold(swap(own, "tensor", 2), loaded[-1:])
    xs = [own, swap(own, "tensor", 1), across, swap(across, "tensor", 1)]

    pieces = []
    for i in range(len(CHUNKS)):
        after = [pieces[i - 2][2]] if i >= 2 else loaded[2 * half:2 * half + 1]
        h = hidden_part(t_index, xs, loaded[2 * i], loaded[2 * i + 1], after)
        pieces.append([h, swap(h, "tensor", 1), swap(h, "tensor", 2)])
    sums = []
    for i, start in enumerate(starts):
        far = hold(pieces[i][2], sums[i - 2:i - 1]) if i >= 2 else pieces[i][2]
        pieces[i] = pieces[i][:2] + [far, swap(far, "tensor", 1)]
        use = [(i, 2), (i, 3)]
        if i == 0:
            use = [(0, 0), (0, 1)] + use
        if i + 1 < len(starts):
            use += [(i + 1, 0), (i + 1, 1)]
        result = down_part(
            t_index, slab, [pieces[n][j] for n, j in use], [(j, starts[n]) for n, j in use], down_weight,
            sums[-1] if sums else None, i + 1 == len(starts),
        )
        sums.append(result[0])
    back = [result[0]] + [swap(result[k], "expert", k) for k in (1, 2, 3)]
    mixed, gate_grad = combine(me, ids_t, probs_t, out_grad, back)
    gate_grad = gate_grad + swap(gate_grad, "tensor", 2)
    gate_grad = gate_grad + swap(gate_grad, "tensor", 1)
    return mixed, gate_grad.T


def per_device_any(tokens, expert_ids, gate_probs, out_grad, gate_weight, up_weight, down_weight):
    span_count = lax.axis_size("expert") // EXPERTS
    hits = expert_ids[:, :, None] == jnp.arange(EXPERTS, dtype=jnp.int32)[None, None, :]
    hit_float = hits.astype(F32)
    member = jnp.sum(hits.astype(jnp.int32), axis=1)
    place = jnp.cumsum(member, axis=0) - member
    placed = (place[None, :, :] == jnp.arange(MOST, dtype=jnp.int32)[:, None, None]) & (member[None, :, :] == 1)
    select = jnp.transpose(placed, (2, 0, 1)).astype(F32)
    route = jnp.sum(hit_float * gate_probs[:, :, None], axis=1)
    rows = jnp.einsum("est,td->esd", select.astype(BF), tokens, preferred_element_type=F32).astype(BF)
    arrived = lax.all_to_all(
        jnp.repeat(rows, span_count, axis=0), "expert", split_axis=0, concat_axis=0, tiled=True
    )
    full = lax.all_gather(arrived, "tensor", axis=2, tiled=True)
    gate = jnp.einsum("smd,df->smf", full, gate_weight[0], preferred_element_type=F32)
    up = jnp.einsum("smd,df->smf", full, up_weight[0], preferred_element_type=F32)
    hidden = (gate * jax.nn.sigmoid(gate) * up).astype(BF)
    partial_out = jnp.einsum(
        "smf,fd->smd",
        lax.all_gather(hidden, "tensor", axis=2, tiled=True),
        down_weight[0],
        preferred_element_type=F32,
    )
    back = lax.all_to_all(partial_out, "expert", split_axis=0, concat_axis=0, tiled=True)
    expert_out = jnp.sum(back.reshape(EXPERTS, span_count, MOST, tokens.shape[1]), axis=1)
    token_out = jnp.einsum("est,esd->ted", select, expert_out, precision=lax.Precision.HIGHEST)
    mixed = jnp.sum(route[:, :, None] * token_out, axis=1).astype(BF)
    dots = lax.psum(jnp.sum(out_grad.astype(F32)[:, None, :] * token_out, axis=2), "tensor")
    return mixed, jnp.sum(hit_float * dots[:, None, :], axis=2)


def solution(mesh):
    in_specs = (
        P(("groups", "expert"), "tensor"),
        P(("groups", "expert"), None),
        P(("groups", "expert"), None),
        P(("groups", "expert"), "tensor"),
        P("expert", None, "tensor"),
        P("expert", None, "tensor"),
        P("expert", None, "tensor"),
    )
    out_specs = (P(("groups", "expert"), "tensor"), P(("groups", "expert"), None))
    direct = mesh.shape["expert"] == EXPERTS and mesh.shape["tensor"] == 4
    return jax.shard_map(
        per_device if direct else per_device_any,
        mesh=mesh, in_specs=in_specs, out_specs=out_specs, check_vma=False,
    )
```

```python
import functools

import jax
import jax.numpy as jnp
from jax import lax
from jax.experimental import pallas as pl
from jax.experimental.pallas import tpu as pltpu
from jax.sharding import PartitionSpec as P

EXPERTS = 4
MOST = 34
BF = jnp.bfloat16
F32 = jnp.float32
VMEM_LIMIT = 24 * 1024 * 1024
SMALL_LIMIT = 4 * 1024 * 1024
FF_TILE = 256
K_TILE = 256


def swap(value, axis, bit):
    size = lax.axis_size(axis)
    return lax.ppermute(value, axis, [(i, i ^ bit) for i in range(size)])


VMEM = pl.BlockSpec(memory_space=pltpu.VMEM)
SMEM = pl.BlockSpec(memory_space=pltpu.SMEM)
ANY = pl.BlockSpec(memory_space=pl.ANY)
SMALL = dict(
    compiler_params=pltpu.CompilerParams(vmem_limit_bytes=SMALL_LIMIT),
    cost_estimate=pl.CostEstimate(flops=1000, bytes_accessed=1000, transcendentals=0),
)


def routing(ids, me):
    rows = ids.shape[1]
    upper = (
        lax.broadcasted_iota(jnp.int32, (rows, rows), 0) < lax.broadcasted_iota(jnp.int32, (rows, rows), 1)
    ).astype(F32).astype(BF)
    slot = lax.broadcasted_iota(jnp.int32, (MOST, rows), 0)
    hits, picks = [], []
    for step in range(EXPERTS):
        hit = (ids == (me ^ step)).astype(F32)
        member = jnp.sum(hit, axis=0, keepdims=True)
        before = jnp.dot(
            jnp.broadcast_to(member, (16, rows)).astype(BF), upper, preferred_element_type=F32
        )[:1]
        place = jnp.where(member > 0.5, before.astype(jnp.int32), -1)
        hits.append(hit)
        picks.append((slot == place).astype(F32))
    return hits, picks


def select_kernel(me_ref, t_ref, ids_hbm, tokens_hbm, *refs):
    out_refs = refs[:EXPERTS]
    ids_ref, tokens_ref, sems = refs[EXPERTS:]
    ids_copy = pltpu.make_async_copy(ids_hbm, ids_ref, sems.at[0])
    tokens_copy = pltpu.make_async_copy(tokens_hbm, tokens_ref, sems.at[1])
    ids_copy.start()
    tokens_copy.start()
    ids_copy.wait()
    _, picks = routing(ids_ref[...], me_ref[0])
    tokens_copy.wait()
    for pick, out_ref in zip(picks, out_refs):
        out_ref[...] = jnp.dot(pick.astype(BF), tokens_ref[...], preferred_element_type=F32).astype(BF)


def select_rows(me, t, ids_t, tokens):
    width = tokens.shape[1]
    return pl.pallas_call(
        select_kernel,
        out_shape=[jax.ShapeDtypeStruct((MOST, width), BF)] * EXPERTS,
        in_specs=[SMEM, SMEM, ANY, ANY],
        out_specs=[VMEM] * EXPERTS,
        scratch_shapes=[
            pltpu.VMEM(ids_t.shape, ids_t.dtype),
            pltpu.VMEM(tokens.shape, tokens.dtype),
            pltpu.SemaphoreType.DMA((2,)),
        ],
        name="select_rows",
        compiler_params=pltpu.CompilerParams(vmem_limit_bytes=SMALL_LIMIT),
        cost_estimate=pl.CostEstimate(flops=8_000_000_000, bytes_accessed=1000, transcendentals=0),
    )(me, t, *(pltpu.with_memory_space_constraint(v, pltpu.HBM) for v in (ids_t, tokens)))


def pack_kernel(*refs):
    blocks = refs[:EXPERTS]
    refs[-1][...] = jnp.concatenate([b[...].astype(F32) for b in blocks], axis=0).astype(BF)


def pack(blocks, after):
    return pl.pallas_call(
        pack_kernel,
        out_shape=jax.ShapeDtypeStruct((EXPERTS * MOST, blocks[0].shape[1]), BF),
        in_specs=[VMEM] * EXPERTS + [ANY] * len(after),
        out_specs=VMEM,
        name="pack",
        **SMALL,
    )(*blocks, *after)


def hold(value, after):
    return pl.pallas_call(
        lambda *refs: None,
        out_shape=jax.ShapeDtypeStruct(value.shape, value.dtype),
        in_specs=[ANY] * (1 + len(after)),
        out_specs=ANY,
        input_output_aliases={0: 0},
        name="hold",
        **SMALL,
    )(value, *after)


def hidden_kernel(parts, start, t_ref, *refs):
    x_refs = refs[:parts]
    gate_ref, up_ref = refs[parts:parts + 2]
    out_ref = refs[-1]
    depth = x_refs[0].shape[1]
    for tile in range(0, out_ref.shape[1], FF_TILE):
        columns = slice(start + tile, start + tile + FF_TILE)
        gate = up = None
        for j in range(parts):
            at = pl.ds(pl.multiple_of((t_ref[0] ^ j) * depth, depth), depth)
            x = x_refs[j][...]
            g = jnp.dot(x, gate_ref[0, at, columns], preferred_element_type=F32)
            u = jnp.dot(x, up_ref[0, at, columns], preferred_element_type=F32)
            gate = g if gate is None else gate + g
            up = u if up is None else up + u
        out_ref[:, tile:tile + FF_TILE] = (gate * jax.nn.sigmoid(gate) * up).astype(BF)


def hidden_part(t, xs, gate_weight, up_weight, start, size, after=()):
    rows = xs[0].shape[0]
    return pl.pallas_call(
        functools.partial(hidden_kernel, len(xs), start),
        out_shape=jax.ShapeDtypeStruct((rows, size), BF),
        in_specs=[SMEM] + [VMEM] * (len(xs) + 2) + [ANY] * len(after),
        out_specs=VMEM,
        compiler_params=pltpu.CompilerParams(vmem_limit_bytes=SMALL_LIMIT),
        cost_estimate=pl.CostEstimate(flops=1000, bytes_accessed=1000, transcendentals=0),
        name="hidden_part",
    )(t, *xs, gate_weight, up_weight, *after)


def down_kernel(count, where, slab, has_sum, last, t_ref, *refs):
    pieces = refs[:count]
    weight_ref = refs[count]
    rest = refs[count + 1:]
    outs = rest[has_sum:]
    total = rest[0][...] if has_sum else None
    for piece, (j, first) in zip(pieces, where):
        size = piece.shape[1]
        row = pl.multiple_of((t_ref[0] ^ j) * slab + first, K_TILE)
        term = jnp.dot(piece[...], weight_ref[0, pl.ds(row, size), :], preferred_element_type=F32)
        total = term if total is None else total + term
    if last:
        for k, out in enumerate(outs):
            out[...] = total[k * MOST:(k + 1) * MOST].astype(BF)
    else:
        outs[0][...] = total


def down_part(t, slab, pieces, where, weight, running, last):
    rows = pieces[0].shape[0]
    width = weight.shape[2]
    has_sum = running is not None
    if last:
        out_shape = [jax.ShapeDtypeStruct((MOST, width), BF)] * EXPERTS
    else:
        out_shape = [jax.ShapeDtypeStruct((rows, width), F32)]
    return pl.pallas_call(
        functools.partial(down_kernel, len(pieces), where, slab, has_sum, last),
        out_shape=out_shape,
        in_specs=[SMEM] + [VMEM] * (len(pieces) + 1 + has_sum),
        out_specs=[VMEM] * len(out_shape),
        compiler_params=pltpu.CompilerParams(vmem_limit_bytes=SMALL_LIMIT),
        cost_estimate=pl.CostEstimate(
            flops=2 * rows * width * sum(p.shape[1] for p in pieces), bytes_accessed=1000, transcendentals=0
        ),
        name="down_part",
    )(t, *pieces, weight, *([running] if has_sum else []))


def combine_kernel(me_ref, ids_ref, probs_ref, grad_ref, *refs):
    back_refs = refs[:EXPERTS]
    mixed_ref, gate_grad_ref = refs[EXPERTS:]
    rows = grad_ref.shape[0]
    hits, picks = routing(ids_ref[...], me_ref[0])
    grad = grad_ref[...].astype(F32)
    column = lax.broadcasted_iota(jnp.int32, (rows, 128), 1)
    dots = jnp.zeros((rows, 128), F32)
    routes = jnp.concatenate(
        [jnp.sum(h * probs_ref[...], axis=0, keepdims=True) for h in hits]
        + [jnp.zeros((128 - EXPERTS, rows), F32)],
        axis=0,
    )
    routes = jnp.concatenate([routes, jnp.zeros((128, 128 - rows), F32)], axis=1).T
    mixed = None
    for k in range(EXPERTS):
        out = lax.dot_general(
            picks[k].astype(BF), back_refs[k][...], (((0,), (0,)), ((), ())), preferred_element_type=F32
        )
        term = routes[:rows, k:k + 1] * out
        mixed = term if mixed is None else mixed + term
        dots = jnp.where(column == k, jnp.sum(grad * out, axis=1, keepdims=True), dots)
    mixed_ref[...] = mixed.astype(BF)
    turned = jnp.concatenate([dots, jnp.zeros((128 - rows, 128), F32)], axis=0).T
    gate_grad = None
    for k in range(EXPERTS):
        term = hits[k] * turned[k:k + 1, :rows]
        gate_grad = term if gate_grad is None else gate_grad + term
    gate_grad_ref[...] = gate_grad


def combine(me, ids_t, probs_t, out_grad, back):
    return pl.pallas_call(
        combine_kernel,
        out_shape=[
            jax.ShapeDtypeStruct(out_grad.shape, BF),
            jax.ShapeDtypeStruct(probs_t.shape, F32),
        ],
        in_specs=[SMEM] + [VMEM] * (3 + EXPERTS),
        out_specs=[VMEM] * 2,
        name="combine",
        **SMALL,
    )(me, ids_t, probs_t, out_grad, *back)


CHUNKS = (512, 1024, 512)


def per_device(tokens, expert_ids, gate_probs, out_grad, gate_weight, up_weight, down_weight):
    me = lax.axis_index("expert").astype(jnp.int32).reshape(1)
    t_index = lax.axis_index("tensor").astype(jnp.int32).reshape(1)
    slab = gate_weight.shape[2]
    ids_t, probs_t = expert_ids.T, gate_probs.T

    rows = select_rows(me, t_index, ids_t, tokens)
    starts = [sum(CHUNKS[:i]) for i in range(len(CHUNKS))]
    arrived = [rows[0]] + [swap(rows[k], "expert", k) for k in (1, 2, 3)]
    own = pack(arrived, [])
    across = swap(own, "tensor", 2)
    xs = [own, swap(own, "tensor", 1), across, swap(across, "tensor", 1)]

    pieces = []
    for i, (start, size) in enumerate(zip(starts, CHUNKS)):
        after = [p[2] for p in pieces[i - 2:i - 1] if i >= 2] + [p[0] for p in pieces[-1:]]
        h = hidden_part(t_index, xs, gate_weight, up_weight, start, size, after)
        pieces.append([h, swap(h, "tensor", 1), swap(h, "tensor", 2)])
    sums = []
    for i, start in enumerate(starts):
        far = hold(pieces[i][2], sums[i - 2:i - 1]) if i >= 2 else pieces[i][2]
        pieces[i] = pieces[i][:2] + [far, swap(far, "tensor", 1)]
        use = [(i, 2), (i, 3)]
        if i == 0:
            use = [(0, 0), (0, 1)] + use
        if i + 1 < len(starts):
            use += [(i + 1, 0), (i + 1, 1)]
        result = down_part(
            t_index, slab, [pieces[n][j] for n, j in use], [(j, starts[n]) for n, j in use], down_weight,
            sums[-1] if sums else None, i + 1 == len(starts),
        )
        sums.append(result[0])
    back = [result[0]] + [swap(result[k], "expert", k) for k in (1, 2, 3)]
    mixed, gate_grad = combine(me, ids_t, probs_t, out_grad, back)
    gate_grad = gate_grad + swap(gate_grad, "tensor", 2)
    gate_grad = gate_grad + swap(gate_grad, "tensor", 1)
    return mixed, gate_grad.T


def per_device_any(tokens, expert_ids, gate_probs, out_grad, gate_weight, up_weight, down_weight):
    span_count = lax.axis_size("expert") // EXPERTS
    hits = expert_ids[:, :, None] == jnp.arange(EXPERTS, dtype=jnp.int32)[None, None, :]
    hit_float = hits.astype(F32)
    member = jnp.sum(hits.astype(jnp.int32), axis=1)
    place = jnp.cumsum(member, axis=0) - member
    placed = (place[None, :, :] == jnp.arange(MOST, dtype=jnp.int32)[:, None, None]) & (member[None, :, :] == 1)
    select = jnp.transpose(placed, (2, 0, 1)).astype(F32)
    route = jnp.sum(hit_float * gate_probs[:, :, None], axis=1)
    rows = jnp.einsum("est,td->esd", select.astype(BF), tokens, preferred_element_type=F32).astype(BF)
    arrived = lax.all_to_all(
        jnp.repeat(rows, span_count, axis=0), "expert", split_axis=0, concat_axis=0, tiled=True
    )
    full = lax.all_gather(arrived, "tensor", axis=2, tiled=True)
    gate = jnp.einsum("smd,df->smf", full, gate_weight[0], preferred_element_type=F32)
    up = jnp.einsum("smd,df->smf", full, up_weight[0], preferred_element_type=F32)
    hidden = (gate * jax.nn.sigmoid(gate) * up).astype(BF)
    partial_out = jnp.einsum(
        "smf,fd->smd",
        lax.all_gather(hidden, "tensor", axis=2, tiled=True),
        down_weight[0],
        preferred_element_type=F32,
    )
    back = lax.all_to_all(partial_out, "expert", split_axis=0, concat_axis=0, tiled=True)
    expert_out = jnp.sum(back.reshape(EXPERTS, span_count, MOST, tokens.shape[1]), axis=1)
    token_out = jnp.einsum("est,esd->ted", select, expert_out, precision=lax.Precision.HIGHEST)
    mixed = jnp.sum(route[:, :, None] * token_out, axis=1).astype(BF)
    dots = lax.psum(jnp.sum(out_grad.astype(F32)[:, None, :] * token_out, axis=2), "tensor")
    return mixed, jnp.sum(hit_float * dots[:, None, :], axis=2)


def solution(mesh):
    in_specs = (
        P(("groups", "expert"), "tensor"),
        P(("groups", "expert"), None),
        P(("groups", "expert"), None),
        P(("groups", "expert"), "tensor"),
        P("expert", None, "tensor"),
        P("expert", None, "tensor"),
        P("expert", None, "tensor"),
    )
    out_specs = (P(("groups", "expert"), "tensor"), P(("groups", "expert"), None))
    direct = mesh.shape["expert"] == EXPERTS and mesh.shape["tensor"] == 4
    return jax.shard_map(
        per_device if direct else per_device_any,
        mesh=mesh, in_specs=in_specs, out_specs=out_specs, check_vma=False,
    )
```

```python
import functools

import jax
import jax.numpy as jnp
from jax import lax
from jax.experimental import pallas as pl
from jax.experimental.pallas import tpu as pltpu
from jax.sharding import PartitionSpec as P

EXPERTS = 4
MOST = 34
BF = jnp.bfloat16
F32 = jnp.float32
VMEM_LIMIT = 24 * 1024 * 1024
SMALL_LIMIT = 4 * 1024 * 1024
FF_TILE = 256
K_TILE = 256


def swap(value, axis, bit):
    size = lax.axis_size(axis)
    return lax.ppermute(value, axis, [(i, i ^ bit) for i in range(size)])


VMEM = pl.BlockSpec(memory_space=pltpu.VMEM)
SMEM = pl.BlockSpec(memory_space=pltpu.SMEM)
ANY = pl.BlockSpec(memory_space=pl.ANY)
SMALL = dict(
    compiler_params=pltpu.CompilerParams(vmem_limit_bytes=SMALL_LIMIT),
    cost_estimate=pl.CostEstimate(flops=1000, bytes_accessed=1000, transcendentals=0),
)


def routing(ids, me):
    rows = ids.shape[1]
    upper = (
        lax.broadcasted_iota(jnp.int32, (rows, rows), 0) < lax.broadcasted_iota(jnp.int32, (rows, rows), 1)
    ).astype(F32).astype(BF)
    slot = lax.broadcasted_iota(jnp.int32, (MOST, rows), 0)
    hits, picks = [], []
    for step in range(EXPERTS):
        hit = (ids == (me ^ step)).astype(F32)
        member = jnp.sum(hit, axis=0, keepdims=True)
        before = jnp.dot(
            jnp.broadcast_to(member, (16, rows)).astype(BF), upper, preferred_element_type=F32
        )[:1]
        place = jnp.where(member > 0.5, before.astype(jnp.int32), -1)
        hits.append(hit)
        picks.append((slot == place).astype(F32))
    return hits, picks


def select_kernel(me_ref, t_ref, ids_hbm, tokens_hbm, *refs):
    out_refs = refs[:EXPERTS]
    ids_ref, tokens_ref, sems = refs[EXPERTS:]
    ids_copy = pltpu.make_async_copy(ids_hbm, ids_ref, sems.at[0])
    tokens_copy = pltpu.make_async_copy(tokens_hbm, tokens_ref, sems.at[1])
    ids_copy.start()
    tokens_copy.start()
    ids_copy.wait()
    _, picks = routing(ids_ref[...], me_ref[0])
    tokens_copy.wait()
    for pick, out_ref in zip(picks, out_refs):
        out_ref[...] = jnp.dot(pick.astype(BF), tokens_ref[...], preferred_element_type=F32).astype(BF)


def select_rows(me, t, ids_t, tokens):
    width = tokens.shape[1]
    return pl.pallas_call(
        select_kernel,
        out_shape=[jax.ShapeDtypeStruct((MOST, width), BF)] * EXPERTS,
        in_specs=[SMEM, SMEM, ANY, ANY],
        out_specs=[VMEM] * EXPERTS,
        scratch_shapes=[
            pltpu.VMEM(ids_t.shape, ids_t.dtype),
            pltpu.VMEM(tokens.shape, tokens.dtype),
            pltpu.SemaphoreType.DMA((2,)),
        ],
        name="select_rows",
        compiler_params=pltpu.CompilerParams(vmem_limit_bytes=SMALL_LIMIT),
        cost_estimate=pl.CostEstimate(flops=8_000_000_000, bytes_accessed=1000, transcendentals=0),
    )(me, t, *(pltpu.with_memory_space_constraint(v, pltpu.HBM) for v in (ids_t, tokens)))


def pack_kernel(*refs):
    blocks = refs[:EXPERTS]
    refs[-1][...] = jnp.concatenate([b[...].astype(F32) for b in blocks], axis=0).astype(BF)


def pack(blocks, after):
    return pl.pallas_call(
        pack_kernel,
        out_shape=jax.ShapeDtypeStruct((EXPERTS * MOST, blocks[0].shape[1]), BF),
        in_specs=[VMEM] * EXPERTS + [ANY] * len(after),
        out_specs=VMEM,
        name="pack",
        **SMALL,
    )(*blocks, *after)


def hold(value, after):
    return pl.pallas_call(
        lambda *refs: None,
        out_shape=jax.ShapeDtypeStruct(value.shape, value.dtype),
        in_specs=[ANY] * (1 + len(after)),
        out_specs=ANY,
        input_output_aliases={0: 0},
        name="hold",
        **SMALL,
    )(value, *after)


def hidden_kernel(parts, start, t_ref, *refs):
    x_refs = refs[:parts]
    gate_ref, up_ref = refs[parts:parts + 2]
    out_ref = refs[-1]
    depth = x_refs[0].shape[1]
    for tile in range(0, out_ref.shape[1], FF_TILE):
        columns = slice(start + tile, start + tile + FF_TILE)
        gate = up = None
        for j in range(parts):
            at = pl.ds(pl.multiple_of((t_ref[0] ^ j) * depth, depth), depth)
            x = x_refs[j][...]
            g = jnp.dot(x, gate_ref[0, at, columns], preferred_element_type=F32)
            u = jnp.dot(x, up_ref[0, at, columns], preferred_element_type=F32)
            gate = g if gate is None else gate + g
            up = u if up is None else up + u
        out_ref[:, tile:tile + FF_TILE] = (gate * jax.nn.sigmoid(gate) * up).astype(BF)


def hidden_part(t, xs, gate_weight, up_weight, start, size, after=()):
    rows = xs[0].shape[0]
    return pl.pallas_call(
        functools.partial(hidden_kernel, len(xs), start),
        out_shape=jax.ShapeDtypeStruct((rows, size), BF),
        in_specs=[SMEM] + [VMEM] * (len(xs) + 2) + [ANY] * len(after),
        out_specs=VMEM,
        compiler_params=pltpu.CompilerParams(vmem_limit_bytes=SMALL_LIMIT),
        cost_estimate=pl.CostEstimate(flops=1000, bytes_accessed=1000, transcendentals=0),
        name="hidden_part",
    )(t, *xs, gate_weight, up_weight, *after)


def down_kernel(count, where, slab, has_sum, last, t_ref, *refs):
    pieces = refs[:count]
    weight_ref = refs[count]
    rest = refs[count + 1:]
    outs = rest[has_sum:]
    total = rest[0][...] if has_sum else None
    for piece, (j, first) in zip(pieces, where):
        size = piece.shape[1]
        row = pl.multiple_of((t_ref[0] ^ j) * slab + first, K_TILE)
        term = jnp.dot(piece[...], weight_ref[0, pl.ds(row, size), :], preferred_element_type=F32)
        total = term if total is None else total + term
    if last:
        for k, out in enumerate(outs):
            out[...] = total[k * MOST:(k + 1) * MOST].astype(BF)
    else:
        outs[0][...] = total


def down_part(t, slab, pieces, where, weight, running, last):
    rows = pieces[0].shape[0]
    width = weight.shape[2]
    has_sum = running is not None
    if last:
        out_shape = [jax.ShapeDtypeStruct((MOST, width), BF)] * EXPERTS
    else:
        out_shape = [jax.ShapeDtypeStruct((rows, width), F32)]
    return pl.pallas_call(
        functools.partial(down_kernel, len(pieces), where, slab, has_sum, last),
        out_shape=out_shape,
        in_specs=[SMEM] + [VMEM] * (len(pieces) + 1 + has_sum),
        out_specs=[VMEM] * len(out_shape),
        compiler_params=pltpu.CompilerParams(vmem_limit_bytes=SMALL_LIMIT),
        cost_estimate=pl.CostEstimate(
            flops=2 * rows * width * sum(p.shape[1] for p in pieces), bytes_accessed=1000, transcendentals=0
        ),
        name="down_part",
    )(t, *pieces, weight, *([running] if has_sum else []))


def combine_kernel(me_ref, ids_ref, probs_ref, grad_ref, *refs):
    back_refs = refs[:EXPERTS]
    mixed_ref, gate_grad_ref = refs[EXPERTS:]
    rows = grad_ref.shape[0]
    hits, picks = routing(ids_ref[...], me_ref[0])
    grad = grad_ref[...].astype(F32)
    column = lax.broadcasted_iota(jnp.int32, (rows, 128), 1)
    dots = jnp.zeros((rows, 128), F32)
    routes = jnp.concatenate(
        [jnp.sum(h * probs_ref[...], axis=0, keepdims=True) for h in hits]
        + [jnp.zeros((128 - EXPERTS, rows), F32)],
        axis=0,
    )
    routes = jnp.concatenate([routes, jnp.zeros((128, 128 - rows), F32)], axis=1).T
    mixed = None
    for k in range(EXPERTS):
        out = lax.dot_general(
            picks[k].astype(BF), back_refs[k][...], (((0,), (0,)), ((), ())), preferred_element_type=F32
        )
        term = routes[:rows, k:k + 1] * out
        mixed = term if mixed is None else mixed + term
        dots = jnp.where(column == k, jnp.sum(grad * out, axis=1, keepdims=True), dots)
    mixed_ref[...] = mixed.astype(BF)
    turned = jnp.concatenate([dots, jnp.zeros((128 - rows, 128), F32)], axis=0).T
    gate_grad = None
    for k in range(EXPERTS):
        term = hits[k] * turned[k:k + 1, :rows]
        gate_grad = term if gate_grad is None else gate_grad + term
    gate_grad_ref[...] = gate_grad


def combine(me, ids_t, probs_t, out_grad, back):
    return pl.pallas_call(
        combine_kernel,
        out_shape=[
            jax.ShapeDtypeStruct(out_grad.shape, BF),
            jax.ShapeDtypeStruct(probs_t.shape, F32),
        ],
        in_specs=[SMEM] + [VMEM] * (3 + EXPERTS),
        out_specs=[VMEM] * 2,
        name="combine",
        **SMALL,
    )(me, ids_t, probs_t, out_grad, *back)


CHUNKS = (256, 512, 768, 512)


def per_device(tokens, expert_ids, gate_probs, out_grad, gate_weight, up_weight, down_weight):
    me = lax.axis_index("expert").astype(jnp.int32).reshape(1)
    t_index = lax.axis_index("tensor").astype(jnp.int32).reshape(1)
    slab = gate_weight.shape[2]
    ids_t, probs_t = expert_ids.T, gate_probs.T

    rows = select_rows(me, t_index, ids_t, tokens)
    starts = [sum(CHUNKS[:i]) for i in range(len(CHUNKS))]
    arrived = [rows[0]] + [swap(rows[k], "expert", k) for k in (1, 2, 3)]
    own = pack(arrived, [])
    across = swap(own, "tensor", 2)
    xs = [own, swap(own, "tensor", 1), across, swap(across, "tensor", 1)]

    pieces = []
    for i, (start, size) in enumerate(zip(starts, CHUNKS)):
        after = [pieces[i - 2][2]] if i >= 2 else []
        h = hidden_part(t_index, xs, gate_weight, up_weight, start, size, after)
        pieces.append([h, swap(h, "tensor", 1), swap(h, "tensor", 2)])
    sums = []
    for i, start in enumerate(starts):
        far = hold(pieces[i][2], sums[i - 2:i - 1]) if i >= 2 else pieces[i][2]
        pieces[i] = pieces[i][:2] + [far, swap(far, "tensor", 1)]
        use = [(i, 2), (i, 3)]
        if i == 0:
            use = [(0, 0), (0, 1)] + use
        if i + 1 < len(starts):
            use += [(i + 1, 0), (i + 1, 1)]
        result = down_part(
            t_index, slab, [pieces[n][j] for n, j in use], [(j, starts[n]) for n, j in use], down_weight,
            sums[-1] if sums else None, i + 1 == len(starts),
        )
        sums.append(result[0])
    back = [result[0]] + [swap(result[k], "expert", k) for k in (1, 2, 3)]
    mixed, gate_grad = combine(me, ids_t, probs_t, out_grad, back)
    gate_grad = gate_grad + swap(gate_grad, "tensor", 2)
    gate_grad = gate_grad + swap(gate_grad, "tensor", 1)
    return mixed, gate_grad.T


def per_device_any(tokens, expert_ids, gate_probs, out_grad, gate_weight, up_weight, down_weight):
    span_count = lax.axis_size("expert") // EXPERTS
    hits = expert_ids[:, :, None] == jnp.arange(EXPERTS, dtype=jnp.int32)[None, None, :]
    hit_float = hits.astype(F32)
    member = jnp.sum(hits.astype(jnp.int32), axis=1)
    place = jnp.cumsum(member, axis=0) - member
    placed = (place[None, :, :] == jnp.arange(MOST, dtype=jnp.int32)[:, None, None]) & (member[None, :, :] == 1)
    select = jnp.transpose(placed, (2, 0, 1)).astype(F32)
    route = jnp.sum(hit_float * gate_probs[:, :, None], axis=1)
    rows = jnp.einsum("est,td->esd", select.astype(BF), tokens, preferred_element_type=F32).astype(BF)
    arrived = lax.all_to_all(
        jnp.repeat(rows, span_count, axis=0), "expert", split_axis=0, concat_axis=0, tiled=True
    )
    full = lax.all_gather(arrived, "tensor", axis=2, tiled=True)
    gate = jnp.einsum("smd,df->smf", full, gate_weight[0], preferred_element_type=F32)
    up = jnp.einsum("smd,df->smf", full, up_weight[0], preferred_element_type=F32)
    hidden = (gate * jax.nn.sigmoid(gate) * up).astype(BF)
    partial_out = jnp.einsum(
        "smf,fd->smd",
        lax.all_gather(hidden, "tensor", axis=2, tiled=True),
        down_weight[0],
        preferred_element_type=F32,
    )
    back = lax.all_to_all(partial_out, "expert", split_axis=0, concat_axis=0, tiled=True)
    expert_out = jnp.sum(back.reshape(EXPERTS, span_count, MOST, tokens.shape[1]), axis=1)
    token_out = jnp.einsum("est,esd->ted", select, expert_out, precision=lax.Precision.HIGHEST)
    mixed = jnp.sum(route[:, :, None] * token_out, axis=1).astype(BF)
    dots = lax.psum(jnp.sum(out_grad.astype(F32)[:, None, :] * token_out, axis=2), "tensor")
    return mixed, jnp.sum(hit_float * dots[:, None, :], axis=2)


def solution(mesh):
    in_specs = (
        P(("groups", "expert"), "tensor"),
        P(("groups", "expert"), None),
        P(("groups", "expert"), None),
        P(("groups", "expert"), "tensor"),
        P("expert", None, "tensor"),
        P("expert", None, "tensor"),
        P("expert", None, "tensor"),
    )
    out_specs = (P(("groups", "expert"), "tensor"), P(("groups", "expert"), None))
    direct = mesh.shape["expert"] == EXPERTS and mesh.shape["tensor"] == 4
    return jax.shard_map(
        per_device if direct else per_device_any,
        mesh=mesh, in_specs=in_specs, out_specs=out_specs, check_vma=False,
    )
```

```python
import functools

import jax
import jax.numpy as jnp
from jax import lax
from jax.experimental import pallas as pl
from jax.experimental.pallas import tpu as pltpu
from jax.sharding import PartitionSpec as P

EXPERTS = 4
MOST = 34
BF = jnp.bfloat16
F32 = jnp.float32
VMEM_LIMIT = 24 * 1024 * 1024
SMALL_LIMIT = 4 * 1024 * 1024
FF_TILE = 256
K_TILE = 256


def swap(value, axis, bit):
    size = lax.axis_size(axis)
    return lax.ppermute(value, axis, [(i, i ^ bit) for i in range(size)])


VMEM = pl.BlockSpec(memory_space=pltpu.VMEM)
SMEM = pl.BlockSpec(memory_space=pltpu.SMEM)
ANY = pl.BlockSpec(memory_space=pl.ANY)
SMALL = dict(
    compiler_params=pltpu.CompilerParams(vmem_limit_bytes=SMALL_LIMIT),
    cost_estimate=pl.CostEstimate(flops=1000, bytes_accessed=1000, transcendentals=0),
)


def routing(ids, me):
    rows = ids.shape[1]
    upper = (
        lax.broadcasted_iota(jnp.int32, (rows, rows), 0) < lax.broadcasted_iota(jnp.int32, (rows, rows), 1)
    ).astype(F32).astype(BF)
    slot = lax.broadcasted_iota(jnp.int32, (MOST, rows), 0)
    hits, picks = [], []
    for step in range(EXPERTS):
        hit = (ids == (me ^ step)).astype(F32)
        member = jnp.sum(hit, axis=0, keepdims=True)
        before = jnp.dot(
            jnp.broadcast_to(member, (16, rows)).astype(BF), upper, preferred_element_type=F32
        )[:1]
        place = jnp.where(member > 0.5, before.astype(jnp.int32), -1)
        hits.append(hit)
        picks.append((slot == place).astype(F32))
    return hits, picks


def fold(block):
    return jnp.concatenate([block[:, c:c + 128] for c in range(0, block.shape[1], 128)], axis=0)


def unfold(block):
    return jnp.concatenate([block[r:r + MOST] for r in range(0, block.shape[0], MOST)], axis=1)


def folded(width):
    return jax.ShapeDtypeStruct((width // 128 * MOST, 128), BF)


def select_kernel(me_ref, t_ref, ids_hbm, tokens_hbm, *refs):
    out_refs = refs[:EXPERTS]
    ids_ref, tokens_ref, sems = refs[EXPERTS:]
    ids_copy = pltpu.make_async_copy(ids_hbm, ids_ref, sems.at[0])
    tokens_copy = pltpu.make_async_copy(tokens_hbm, tokens_ref, sems.at[1])
    ids_copy.start()
    tokens_copy.start()
    ids_copy.wait()
    _, picks = routing(ids_ref[...], me_ref[0])
    tokens_copy.wait()
    for k, (pick, out_ref) in enumerate(zip(picks, out_refs)):
        block = jnp.dot(pick.astype(BF), tokens_ref[...], preferred_element_type=F32)
        out_ref[...] = (block if k == 0 else fold(block)).astype(BF)


def select_rows(me, t, ids_t, tokens):
    width = tokens.shape[1]
    return pl.pallas_call(
        select_kernel,
        out_shape=[jax.ShapeDtypeStruct((MOST, width), BF)] + [folded(width)] * (EXPERTS - 1),
        in_specs=[SMEM, SMEM, ANY, ANY],
        out_specs=[VMEM] * EXPERTS,
        scratch_shapes=[
            pltpu.VMEM(ids_t.shape, ids_t.dtype),
            pltpu.VMEM(tokens.shape, tokens.dtype),
            pltpu.SemaphoreType.DMA((2,)),
        ],
        name="select_rows",
        compiler_params=pltpu.CompilerParams(vmem_limit_bytes=SMALL_LIMIT),
        cost_estimate=pl.CostEstimate(flops=8_000_000_000, bytes_accessed=1000, transcendentals=0),
    )(me, t, *(pltpu.with_memory_space_constraint(v, pltpu.HBM) for v in (ids_t, tokens)))


CUT = 2 * MOST // 16 * 16


def near_kernel(own_ref, next_ref, out_ref):
    both = jnp.concatenate([own_ref[...].astype(F32), unfold(next_ref[...].astype(F32))], axis=0)
    out_ref[...] = both[:CUT].astype(BF)


def far_kernel(next_ref, third_ref, fourth_ref, out_ref):
    rest = unfold(next_ref[...].astype(F32))[CUT - MOST:]
    blocks = [rest] + [unfold(r[...].astype(F32)) for r in (third_ref, fourth_ref)]
    out_ref[...] = jnp.concatenate(blocks, axis=0).astype(BF)


def pack_near(own, following):
    return pl.pallas_call(
        near_kernel,
        out_shape=jax.ShapeDtypeStruct((CUT, own.shape[1]), BF),
        in_specs=[VMEM] * 2,
        out_specs=VMEM,
        name="pack_near",
        **SMALL,
    )(own, following)


def pack_far(blocks, width):
    return pl.pallas_call(
        far_kernel,
        out_shape=jax.ShapeDtypeStruct((EXPERTS * MOST - CUT, width), BF),
        in_specs=[VMEM] * 3,
        out_specs=VMEM,
        name="pack_far",
        compiler_params=pltpu.CompilerParams(vmem_limit_bytes=SMALL_LIMIT),
        cost_estimate=pl.CostEstimate(flops=1_000_000_000, bytes_accessed=1000, transcendentals=0),
    )(*blocks)


def hold(value, after):
    return pl.pallas_call(
        lambda *refs: None,
        out_shape=jax.ShapeDtypeStruct(value.shape, value.dtype),
        in_specs=[ANY] * (1 + len(after)),
        out_specs=ANY,
        input_output_aliases={0: 0},
        name="hold",
        **SMALL,
    )(value, *after)


def hidden_kernel(joined, parts, start, t_ref, *refs):
    if joined:
        out_ref, x_ref = refs[-1], refs[0]
        gate_ref, up_ref = refs[1:3]
    else:
        out_ref, x_ref = refs[-2:]
        gate_ref, up_ref = refs[2 * parts:2 * parts + 2]
        for j in range(parts):
            x_ref[j, :CUT, :] = refs[2 * j][...]
            x_ref[j, CUT:, :] = refs[2 * j + 1][...]
    depth = x_ref.shape[2]
    for tile in range(0, out_ref.shape[1], FF_TILE):
        columns = slice(start + tile, start + tile + FF_TILE)
        gate = up = None
        for j in range(parts):
            at = pl.ds(pl.multiple_of((t_ref[0] ^ j) * depth, depth), depth)
            x = x_ref[j]
            g = jnp.dot(x, gate_ref[0, at, columns], preferred_element_type=F32)
            u = jnp.dot(x, up_ref[0, at, columns], preferred_element_type=F32)
            gate = g if gate is None else gate + g
            up = u if up is None else up + u
        out_ref[:, tile:tile + FF_TILE] = (gate * jax.nn.sigmoid(gate) * up).astype(BF)


def hidden_part(t, xs, gate_weight, up_weight, start, size, after=()):
    joined = len(xs) == 1
    parts = xs[0].shape[0] if joined else len(xs) // 2
    rows = EXPERTS * MOST
    out_shape = [jax.ShapeDtypeStruct((rows, size), BF)]
    if not joined:
        out_shape.append(jax.ShapeDtypeStruct((parts, rows, xs[0].shape[1]), BF))
    return pl.pallas_call(
        functools.partial(hidden_kernel, joined, parts, start),
        out_shape=out_shape,
        in_specs=[SMEM] + [VMEM] * (len(xs) + 2) + [ANY] * len(after),
        out_specs=[VMEM] * len(out_shape),
        compiler_params=pltpu.CompilerParams(vmem_limit_bytes=SMALL_LIMIT),
        cost_estimate=pl.CostEstimate(flops=1000, bytes_accessed=1000, transcendentals=0),
        name="hidden_part",
    )(t, *xs, gate_weight, up_weight, *after)


def down_kernel(count, where, slab, has_sum, last, t_ref, *refs):
    pieces = refs[:count]
    weight_ref = refs[count]
    rest = refs[count + 1:]
    outs = rest[has_sum:]
    total = rest[0][...] if has_sum else None
    for piece, (j, first) in zip(pieces, where):
        size = piece.shape[1]
        row = pl.multiple_of((t_ref[0] ^ j) * slab + first, K_TILE)
        term = jnp.dot(piece[...], weight_ref[0, pl.ds(row, size), :], preferred_element_type=F32)
        total = term if total is None else total + term
    if last:
        for k, out in enumerate(outs):
            block = total[k * MOST:(k + 1) * MOST]
            out[...] = (block if k == 0 else fold(block)).astype(BF)
    else:
        outs[0][...] = total


def down_part(t, slab, pieces, where, weight, running, last):
    rows = pieces[0].shape[0]
    width = weight.shape[2]
    has_sum = running is not None
    if last:
        out_shape = [jax.ShapeDtypeStruct((MOST, width), BF)] + [folded(width)] * (EXPERTS - 1)
    else:
        out_shape = [jax.ShapeDtypeStruct((rows, width), F32)]
    return pl.pallas_call(
        functools.partial(down_kernel, len(pieces), where, slab, has_sum, last),
        out_shape=out_shape,
        in_specs=[SMEM] + [VMEM] * (len(pieces) + 1 + has_sum),
        out_specs=[VMEM] * len(out_shape),
        compiler_params=pltpu.CompilerParams(vmem_limit_bytes=SMALL_LIMIT),
        cost_estimate=pl.CostEstimate(
            flops=2 * rows * width * sum(p.shape[1] for p in pieces), bytes_accessed=1000, transcendentals=0
        ),
        name="down_part",
    )(t, *pieces, weight, *([running] if has_sum else []))


def combine_kernel(me_ref, ids_ref, probs_ref, grad_ref, *refs):
    back_refs = refs[:EXPERTS]
    mixed_ref, gate_grad_ref = refs[EXPERTS:]
    rows = grad_ref.shape[0]
    hits, picks = routing(ids_ref[...], me_ref[0])
    grad = grad_ref[...].astype(F32)
    column = lax.broadcasted_iota(jnp.int32, (rows, 128), 1)
    dots = jnp.zeros((rows, 128), F32)
    routes = jnp.concatenate(
        [jnp.sum(h * probs_ref[...], axis=0, keepdims=True) for h in hits]
        + [jnp.zeros((128 - EXPERTS, rows), F32)],
        axis=0,
    )
    routes = jnp.concatenate([routes, jnp.zeros((128, 128 - rows), F32)], axis=1).T
    mixed = None
    for k in range(EXPERTS):
        block = back_refs[k][...] if k == 0 else unfold(back_refs[k][...].astype(F32)).astype(BF)
        out = lax.dot_general(
            picks[k].astype(BF), block, (((0,), (0,)), ((), ())), preferred_element_type=F32
        )
        term = routes[:rows, k:k + 1] * out
        mixed = term if mixed is None else mixed + term
        dots = jnp.where(column == k, jnp.sum(grad * out, axis=1, keepdims=True), dots)
    mixed_ref[...] = mixed.astype(BF)
    turned = jnp.concatenate([dots, jnp.zeros((128 - rows, 128), F32)], axis=0).T
    gate_grad = None
    for k in range(EXPERTS):
        term = hits[k] * turned[k:k + 1, :rows]
        gate_grad = term if gate_grad is None else gate_grad + term
    gate_grad_ref[...] = gate_grad


def combine(me, ids_t, probs_t, out_grad, back):
    return pl.pallas_call(
        combine_kernel,
        out_shape=[
            jax.ShapeDtypeStruct(out_grad.shape, BF),
            jax.ShapeDtypeStruct(probs_t.shape, F32),
        ],
        in_specs=[SMEM] + [VMEM] * (3 + EXPERTS),
        out_specs=[VMEM] * 2,
        name="combine",
        **SMALL,
    )(me, ids_t, probs_t, out_grad, *back)


Z_ORDER = (1, 2, 3)
CHUNKS = (256, 512, 768, 512)


def per_device(tokens, expert_ids, gate_probs, out_grad, gate_weight, up_weight, down_weight):
    me = lax.axis_index("expert").astype(jnp.int32).reshape(1)
    t_index = lax.axis_index("tensor").astype(jnp.int32).reshape(1)
    slab = gate_weight.shape[2]
    ids_t, probs_t = expert_ids.T, gate_probs.T

    rows = select_rows(me, t_index, ids_t, tokens)
    starts = [sum(CHUNKS[:i]) for i in range(len(CHUNKS))]
    arrived = {k: swap(rows[k], "expert", k) for k in Z_ORDER}
    near = pack_near(rows[0], arrived[1])
    near_across = swap(near, "tensor", 2)
    far = hold(pack_far([arrived[k] for k in (1, 2, 3)], tokens.shape[1]), [near_across])
    far_across = swap(far, "tensor", 2)
    sides = [swap(v, "tensor", 1) for v in (near, far, near_across)]
    far_across = hold(far_across, sides)
    xs = [near, far, sides[0], sides[1], near_across, far_across, sides[2], swap(far_across, "tensor", 1)]

    pieces = []
    for i, (start, size) in enumerate(zip(starts, CHUNKS)):
        after = [pieces[i - 2][2]] if i >= 2 else []
        h, *whole = hidden_part(t_index, xs, gate_weight, up_weight, start, size, after)
        xs = whole or xs
        pieces.append([h, swap(h, "tensor", 1), swap(h, "tensor", 2)])
    sums = []
    for i, start in enumerate(starts):
        far = hold(pieces[i][2], sums[i - 2:i - 1]) if i >= 2 else pieces[i][2]
        pieces[i] = pieces[i][:2] + [far, swap(far, "tensor", 1)]
        use = [(i, 2), (i, 3)]
        if i == 0:
            use = [(0, 0), (0, 1)] + use
        if i + 1 < len(starts):
            use += [(i + 1, 0), (i + 1, 1)]
        result = down_part(
            t_index, slab, [pieces[n][j] for n, j in use], [(j, starts[n]) for n, j in use], down_weight,
            sums[-1] if sums else None, i + 1 == len(starts),
        )
        sums.append(result[0])
    back = [result[0]] + [swap(result[k], "expert", k) for k in (1, 2, 3)]
    mixed, gate_grad = combine(me, ids_t, probs_t, out_grad, back)
    gate_grad = gate_grad + swap(gate_grad, "tensor", 2)
    gate_grad = gate_grad + swap(gate_grad, "tensor", 1)
    return mixed, gate_grad.T


def per_device_any(tokens, expert_ids, gate_probs, out_grad, gate_weight, up_weight, down_weight):
    span_count = lax.axis_size("expert") // EXPERTS
    hits = expert_ids[:, :, None] == jnp.arange(EXPERTS, dtype=jnp.int32)[None, None, :]
    hit_float = hits.astype(F32)
    member = jnp.sum(hits.astype(jnp.int32), axis=1)
    place = jnp.cumsum(member, axis=0) - member
    placed = (place[None, :, :] == jnp.arange(MOST, dtype=jnp.int32)[:, None, None]) & (member[None, :, :] == 1)
    select = jnp.transpose(placed, (2, 0, 1)).astype(F32)
    route = jnp.sum(hit_float * gate_probs[:, :, None], axis=1)
    rows = jnp.einsum("est,td->esd", select.astype(BF), tokens, preferred_element_type=F32).astype(BF)
    arrived = lax.all_to_all(
        jnp.repeat(rows, span_count, axis=0), "expert", split_axis=0, concat_axis=0, tiled=True
    )
    full = lax.all_gather(arrived, "tensor", axis=2, tiled=True)
    gate = jnp.einsum("smd,df->smf", full, gate_weight[0], preferred_element_type=F32)
    up = jnp.einsum("smd,df->smf", full, up_weight[0], preferred_element_type=F32)
    hidden = (gate * jax.nn.sigmoid(gate) * up).astype(BF)
    partial_out = jnp.einsum(
        "smf,fd->smd",
        lax.all_gather(hidden, "tensor", axis=2, tiled=True),
        down_weight[0],
        preferred_element_type=F32,
    )
    back = lax.all_to_all(partial_out, "expert", split_axis=0, concat_axis=0, tiled=True)
    expert_out = jnp.sum(back.reshape(EXPERTS, span_count, MOST, tokens.shape[1]), axis=1)
    token_out = jnp.einsum("est,esd->ted", select, expert_out, precision=lax.Precision.HIGHEST)
    mixed = jnp.sum(route[:, :, None] * token_out, axis=1).astype(BF)
    dots = lax.psum(jnp.sum(out_grad.astype(F32)[:, None, :] * token_out, axis=2), "tensor")
    return mixed, jnp.sum(hit_float * dots[:, None, :], axis=2)


def solution(mesh):
    in_specs = (
        P(("groups", "expert"), "tensor"),
        P(("groups", "expert"), None),
        P(("groups", "expert"), None),
        P(("groups", "expert"), "tensor"),
        P("expert", None, "tensor"),
        P("expert", None, "tensor"),
        P("expert", None, "tensor"),
    )
    out_specs = (P(("groups", "expert"), "tensor"), P(("groups", "expert"), None))
    direct = mesh.shape["expert"] == EXPERTS and mesh.shape["tensor"] == 4
    return jax.shard_map(
        per_device if direct else per_device_any,
        mesh=mesh, in_specs=in_specs, out_specs=out_specs, check_vma=False,
    )
```

```python
import functools

import jax
import jax.numpy as jnp
from jax import lax
from jax.experimental import pallas as pl
from jax.experimental.pallas import tpu as pltpu
from jax.sharding import PartitionSpec as P

EXPERTS = 4
MOST = 34
BF = jnp.bfloat16
F32 = jnp.float32
VMEM_LIMIT = 24 * 1024 * 1024
SMALL_LIMIT = 4 * 1024 * 1024
FF_TILE = 256
K_TILE = 256


def swap(value, axis, bit):
    size = lax.axis_size(axis)
    return lax.ppermute(value, axis, [(i, i ^ bit) for i in range(size)])


VMEM = pl.BlockSpec(memory_space=pltpu.VMEM)
SMEM = pl.BlockSpec(memory_space=pltpu.SMEM)
ANY = pl.BlockSpec(memory_space=pl.ANY)
SMALL = dict(
    compiler_params=pltpu.CompilerParams(vmem_limit_bytes=SMALL_LIMIT),
    cost_estimate=pl.CostEstimate(flops=1000, bytes_accessed=1000, transcendentals=0),
)


def routing(ids, me):
    rows = ids.shape[1]
    upper = (
        lax.broadcasted_iota(jnp.int32, (rows, rows), 0) < lax.broadcasted_iota(jnp.int32, (rows, rows), 1)
    ).astype(F32).astype(BF)
    slot = lax.broadcasted_iota(jnp.int32, (MOST, rows), 0)
    hits, picks = [], []
    for step in range(EXPERTS):
        hit = (ids == (me ^ step)).astype(F32)
        member = jnp.sum(hit, axis=0, keepdims=True)
        before = jnp.dot(
            jnp.broadcast_to(member, (16, rows)).astype(BF), upper, preferred_element_type=F32
        )[:1]
        place = jnp.where(member > 0.5, before.astype(jnp.int32), -1)
        hits.append(hit)
        picks.append((slot == place).astype(F32))
    return hits, picks


def fold(block):
    return jnp.concatenate([block[:, c:c + 128] for c in range(0, block.shape[1], 128)], axis=0)


def unfold(block):
    return jnp.concatenate([block[r:r + MOST] for r in range(0, block.shape[0], MOST)], axis=1)


def folded(width):
    return jax.ShapeDtypeStruct((width // 128 * MOST, 128), BF)


def select_kernel(me_ref, t_ref, ids_hbm, tokens_hbm, *refs):
    out_refs = refs[:EXPERTS]
    ids_ref, tokens_ref, sems = refs[EXPERTS:]
    ids_copy = pltpu.make_async_copy(ids_hbm, ids_ref, sems.at[0])
    tokens_copy = pltpu.make_async_copy(tokens_hbm, tokens_ref, sems.at[1])
    ids_copy.start()
    tokens_copy.start()
    ids_copy.wait()
    _, picks = routing(ids_ref[...], me_ref[0])
    tokens_copy.wait()
    for k, (pick, out_ref) in enumerate(zip(picks, out_refs)):
        block = jnp.dot(pick.astype(BF), tokens_ref[...], preferred_element_type=F32)
        out_ref[...] = (block if k == 0 else fold(block)).astype(BF)


def select_rows(me, t, ids_t, tokens):
    width = tokens.shape[1]
    return pl.pallas_call(
        select_kernel,
        out_shape=[jax.ShapeDtypeStruct((MOST, width), BF)] + [folded(width)] * (EXPERTS - 1),
        in_specs=[SMEM, SMEM, ANY, ANY],
        out_specs=[VMEM] * EXPERTS,
        scratch_shapes=[
            pltpu.VMEM(ids_t.shape, ids_t.dtype),
            pltpu.VMEM(tokens.shape, tokens.dtype),
            pltpu.SemaphoreType.DMA((2,)),
        ],
        name="select_rows",
        compiler_params=pltpu.CompilerParams(vmem_limit_bytes=SMALL_LIMIT),
        cost_estimate=pl.CostEstimate(flops=8_000_000_000, bytes_accessed=1000, transcendentals=0),
    )(me, t, *(pltpu.with_memory_space_constraint(v, pltpu.HBM) for v in (ids_t, tokens)))


CUT = 2 * MOST // 16 * 16


def near_kernel(own_ref, next_ref, out_ref):
    both = jnp.concatenate([own_ref[...].astype(F32), unfold(next_ref[...].astype(F32))], axis=0)
    out_ref[...] = both[:CUT].astype(BF)


def far_kernel(next_ref, third_ref, fourth_ref, out_ref):
    rest = unfold(next_ref[...].astype(F32))[CUT - MOST:]
    blocks = [rest] + [unfold(r[...].astype(F32)) for r in (third_ref, fourth_ref)]
    out_ref[...] = jnp.concatenate(blocks, axis=0).astype(BF)


def pack_near(own, following):
    return pl.pallas_call(
        near_kernel,
        out_shape=jax.ShapeDtypeStruct((CUT, own.shape[1]), BF),
        in_specs=[VMEM] * 2,
        out_specs=VMEM,
        name="pack_near",
        **SMALL,
    )(own, following)


def pack_far(blocks, width):
    return pl.pallas_call(
        far_kernel,
        out_shape=jax.ShapeDtypeStruct((EXPERTS * MOST - CUT, width), BF),
        in_specs=[VMEM] * 3,
        out_specs=VMEM,
        name="pack_far",
        compiler_params=pltpu.CompilerParams(vmem_limit_bytes=SMALL_LIMIT),
        cost_estimate=pl.CostEstimate(flops=1_000_000_000, bytes_accessed=1000, transcendentals=0),
    )(*blocks)


def hold(value, after):
    return pl.pallas_call(
        lambda *refs: None,
        out_shape=jax.ShapeDtypeStruct(value.shape, value.dtype),
        in_specs=[ANY] * (1 + len(after)),
        out_specs=ANY,
        input_output_aliases={0: 0},
        name="hold",
        **SMALL,
    )(value, *after)


def hidden_kernel(joined, parts, start, t_ref, *refs):
    if joined:
        out_ref, x_ref = refs[-1], refs[0]
        gate_ref, up_ref = refs[1:3]
    else:
        out_ref, x_ref = refs[-2:]
        gate_ref, up_ref = refs[2 * parts:2 * parts + 2]
        for j in range(parts):
            x_ref[j, :CUT, :] = refs[2 * j][...]
            x_ref[j, CUT:, :] = refs[2 * j + 1][...]
    depth = x_ref.shape[2]
    for tile in range(0, out_ref.shape[1], FF_TILE):
        columns = slice(start + tile, start + tile + FF_TILE)
        gate = up = None
        for j in range(parts):
            at = pl.ds(pl.multiple_of((t_ref[0] ^ j) * depth, depth), depth)
            x = x_ref[j]
            g = jnp.dot(x, gate_ref[0, at, columns], preferred_element_type=F32)
            u = jnp.dot(x, up_ref[0, at, columns], preferred_element_type=F32)
            gate = g if gate is None else gate + g
            up = u if up is None else up + u
        out_ref[:, tile:tile + FF_TILE] = (gate * jax.nn.sigmoid(gate) * up).astype(BF)


def hidden_part(t, xs, gate_weight, up_weight, start, size, after=()):
    joined = len(xs) == 1
    parts = xs[0].shape[0] if joined else len(xs) // 2
    rows = EXPERTS * MOST
    out_shape = [jax.ShapeDtypeStruct((rows, size), BF)]
    if not joined:
        out_shape.append(jax.ShapeDtypeStruct((parts, rows, xs[0].shape[1]), BF))
    return pl.pallas_call(
        functools.partial(hidden_kernel, joined, parts, start),
        out_shape=out_shape,
        in_specs=[SMEM] + [VMEM] * (len(xs) + 2) + [ANY] * len(after),
        out_specs=[VMEM] * len(out_shape),
        compiler_params=pltpu.CompilerParams(vmem_limit_bytes=SMALL_LIMIT),
        cost_estimate=pl.CostEstimate(flops=1000, bytes_accessed=1000, transcendentals=0),
        name="hidden_part",
    )(t, *xs, gate_weight, up_weight, *after)


def down_kernel(count, where, slab, has_sum, last, t_ref, *refs):
    pieces = refs[:count]
    weight_ref = refs[count]
    rest = refs[count + 1:]
    outs = rest[has_sum:]
    total = rest[0][...] if has_sum else None
    for piece, (j, first) in zip(pieces, where):
        size = piece.shape[1]
        row = pl.multiple_of((t_ref[0] ^ j) * slab + first, K_TILE)
        term = jnp.dot(piece[...], weight_ref[0, pl.ds(row, size), :], preferred_element_type=F32)
        total = term if total is None else total + term
    if last:
        for k, out in enumerate(outs):
            block = total[k * MOST:(k + 1) * MOST]
            out[...] = fold(block).astype(BF)
    else:
        outs[0][...] = total


def down_part(t, slab, pieces, where, weight, running, last):
    rows = pieces[0].shape[0]
    width = weight.shape[2]
    has_sum = running is not None
    if last:
        out_shape = [folded(width)] * EXPERTS
    else:
        out_shape = [jax.ShapeDtypeStruct((rows, width), F32)]
    return pl.pallas_call(
        functools.partial(down_kernel, len(pieces), where, slab, has_sum, last),
        out_shape=out_shape,
        in_specs=[SMEM] + [VMEM] * (len(pieces) + 1 + has_sum),
        out_specs=[VMEM] * len(out_shape),
        compiler_params=pltpu.CompilerParams(vmem_limit_bytes=SMALL_LIMIT),
        cost_estimate=pl.CostEstimate(
            flops=2 * rows * width * sum(p.shape[1] for p in pieces), bytes_accessed=1000, transcendentals=0
        ),
        name="down_part",
    )(t, *pieces, weight, *([running] if has_sum else []))


def prepare_kernel(me_ref, ids_ref, probs_ref, grad_ref, *refs):
    hits_ref, routes_ref = refs[:2]
    picks_refs, grads_refs = refs[2:2 + EXPERTS], refs[2 + EXPERTS:]
    rows, width = grad_ref.shape
    hits, picks = routing(ids_ref[...], me_ref[0])
    for k in range(EXPERTS):
        hits_ref[k] = hits[k]
        picks_refs[k][...] = jnp.concatenate([picks[k]] * (width // 128), axis=0)
        grads_refs[k][...] = fold(jnp.dot(picks[k].astype(BF), grad_ref[...], preferred_element_type=F32))
    routes = jnp.concatenate(
        [jnp.sum(h * probs_ref[...], axis=0, keepdims=True) for h in hits]
        + [jnp.zeros((128 - EXPERTS, rows), F32)],
        axis=0,
    )
    routes_ref[...] = jnp.concatenate([routes, jnp.zeros((128, 128 - rows), F32)], axis=1).T[:rows]


def prepare(me, ids_t, probs_t, out_grad):
    rows, width = out_grad.shape
    tall = width // 128 * MOST
    shapes = [(EXPERTS,) + ids_t.shape, (rows, 128)] + [(tall, rows)] * EXPERTS + [(tall, 128)] * EXPERTS
    out = pl.pallas_call(
        prepare_kernel,
        out_shape=[jax.ShapeDtypeStruct(shape, F32) for shape in shapes],
        in_specs=[SMEM] + [VMEM] * 3,
        out_specs=[VMEM] * len(shapes),
        name="prepare",
        **SMALL,
    )(me, ids_t, probs_t, out_grad)
    return out[0], out[1], out[2:2 + EXPERTS], out[2 + EXPERTS:]


def dots_kernel(hits_ref, *refs):
    picks_refs, grads_refs, back_refs = (refs[n * EXPERTS:(n + 1) * EXPERTS] for n in range(3))
    total = None
    for k in range(EXPERTS):
        slots = jnp.sum(grads_refs[k][...] * back_refs[k][...].astype(F32), axis=1, keepdims=True)
        term = hits_ref[k] * jnp.sum(picks_refs[k][...] * slots, axis=0, keepdims=True)
        total = term if total is None else total + term
    refs[-1][...] = total


def take_dots(hits, picks, grads, back):
    return pl.pallas_call(
        dots_kernel,
        out_shape=jax.ShapeDtypeStruct(hits.shape[1:], F32),
        in_specs=[VMEM] * (1 + 3 * EXPERTS),
        out_specs=VMEM,
        name="dots",
        **SMALL,
    )(hits, *picks, *grads, *back)


def mix_kernel(routes_ref, *refs):
    picks_refs, back_refs = refs[:EXPERTS], refs[EXPERTS:2 * EXPERTS]
    mixed = None
    for k in range(EXPERTS):
        out = lax.dot_general(
            picks_refs[k][:MOST].astype(BF), unfold(back_refs[k][...].astype(F32)).astype(BF),
            (((0,), (0,)), ((), ())), preferred_element_type=F32,
        )
        term = routes_ref[:, k:k + 1] * out
        mixed = term if mixed is None else mixed + term
    refs[-1][...] = mixed.astype(BF)


def mix(routes, picks, back, width):
    return pl.pallas_call(
        mix_kernel,
        out_shape=jax.ShapeDtypeStruct((routes.shape[0], width), BF),
        in_specs=[VMEM] * (1 + 2 * EXPERTS),
        out_specs=VMEM,
        compiler_params=pltpu.CompilerParams(vmem_limit_bytes=SMALL_LIMIT),
        cost_estimate=pl.CostEstimate(flops=1_000_000_000, bytes_accessed=1000, transcendentals=0),
        name="mix",
    )(routes, *picks, *back)


Z_ORDER = (1, 2, 3)
CHUNKS = (256, 512, 768, 512)


def per_device(tokens, expert_ids, gate_probs, out_grad, gate_weight, up_weight, down_weight):
    me = lax.axis_index("expert").astype(jnp.int32).reshape(1)
    t_index = lax.axis_index("tensor").astype(jnp.int32).reshape(1)
    slab = gate_weight.shape[2]
    ids_t, probs_t = expert_ids.T, gate_probs.T

    rows = select_rows(me, t_index, ids_t, tokens)
    starts = [sum(CHUNKS[:i]) for i in range(len(CHUNKS))]
    arrived = {k: swap(rows[k], "expert", k) for k in Z_ORDER}
    near = pack_near(rows[0], arrived[1])
    near_across = swap(near, "tensor", 2)
    far = hold(pack_far([arrived[k] for k in (1, 2, 3)], tokens.shape[1]), [near_across])
    far_across = swap(far, "tensor", 2)
    sides = [swap(v, "tensor", 1) for v in (near, far, near_across)]
    far_across = hold(far_across, sides)
    xs = [near, far, sides[0], sides[1], near_across, far_across, sides[2], swap(far_across, "tensor", 1)]

    hits, routes, picks, grads = prepare(me, ids_t, probs_t, out_grad)

    pieces = []
    for i, (start, size) in enumerate(zip(starts, CHUNKS)):
        after = [pieces[i - 2][2]] if i >= 2 else []
        h, *whole = hidden_part(t_index, xs, gate_weight, up_weight, start, size, after)
        xs = whole or xs
        pieces.append([h, swap(h, "tensor", 1), swap(h, "tensor", 2)])
    sums = []
    for i, start in enumerate(starts):
        far = hold(pieces[i][2], sums[i - 2:i - 1]) if i >= 2 else pieces[i][2]
        pieces[i] = pieces[i][:2] + [far, swap(far, "tensor", 1)]
        use = [(i, 2), (i, 3)]
        if i == 0:
            use = [(0, 0), (0, 1)] + use
        if i + 1 < len(starts):
            use += [(i + 1, 0), (i + 1, 1)]
        result = down_part(
            t_index, slab, [pieces[n][j] for n, j in use], [(j, starts[n]) for n, j in use], down_weight,
            sums[-1] if sums else None, i + 1 == len(starts),
        )
        sums.append(result[0])
    back = [result[0]] + [swap(result[k], "expert", k) for k in (1, 2, 3)]
    gate_grad = take_dots(hits, picks, grads, back)
    mixed = mix(routes, picks, back, tokens.shape[1])
    gate_grad = gate_grad + hold(swap(gate_grad, "tensor", 2), [mixed])
    gate_grad = gate_grad + swap(gate_grad, "tensor", 1)
    return mixed, gate_grad.T


def per_device_any(tokens, expert_ids, gate_probs, out_grad, gate_weight, up_weight, down_weight):
    span_count = lax.axis_size("expert") // EXPERTS
    hits = expert_ids[:, :, None] == jnp.arange(EXPERTS, dtype=jnp.int32)[None, None, :]
    hit_float = hits.astype(F32)
    member = jnp.sum(hits.astype(jnp.int32), axis=1)
    place = jnp.cumsum(member, axis=0) - member
    placed = (place[None, :, :] == jnp.arange(MOST, dtype=jnp.int32)[:, None, None]) & (member[None, :, :] == 1)
    select = jnp.transpose(placed, (2, 0, 1)).astype(F32)
    route = jnp.sum(hit_float * gate_probs[:, :, None], axis=1)
    rows = jnp.einsum("est,td->esd", select.astype(BF), tokens, preferred_element_type=F32).astype(BF)
    arrived = lax.all_to_all(
        jnp.repeat(rows, span_count, axis=0), "expert", split_axis=0, concat_axis=0, tiled=True
    )
    full = lax.all_gather(arrived, "tensor", axis=2, tiled=True)
    gate = jnp.einsum("smd,df->smf", full, gate_weight[0], preferred_element_type=F32)
    up = jnp.einsum("smd,df->smf", full, up_weight[0], preferred_element_type=F32)
    hidden = (gate * jax.nn.sigmoid(gate) * up).astype(BF)
    partial_out = jnp.einsum(
        "smf,fd->smd",
        lax.all_gather(hidden, "tensor", axis=2, tiled=True),
        down_weight[0],
        preferred_element_type=F32,
    )
    back = lax.all_to_all(partial_out, "expert", split_axis=0, concat_axis=0, tiled=True)
    expert_out = jnp.sum(back.reshape(EXPERTS, span_count, MOST, tokens.shape[1]), axis=1)
    token_out = jnp.einsum("est,esd->ted", select, expert_out, precision=lax.Precision.HIGHEST)
    mixed = jnp.sum(route[:, :, None] * token_out, axis=1).astype(BF)
    dots = lax.psum(jnp.sum(out_grad.astype(F32)[:, None, :] * token_out, axis=2), "tensor")
    return mixed, jnp.sum(hit_float * dots[:, None, :], axis=2)


def solution(mesh):
    in_specs = (
        P(("groups", "expert"), "tensor"),
        P(("groups", "expert"), None),
        P(("groups", "expert"), None),
        P(("groups", "expert"), "tensor"),
        P("expert", None, "tensor"),
        P("expert", None, "tensor"),
        P("expert", None, "tensor"),
    )
    out_specs = (P(("groups", "expert"), "tensor"), P(("groups", "expert"), None))
    direct = mesh.shape["expert"] == EXPERTS and mesh.shape["tensor"] == 4
    return jax.shard_map(
        per_device if direct else per_device_any,
        mesh=mesh, in_specs=in_specs, out_specs=out_specs, check_vma=False,
    )
```

```python
import functools

import jax
import jax.numpy as jnp
from jax import lax
from jax.experimental import pallas as pl
from jax.experimental.pallas import tpu as pltpu
from jax.sharding import PartitionSpec as P

EXPERTS = 4
MOST = 34
BF = jnp.bfloat16
F32 = jnp.float32
VMEM_LIMIT = 24 * 1024 * 1024
SMALL_LIMIT = 4 * 1024 * 1024
FF_TILE = 256
K_TILE = 256


def swap(value, axis, bit):
    size = lax.axis_size(axis)
    return lax.ppermute(value, axis, [(i, i ^ bit) for i in range(size)])


VMEM = pl.BlockSpec(memory_space=pltpu.VMEM)
SMEM = pl.BlockSpec(memory_space=pltpu.SMEM)
ANY = pl.BlockSpec(memory_space=pl.ANY)
SMALL = dict(
    compiler_params=pltpu.CompilerParams(vmem_limit_bytes=SMALL_LIMIT),
    cost_estimate=pl.CostEstimate(flops=1000, bytes_accessed=1000, transcendentals=0),
)


def routing(ids, me):
    rows = ids.shape[1]
    upper = (
        lax.broadcasted_iota(jnp.int32, (rows, rows), 0) < lax.broadcasted_iota(jnp.int32, (rows, rows), 1)
    ).astype(F32).astype(BF)
    slot = lax.broadcasted_iota(jnp.int32, (MOST, rows), 0)
    hits, picks = [], []
    for step in range(EXPERTS):
        hit = (ids == (me ^ step)).astype(F32)
        member = jnp.sum(hit, axis=0, keepdims=True)
        before = jnp.dot(
            jnp.broadcast_to(member, (16, rows)).astype(BF), upper, preferred_element_type=F32
        )[:1]
        place = jnp.where(member > 0.5, before.astype(jnp.int32), -1)
        hits.append(hit)
        picks.append((slot == place).astype(F32))
    return hits, picks


def fold(block):
    return jnp.concatenate([block[:, c:c + 128] for c in range(0, block.shape[1], 128)], axis=0)


def unfold(block):
    return jnp.concatenate([block[r:r + MOST] for r in range(0, block.shape[0], MOST)], axis=1)


def folded(width):
    return jax.ShapeDtypeStruct((width // 128 * MOST, 128), BF)


def select_kernel(me_ref, t_ref, ids_hbm, tokens_hbm, *refs):
    out_refs = refs[:EXPERTS]
    ids_ref, tokens_ref, sems = refs[EXPERTS:]
    ids_copy = pltpu.make_async_copy(ids_hbm, ids_ref, sems.at[0])
    tokens_copy = pltpu.make_async_copy(tokens_hbm, tokens_ref, sems.at[1])
    ids_copy.start()
    tokens_copy.start()
    ids_copy.wait()
    _, picks = routing(ids_ref[...], me_ref[0])
    tokens_copy.wait()
    for k, (pick, out_ref) in enumerate(zip(picks, out_refs)):
        block = jnp.dot(pick.astype(BF), tokens_ref[...], preferred_element_type=F32)
        out_ref[...] = (block if k == 0 else fold(block)).astype(BF)


def select_rows(me, t, ids_t, tokens):
    width = tokens.shape[1]
    return pl.pallas_call(
        select_kernel,
        out_shape=[jax.ShapeDtypeStruct((MOST, width), BF)] + [folded(width)] * (EXPERTS - 1),
        in_specs=[SMEM, SMEM, ANY, ANY],
        out_specs=[VMEM] * EXPERTS,
        scratch_shapes=[
            pltpu.VMEM(ids_t.shape, ids_t.dtype),
            pltpu.VMEM(tokens.shape, tokens.dtype),
            pltpu.SemaphoreType.DMA((2,)),
        ],
        name="select_rows",
        compiler_params=pltpu.CompilerParams(vmem_limit_bytes=SMALL_LIMIT),
        cost_estimate=pl.CostEstimate(flops=8_000_000_000, bytes_accessed=1000, transcendentals=0),
    )(me, t, *(pltpu.with_memory_space_constraint(v, pltpu.HBM) for v in (ids_t, tokens)))


CUT = 2 * MOST // 16 * 16


def near_kernel(own_ref, next_ref, out_ref):
    both = jnp.concatenate([own_ref[...].astype(F32), unfold(next_ref[...].astype(F32))], axis=0)
    out_ref[...] = both[:CUT].astype(BF)


def far_kernel(next_ref, third_ref, fourth_ref, out_ref):
    rest = unfold(next_ref[...].astype(F32))[CUT - MOST:]
    blocks = [rest] + [unfold(r[...].astype(F32)) for r in (third_ref, fourth_ref)]
    out_ref[...] = jnp.concatenate(blocks, axis=0).astype(BF)


def pack_near(own, following):
    return pl.pallas_call(
        near_kernel,
        out_shape=jax.ShapeDtypeStruct((CUT, own.shape[1]), BF),
        in_specs=[VMEM] * 2,
        out_specs=VMEM,
        name="pack_near",
        **SMALL,
    )(own, following)


def pack_far(blocks, width):
    return pl.pallas_call(
        far_kernel,
        out_shape=jax.ShapeDtypeStruct((EXPERTS * MOST - CUT, width), BF),
        in_specs=[VMEM] * 3,
        out_specs=VMEM,
        name="pack_far",
        compiler_params=pltpu.CompilerParams(vmem_limit_bytes=SMALL_LIMIT),
        cost_estimate=pl.CostEstimate(flops=1_000_000_000, bytes_accessed=1000, transcendentals=0),
    )(*blocks)


def hold(value, after):
    return pl.pallas_call(
        lambda *refs: None,
        out_shape=jax.ShapeDtypeStruct(value.shape, value.dtype),
        in_specs=[ANY] * (1 + len(after)),
        out_specs=ANY,
        input_output_aliases={0: 0},
        name="hold",
        **SMALL,
    )(value, *after)


def hidden_kernel(joined, parts, start, t_ref, *refs):
    if joined:
        out_ref, x_ref = refs[-1], refs[0]
        gate_ref, up_ref = refs[1:3]
    else:
        out_ref, x_ref = refs[-2:]
        gate_ref, up_ref = refs[2 * parts:2 * parts + 2]
        for j in range(parts):
            x_ref[j, :CUT, :] = refs[2 * j][...]
            x_ref[j, CUT:, :] = refs[2 * j + 1][...]
    depth = x_ref.shape[2]
    for tile in range(0, out_ref.shape[1], FF_TILE):
        columns = slice(start + tile, start + tile + FF_TILE)
        gate = up = None
        for j in range(parts):
            at = pl.ds(pl.multiple_of((t_ref[0] ^ j) * depth, depth), depth)
            x = x_ref[j]
            g = jnp.dot(x, gate_ref[0, at, columns], preferred_element_type=F32)
            u = jnp.dot(x, up_ref[0, at, columns], preferred_element_type=F32)
            gate = g if gate is None else gate + g
            up = u if up is None else up + u
        out_ref[:, tile:tile + FF_TILE] = (gate * jax.nn.sigmoid(gate) * up).astype(BF)


def hidden_part(t, xs, gate_weight, up_weight, start, size, after=()):
    joined = len(xs) == 1
    parts = xs[0].shape[0] if joined else len(xs) // 2
    rows = EXPERTS * MOST
    out_shape = [jax.ShapeDtypeStruct((rows, size), BF)]
    if not joined:
        out_shape.append(jax.ShapeDtypeStruct((parts, rows, xs[0].shape[1]), BF))
    return pl.pallas_call(
        functools.partial(hidden_kernel, joined, parts, start),
        out_shape=out_shape,
        in_specs=[SMEM] + [VMEM] * (len(xs) + 2) + [ANY] * len(after),
        out_specs=[VMEM] * len(out_shape),
        compiler_params=pltpu.CompilerParams(vmem_limit_bytes=SMALL_LIMIT),
        cost_estimate=pl.CostEstimate(flops=1000, bytes_accessed=1000, transcendentals=0),
        name="hidden_part",
    )(t, *xs, gate_weight, up_weight, *after)


def down_kernel(count, where, slab, has_sum, last, t_ref, *refs):
    pieces = refs[:count]
    weight_ref = refs[count]
    rest = refs[count + 1:]
    outs = rest[has_sum:]
    total = rest[0][...] if has_sum else None
    for piece, (j, first) in zip(pieces, where):
        size = piece.shape[1]
        row = pl.multiple_of((t_ref[0] ^ j) * slab + first, K_TILE)
        term = jnp.dot(piece[...], weight_ref[0, pl.ds(row, size), :], preferred_element_type=F32)
        total = term if total is None else total + term
    if last:
        for k, out in enumerate(outs):
            block = total[k * MOST:(k + 1) * MOST]
            out[...] = fold(block).astype(BF)
    else:
        outs[0][...] = total


def down_part(t, slab, pieces, where, weight, running, last):
    rows = pieces[0].shape[0]
    width = weight.shape[2]
    has_sum = running is not None
    if last:
        out_shape = [folded(width)] * EXPERTS
    else:
        out_shape = [jax.ShapeDtypeStruct((rows, width), F32)]
    return pl.pallas_call(
        functools.partial(down_kernel, len(pieces), where, slab, has_sum, last),
        out_shape=out_shape,
        in_specs=[SMEM] + [VMEM] * (len(pieces) + 1 + has_sum),
        out_specs=[VMEM] * len(out_shape),
        compiler_params=pltpu.CompilerParams(vmem_limit_bytes=SMALL_LIMIT),
        cost_estimate=pl.CostEstimate(
            flops=2 * rows * width * sum(p.shape[1] for p in pieces), bytes_accessed=1000, transcendentals=0
        ),
        name="down_part",
    )(t, *pieces, weight, *([running] if has_sum else []))


def prepare_kernel(me_ref, ids_ref, probs_ref, grad_ref, *refs):
    hits_ref, routes_ref = refs[:2]
    picks_refs, grads_refs = refs[2:2 + EXPERTS], refs[2 + EXPERTS:]
    rows, width = grad_ref.shape
    hits, picks = routing(ids_ref[...], me_ref[0])
    for k in range(EXPERTS):
        hits_ref[k] = hits[k]
        picks_refs[k][...] = jnp.concatenate([picks[k]] * (width // 128), axis=0)
        grads_refs[k][...] = fold(jnp.dot(picks[k].astype(BF), grad_ref[...], preferred_element_type=F32))
    routes = jnp.concatenate(
        [jnp.sum(h * probs_ref[...], axis=0, keepdims=True) for h in hits]
        + [jnp.zeros((128 - EXPERTS, rows), F32)],
        axis=0,
    )
    routes_ref[...] = jnp.concatenate([routes, jnp.zeros((128, 128 - rows), F32)], axis=1).T[:rows]


def prepare(me, ids_t, probs_t, out_grad):
    rows, width = out_grad.shape
    tall = width // 128 * MOST
    shapes = [(EXPERTS,) + ids_t.shape, (rows, 128)] + [(tall, rows)] * EXPERTS + [(tall, 128)] * EXPERTS
    out = pl.pallas_call(
        prepare_kernel,
        out_shape=[jax.ShapeDtypeStruct(shape, F32) for shape in shapes],
        in_specs=[SMEM] + [VMEM] * 3,
        out_specs=[VMEM] * len(shapes),
        name="prepare",
        **SMALL,
    )(me, ids_t, probs_t, out_grad)
    return out[0], out[1], out[2:2 + EXPERTS], out[2 + EXPERTS:]


def dots_kernel(hits_ref, *refs):
    picks_refs, grads_refs, back_refs = (refs[n * EXPERTS:(n + 1) * EXPERTS] for n in range(3))
    total = None
    for k in range(EXPERTS):
        slots = jnp.sum(grads_refs[k][...] * back_refs[k][...].astype(F32), axis=1, keepdims=True)
        term = hits_ref[k] * jnp.sum(picks_refs[k][...] * slots, axis=0, keepdims=True)
        total = term if total is None else total + term
    refs[-1][...] = total


def take_dots(hits, picks, grads, back):
    return pl.pallas_call(
        dots_kernel,
        out_shape=jax.ShapeDtypeStruct(hits.shape[1:], F32),
        in_specs=[VMEM] * (1 + 3 * EXPERTS),
        out_specs=VMEM,
        name="dots",
        **SMALL,
    )(hits, *picks, *grads, *back)


def mix_kernel(routes_ref, *refs):
    picks_refs, back_refs = refs[:EXPERTS], refs[EXPERTS:2 * EXPERTS]
    mixed = None
    for k in range(EXPERTS):
        out = lax.dot_general(
            picks_refs[k][:MOST].astype(BF), unfold(back_refs[k][...].astype(F32)).astype(BF),
            (((0,), (0,)), ((), ())), preferred_element_type=F32,
        )
        term = routes_ref[:, k:k + 1] * out
        mixed = term if mixed is None else mixed + term
    refs[-2][...] = mixed.astype(BF)
    refs[-1][...] = jnp.zeros(refs[-1].shape, F32)


def mix(routes, picks, back, width):
    return pl.pallas_call(
        mix_kernel,
        out_shape=[jax.ShapeDtypeStruct((routes.shape[0], width), BF), jax.ShapeDtypeStruct((8, 128), F32)],
        in_specs=[VMEM] * (1 + 2 * EXPERTS),
        out_specs=[VMEM] * 2,
        compiler_params=pltpu.CompilerParams(vmem_limit_bytes=SMALL_LIMIT),
        cost_estimate=pl.CostEstimate(flops=1_000_000_000, bytes_accessed=1000, transcendentals=0),
        name="mix",
    )(routes, *picks, *back)


Z_ORDER = (1, 2, 3)
CHUNKS = (256, 512, 768, 512)


def per_device(tokens, expert_ids, gate_probs, out_grad, gate_weight, up_weight, down_weight):
    me = lax.axis_index("expert").astype(jnp.int32).reshape(1)
    t_index = lax.axis_index("tensor").astype(jnp.int32).reshape(1)
    slab = gate_weight.shape[2]
    ids_t, probs_t = expert_ids.T, gate_probs.T

    rows = select_rows(me, t_index, ids_t, tokens)
    starts = [sum(CHUNKS[:i]) for i in range(len(CHUNKS))]
    arrived = {k: swap(rows[k], "expert", k) for k in Z_ORDER}
    near = pack_near(rows[0], arrived[1])
    near_across = swap(near, "tensor", 2)
    far = hold(pack_far([arrived[k] for k in (1, 2, 3)], tokens.shape[1]), [near_across])
    far_across = swap(far, "tensor", 2)
    sides = [swap(v, "tensor", 1) for v in (near, far, near_across)]
    far_across = hold(far_across, sides)
    xs = [near, far, sides[0], sides[1], near_across, far_across, sides[2], swap(far_across, "tensor", 1)]

    hits, routes, picks, grads = prepare(me, ids_t, probs_t, out_grad)

    pieces = []
    for i, (start, size) in enumerate(zip(starts, CHUNKS)):
        after = [pieces[i - 2][2]] if i >= 2 else []
        h, *whole = hidden_part(t_index, xs, gate_weight, up_weight, start, size, after)
        xs = whole or xs
        pieces.append([h, swap(h, "tensor", 1), swap(h, "tensor", 2)])
    sums = []
    for i, start in enumerate(starts):
        far = hold(pieces[i][2], sums[i - 2:i - 1]) if i >= 2 else pieces[i][2]
        pieces[i] = pieces[i][:2] + [far, swap(far, "tensor", 1)]
        use = [(i, 2), (i, 3)]
        if i == 0:
            use = [(0, 0), (0, 1)] + use
        if i + 1 < len(starts):
            use += [(i + 1, 0), (i + 1, 1)]
        result = down_part(
            t_index, slab, [pieces[n][j] for n, j in use], [(j, starts[n]) for n, j in use], down_weight,
            sums[-1] if sums else None, i + 1 == len(starts),
        )
        sums.append(result[0])
    back = [result[0]] + [swap(result[k], "expert", k) for k in (1, 2, 3)]
    gate_grad = take_dots(hits, picks, grads, back)
    mixed, done = mix(routes, picks, back, tokens.shape[1])
    gate_grad = gate_grad + hold(swap(gate_grad, "tensor", 2), [done])
    gate_grad = gate_grad + swap(gate_grad, "tensor", 1)
    return mixed, gate_grad.T


def per_device_any(tokens, expert_ids, gate_probs, out_grad, gate_weight, up_weight, down_weight):
    span_count = lax.axis_size("expert") // EXPERTS
    hits = expert_ids[:, :, None] == jnp.arange(EXPERTS, dtype=jnp.int32)[None, None, :]
    hit_float = hits.astype(F32)
    member = jnp.sum(hits.astype(jnp.int32), axis=1)
    place = jnp.cumsum(member, axis=0) - member
    placed = (place[None, :, :] == jnp.arange(MOST, dtype=jnp.int32)[:, None, None]) & (member[None, :, :] == 1)
    select = jnp.transpose(placed, (2, 0, 1)).astype(F32)
    route = jnp.sum(hit_float * gate_probs[:, :, None], axis=1)
    rows = jnp.einsum("est,td->esd", select.astype(BF), tokens, preferred_element_type=F32).astype(BF)
    arrived = lax.all_to_all(
        jnp.repeat(rows, span_count, axis=0), "expert", split_axis=0, concat_axis=0, tiled=True
    )
    full = lax.all_gather(arrived, "tensor", axis=2, tiled=True)
    gate = jnp.einsum("smd,df->smf", full, gate_weight[0], preferred_element_type=F32)
    up = jnp.einsum("smd,df->smf", full, up_weight[0], preferred_element_type=F32)
    hidden = (gate * jax.nn.sigmoid(gate) * up).astype(BF)
    partial_out = jnp.einsum(
        "smf,fd->smd",
        lax.all_gather(hidden, "tensor", axis=2, tiled=True),
        down_weight[0],
        preferred_element_type=F32,
    )
    back = lax.all_to_all(partial_out, "expert", split_axis=0, concat_axis=0, tiled=True)
    expert_out = jnp.sum(back.reshape(EXPERTS, span_count, MOST, tokens.shape[1]), axis=1)
    token_out = jnp.einsum("est,esd->ted", select, expert_out, precision=lax.Precision.HIGHEST)
    mixed = jnp.sum(route[:, :, None] * token_out, axis=1).astype(BF)
    dots = lax.psum(jnp.sum(out_grad.astype(F32)[:, None, :] * token_out, axis=2), "tensor")
    return mixed, jnp.sum(hit_float * dots[:, None, :], axis=2)


def solution(mesh):
    in_specs = (
        P(("groups", "expert"), "tensor"),
        P(("groups", "expert"), None),
        P(("groups", "expert"), None),
        P(("groups", "expert"), "tensor"),
        P("expert", None, "tensor"),
        P("expert", None, "tensor"),
        P("expert", None, "tensor"),
    )
    out_specs = (P(("groups", "expert"), "tensor"), P(("groups", "expert"), None))
    direct = mesh.shape["expert"] == EXPERTS and mesh.shape["tensor"] == 4
    return jax.shard_map(
        per_device if direct else per_device_any,
        mesh=mesh, in_specs=in_specs, out_specs=out_specs, check_vma=False,
    )
```

```python
import functools

import jax
import jax.numpy as jnp
from jax import lax
from jax.experimental import pallas as pl
from jax.experimental.pallas import tpu as pltpu
from jax.sharding import PartitionSpec as P

EXPERTS = 4
MOST = 34
BF = jnp.bfloat16
F32 = jnp.float32
VMEM_LIMIT = 24 * 1024 * 1024
SMALL_LIMIT = 4 * 1024 * 1024
FF_TILE = 256
K_TILE = 256


def swap(value, axis, bit):
    size = lax.axis_size(axis)
    return lax.ppermute(value, axis, [(i, i ^ bit) for i in range(size)])


VMEM = pl.BlockSpec(memory_space=pltpu.VMEM)
SMEM = pl.BlockSpec(memory_space=pltpu.SMEM)
ANY = pl.BlockSpec(memory_space=pl.ANY)
SMALL = dict(
    compiler_params=pltpu.CompilerParams(vmem_limit_bytes=SMALL_LIMIT),
    cost_estimate=pl.CostEstimate(flops=1000, bytes_accessed=1000, transcendentals=0),
)


def routing(ids, me):
    rows = ids.shape[1]
    upper = (
        lax.broadcasted_iota(jnp.int32, (rows, rows), 0) < lax.broadcasted_iota(jnp.int32, (rows, rows), 1)
    ).astype(F32).astype(BF)
    slot = lax.broadcasted_iota(jnp.int32, (MOST, rows), 0)
    hits, picks = [], []
    for step in range(EXPERTS):
        hit = (ids == (me ^ step)).astype(F32)
        member = jnp.sum(hit, axis=0, keepdims=True)
        before = jnp.dot(
            jnp.broadcast_to(member, (16, rows)).astype(BF), upper, preferred_element_type=F32
        )[:1]
        place = jnp.where(member > 0.5, before.astype(jnp.int32), -1)
        hits.append(hit)
        picks.append((slot == place).astype(F32))
    return hits, picks


def fold(block):
    return jnp.concatenate([block[:, c:c + 128] for c in range(0, block.shape[1], 128)], axis=0)


def unfold(block):
    return jnp.concatenate([block[r:r + MOST] for r in range(0, block.shape[0] - MOST + 1, MOST)], axis=1)


def folded(width, more=0):
    return jax.ShapeDtypeStruct((width // 128 * MOST + more, 128), BF)


def select_kernel(me_ref, t_ref, ids_hbm, tokens_hbm, *refs):
    out_refs = refs[:EXPERTS]
    ids_ref, tokens_ref, sems = refs[EXPERTS:]
    ids_copy = pltpu.make_async_copy(ids_hbm, ids_ref, sems.at[0])
    tokens_copy = pltpu.make_async_copy(tokens_hbm, tokens_ref, sems.at[1])
    ids_copy.start()
    tokens_copy.start()
    ids_copy.wait()
    _, picks = routing(ids_ref[...], me_ref[0])
    tokens_copy.wait()
    for k, (pick, out_ref) in enumerate(zip(picks, out_refs)):
        block = jnp.dot(pick.astype(BF), tokens_ref[...], preferred_element_type=F32)
        block = block if k == 0 else fold(block)
        if out_ref.shape[0] > block.shape[0]:
            block = jnp.concatenate([block, jnp.zeros((out_ref.shape[0] - block.shape[0], 128), F32)], axis=0)
        out_ref[...] = block.astype(BF)


def select_rows(me, t, ids_t, tokens):
    width = tokens.shape[1]
    return pl.pallas_call(
        select_kernel,
        out_shape=[jax.ShapeDtypeStruct((MOST, width), BF), folded(width)] + [folded(width, 4)] * (EXPERTS - 2),
        in_specs=[SMEM, SMEM, ANY, ANY],
        out_specs=[VMEM] * EXPERTS,
        scratch_shapes=[
            pltpu.VMEM(ids_t.shape, ids_t.dtype),
            pltpu.VMEM(tokens.shape, tokens.dtype),
            pltpu.SemaphoreType.DMA((2,)),
        ],
        name="select_rows",
        compiler_params=pltpu.CompilerParams(vmem_limit_bytes=SMALL_LIMIT),
        cost_estimate=pl.CostEstimate(flops=8_000_000_000, bytes_accessed=1000, transcendentals=0),
    )(me, t, *(pltpu.with_memory_space_constraint(v, pltpu.HBM) for v in (ids_t, tokens)))


CUT = 2 * MOST // 16 * 16


def near_kernel(own_ref, next_ref, out_ref):
    both = jnp.concatenate([own_ref[...].astype(F32), unfold(next_ref[...].astype(F32))], axis=0)
    out_ref[...] = both[:CUT].astype(BF)


def far_kernel(next_ref, third_ref, fourth_ref, out_ref):
    rest = unfold(next_ref[...].astype(F32))[CUT - MOST:]
    blocks = [rest] + [unfold(r[...].astype(F32)) for r in (third_ref, fourth_ref)]
    out_ref[...] = jnp.concatenate(blocks, axis=0).astype(BF)


def pack_near(own, following):
    return pl.pallas_call(
        near_kernel,
        out_shape=jax.ShapeDtypeStruct((CUT, own.shape[1]), BF),
        in_specs=[VMEM] * 2,
        out_specs=VMEM,
        name="pack_near",
        **SMALL,
    )(own, following)


def pack_far(blocks, width):
    return pl.pallas_call(
        far_kernel,
        out_shape=jax.ShapeDtypeStruct((EXPERTS * MOST - CUT, width), BF),
        in_specs=[VMEM] * 3,
        out_specs=VMEM,
        name="pack_far",
        compiler_params=pltpu.CompilerParams(vmem_limit_bytes=SMALL_LIMIT),
        cost_estimate=pl.CostEstimate(flops=2_000_000_000, bytes_accessed=1000, transcendentals=0),
    )(*blocks)


def hold(value, after):
    return pl.pallas_call(
        lambda *refs: None,
        out_shape=jax.ShapeDtypeStruct(value.shape, value.dtype),
        in_specs=[ANY] * (1 + len(after)),
        out_specs=ANY,
        input_output_aliases={0: 0},
        name="hold",
        **SMALL,
    )(value, *after)


def hidden_kernel(joined, parts, start, t_ref, *refs):
    if joined:
        out_ref, x_ref = refs[-1], refs[0]
        gate_ref, up_ref = refs[1:3]
    else:
        out_ref, x_ref = refs[-2:]
        gate_ref, up_ref = refs[2 * parts:2 * parts + 2]
        for j in range(parts):
            x_ref[j, :CUT, :] = refs[2 * j][...]
            x_ref[j, CUT:, :] = refs[2 * j + 1][...]
    depth = x_ref.shape[2]
    for tile in range(0, out_ref.shape[1], FF_TILE):
        columns = slice(start + tile, start + tile + FF_TILE)
        gate = up = None
        for j in range(parts):
            at = pl.ds(pl.multiple_of((t_ref[0] ^ j) * depth, depth), depth)
            x = x_ref[j]
            g = jnp.dot(x, gate_ref[0, at, columns], preferred_element_type=F32)
            u = jnp.dot(x, up_ref[0, at, columns], preferred_element_type=F32)
            gate = g if gate is None else gate + g
            up = u if up is None else up + u
        out_ref[:, tile:tile + FF_TILE] = (gate * jax.nn.sigmoid(gate) * up).astype(BF)


def hidden_part(t, xs, gate_weight, up_weight, start, size, after=()):
    joined = len(xs) == 1
    parts = xs[0].shape[0] if joined else len(xs) // 2
    rows = EXPERTS * MOST
    out_shape = [jax.ShapeDtypeStruct((rows, size), BF)]
    if not joined:
        out_shape.append(jax.ShapeDtypeStruct((parts, rows, xs[0].shape[1]), BF))
    return pl.pallas_call(
        functools.partial(hidden_kernel, joined, parts, start),
        out_shape=out_shape,
        in_specs=[SMEM] + [VMEM] * (len(xs) + 2) + [ANY] * len(after),
        out_specs=[VMEM] * len(out_shape),
        compiler_params=pltpu.CompilerParams(vmem_limit_bytes=SMALL_LIMIT),
        cost_estimate=pl.CostEstimate(flops=1000, bytes_accessed=1000, transcendentals=0),
        name="hidden_part",
    )(t, *xs, gate_weight, up_weight, *after)


def down_kernel(count, where, slab, has_sum, last, t_ref, *refs):
    pieces = refs[:count]
    weight_ref = refs[count]
    rest = refs[count + 1:]
    outs = rest[has_sum:]
    total = rest[0][...] if has_sum else None
    for piece, (j, first) in zip(pieces, where):
        size = piece.shape[1]
        row = pl.multiple_of((t_ref[0] ^ j) * slab + first, K_TILE)
        term = jnp.dot(piece[...], weight_ref[0, pl.ds(row, size), :], preferred_element_type=F32)
        total = term if total is None else total + term
    if last:
        for k, out in enumerate(outs):
            block = total[k * MOST:(k + 1) * MOST]
            out[...] = fold(block).astype(BF)
    else:
        outs[0][...] = total


def down_part(t, slab, pieces, where, weight, running, last):
    rows = pieces[0].shape[0]
    width = weight.shape[2]
    has_sum = running is not None
    if last:
        out_shape = [folded(width)] * EXPERTS
    else:
        out_shape = [jax.ShapeDtypeStruct((rows, width), F32)]
    return pl.pallas_call(
        functools.partial(down_kernel, len(pieces), where, slab, has_sum, last),
        out_shape=out_shape,
        in_specs=[SMEM] + [VMEM] * (len(pieces) + 1 + has_sum),
        out_specs=[VMEM] * len(out_shape),
        compiler_params=pltpu.CompilerParams(vmem_limit_bytes=SMALL_LIMIT),
        cost_estimate=pl.CostEstimate(
            flops=2 * rows * width * sum(p.shape[1] for p in pieces), bytes_accessed=1000, transcendentals=0
        ),
        name="down_part",
    )(t, *pieces, weight, *([running] if has_sum else []))


def prepare_kernel(me_ref, ids_ref, probs_ref, grad_ref, *refs):
    hits_ref, routes_ref = refs[:2]
    picks_refs, grads_refs = refs[2:2 + EXPERTS], refs[2 + EXPERTS:]
    rows, width = grad_ref.shape
    hits, picks = routing(ids_ref[...], me_ref[0])
    for k in range(EXPERTS):
        hits_ref[k] = hits[k]
        picks_refs[k][...] = jnp.concatenate([picks[k]] * (width // 128), axis=0)
        grads_refs[k][...] = fold(jnp.dot(picks[k].astype(BF), grad_ref[...], preferred_element_type=F32))
    routes = jnp.concatenate(
        [jnp.sum(h * probs_ref[...], axis=0, keepdims=True) for h in hits]
        + [jnp.zeros((128 - EXPERTS, rows), F32)],
        axis=0,
    )
    routes_ref[...] = jnp.concatenate([routes, jnp.zeros((128, 128 - rows), F32)], axis=1).T[:rows]


def prepare(me, ids_t, probs_t, out_grad):
    rows, width = out_grad.shape
    tall = width // 128 * MOST
    shapes = [(EXPERTS,) + ids_t.shape, (rows, 128)] + [(tall, rows)] * EXPERTS + [(tall, 128)] * EXPERTS
    out = pl.pallas_call(
        prepare_kernel,
        out_shape=[jax.ShapeDtypeStruct(shape, F32) for shape in shapes],
        in_specs=[SMEM] + [VMEM] * 3,
        out_specs=[VMEM] * len(shapes),
        name="prepare",
        **SMALL,
    )(me, ids_t, probs_t, out_grad)
    return out[0], out[1], out[2:2 + EXPERTS], out[2 + EXPERTS:]


def dots_kernel(hits_ref, *refs):
    picks_refs, grads_refs, back_refs = (refs[n * EXPERTS:(n + 1) * EXPERTS] for n in range(3))
    total = None
    for k in range(EXPERTS):
        slots = jnp.sum(grads_refs[k][...] * back_refs[k][...].astype(F32), axis=1, keepdims=True)
        term = hits_ref[k] * jnp.sum(picks_refs[k][...] * slots, axis=0, keepdims=True)
        total = term if total is None else total + term
    refs[-1][...] = total


def take_dots(hits, picks, grads, back):
    return pl.pallas_call(
        dots_kernel,
        out_shape=jax.ShapeDtypeStruct(hits.shape[1:], F32),
        in_specs=[VMEM] * (1 + 3 * EXPERTS),
        out_specs=VMEM,
        name="dots",
        **SMALL,
    )(hits, *picks, *grads, *back)


def mix_kernel(routes_ref, *refs):
    picks_refs, back_refs = refs[:EXPERTS], refs[EXPERTS:2 * EXPERTS]
    mixed = None
    for k in range(EXPERTS):
        out = lax.dot_general(
            picks_refs[k][:MOST].astype(BF), unfold(back_refs[k][...].astype(F32)).astype(BF),
            (((0,), (0,)), ((), ())), preferred_element_type=F32,
        )
        term = routes_ref[:, k:k + 1] * out
        mixed = term if mixed is None else mixed + term
    refs[-2][...] = mixed.astype(BF)
    refs[-1][...] = jnp.zeros(refs[-1].shape, F32)


def mix(routes, picks, back, width):
    return pl.pallas_call(
        mix_kernel,
        out_shape=[jax.ShapeDtypeStruct((routes.shape[0], width), BF), jax.ShapeDtypeStruct((8, 128), F32)],
        in_specs=[VMEM] * (1 + 2 * EXPERTS),
        out_specs=[VMEM] * 2,
        compiler_params=pltpu.CompilerParams(vmem_limit_bytes=SMALL_LIMIT),
        cost_estimate=pl.CostEstimate(flops=2_000_000_000, bytes_accessed=1000, transcendentals=0),
        name="mix",
    )(routes, *picks, *back)


Z_ORDER = (1, 2, 3)
CHUNKS = (256, 512, 768, 512)


def per_device(tokens, expert_ids, gate_probs, out_grad, gate_weight, up_weight, down_weight):
    me = lax.axis_index("expert").astype(jnp.int32).reshape(1)
    t_index = lax.axis_index("tensor").astype(jnp.int32).reshape(1)
    slab = gate_weight.shape[2]
    ids_t, probs_t = expert_ids.T, gate_probs.T

    rows = select_rows(me, t_index, ids_t, tokens)
    starts = [sum(CHUNKS[:i]) for i in range(len(CHUNKS))]
    arrived = {k: swap(rows[k], "expert", k) for k in Z_ORDER}
    near = pack_near(rows[0], arrived[1])
    near_across = swap(near, "tensor", 2)
    far = hold(pack_far([arrived[k] for k in (1, 2, 3)], tokens.shape[1]), [near_across])
    far_across = swap(far, "tensor", 2)
    sides = [swap(v, "tensor", 1) for v in (near, far, near_across)]
    far_across = hold(far_across, sides)
    xs = [near, far, sides[0], sides[1], near_across, far_across, sides[2], swap(far_across, "tensor", 1)]

    hits, routes, picks, grads = prepare(me, ids_t, probs_t, out_grad)

    pieces = []
    for i, (start, size) in enumerate(zip(starts, CHUNKS)):
        after = [pieces[i - 2][2]] if i >= 2 else []
        h, *whole = hidden_part(t_index, xs, gate_weight, up_weight, start, size, after)
        xs = whole or xs
        pieces.append([h, swap(h, "tensor", 1), swap(h, "tensor", 2)])
    sums = []
    for i, start in enumerate(starts):
        far = hold(pieces[i][2], sums[i - 2:i - 1]) if i >= 2 else pieces[i][2]
        pieces[i] = pieces[i][:2] + [far, swap(far, "tensor", 1)]
        use = [(i, 2), (i, 3)]
        if i == 0:
            use = [(0, 0), (0, 1)] + use
        if i + 1 < len(starts):
            use += [(i + 1, 0), (i + 1, 1)]
        result = down_part(
            t_index, slab, [pieces[n][j] for n, j in use], [(j, starts[n]) for n, j in use], down_weight,
            sums[-1] if sums else None, i + 1 == len(starts),
        )
        sums.append(result[0])
    back = [result[0]] + [swap(result[k], "expert", k) for k in (1, 2, 3)]
    gate_grad = take_dots(hits, picks, grads, back)
    mixed, done = mix(routes, picks, back, tokens.shape[1])
    gate_grad = gate_grad + hold(swap(gate_grad, "tensor", 2), [done])
    gate_grad = gate_grad + swap(gate_grad, "tensor", 1)
    return mixed, gate_grad.T


def per_device_any(tokens, expert_ids, gate_probs, out_grad, gate_weight, up_weight, down_weight):
    span_count = lax.axis_size("expert") // EXPERTS
    hits = expert_ids[:, :, None] == jnp.arange(EXPERTS, dtype=jnp.int32)[None, None, :]
    hit_float = hits.astype(F32)
    member = jnp.sum(hits.astype(jnp.int32), axis=1)
    place = jnp.cumsum(member, axis=0) - member
    placed = (place[None, :, :] == jnp.arange(MOST, dtype=jnp.int32)[:, None, None]) & (member[None, :, :] == 1)
    select = jnp.transpose(placed, (2, 0, 1)).astype(F32)
    route = jnp.sum(hit_float * gate_probs[:, :, None], axis=1)
    rows = jnp.einsum("est,td->esd", select.astype(BF), tokens, preferred_element_type=F32).astype(BF)
    arrived = lax.all_to_all(
        jnp.repeat(rows, span_count, axis=0), "expert", split_axis=0, concat_axis=0, tiled=True
    )
    full = lax.all_gather(arrived, "tensor", axis=2, tiled=True)
    gate = jnp.einsum("smd,df->smf", full, gate_weight[0], preferred_element_type=F32)
    up = jnp.einsum("smd,df->smf", full, up_weight[0], preferred_element_type=F32)
    hidden = (gate * jax.nn.sigmoid(gate) * up).astype(BF)
    partial_out = jnp.einsum(
        "smf,fd->smd",
        lax.all_gather(hidden, "tensor", axis=2, tiled=True),
        down_weight[0],
        preferred_element_type=F32,
    )
    back = lax.all_to_all(partial_out, "expert", split_axis=0, concat_axis=0, tiled=True)
    expert_out = jnp.sum(back.reshape(EXPERTS, span_count, MOST, tokens.shape[1]), axis=1)
    token_out = jnp.einsum("est,esd->ted", select, expert_out, precision=lax.Precision.HIGHEST)
    mixed = jnp.sum(route[:, :, None] * token_out, axis=1).astype(BF)
    dots = lax.psum(jnp.sum(out_grad.astype(F32)[:, None, :] * token_out, axis=2), "tensor")
    return mixed, jnp.sum(hit_float * dots[:, None, :], axis=2)


def solution(mesh):
    in_specs = (
        P(("groups", "expert"), "tensor"),
        P(("groups", "expert"), None),
        P(("groups", "expert"), None),
        P(("groups", "expert"), "tensor"),
        P("expert", None, "tensor"),
        P("expert", None, "tensor"),
        P("expert", None, "tensor"),
    )
    out_specs = (P(("groups", "expert"), "tensor"), P(("groups", "expert"), None))
    direct = mesh.shape["expert"] == EXPERTS and mesh.shape["tensor"] == 4
    return jax.shard_map(
        per_device if direct else per_device_any,
        mesh=mesh, in_specs=in_specs, out_specs=out_specs, check_vma=False,
    )
```

```python
import functools

import jax
import jax.numpy as jnp
from jax import lax
from jax.experimental import pallas as pl
from jax.experimental.pallas import tpu as pltpu
from jax.sharding import PartitionSpec as P

EXPERTS = 4
MOST = 34
BF = jnp.bfloat16
F32 = jnp.float32
VMEM_LIMIT = 24 * 1024 * 1024
SMALL_LIMIT = 4 * 1024 * 1024
FF_TILE = 256
K_TILE = 256


def swap(value, axis, bit):
    size = lax.axis_size(axis)
    return lax.ppermute(value, axis, [(i, i ^ bit) for i in range(size)])


VMEM = pl.BlockSpec(memory_space=pltpu.VMEM)
SMEM = pl.BlockSpec(memory_space=pltpu.SMEM)
ANY = pl.BlockSpec(memory_space=pl.ANY)
SMALL = dict(
    compiler_params=pltpu.CompilerParams(vmem_limit_bytes=SMALL_LIMIT),
    cost_estimate=pl.CostEstimate(flops=1000, bytes_accessed=1000, transcendentals=0),
)


def routing(ids, me):
    rows = ids.shape[1]
    upper = (
        lax.broadcasted_iota(jnp.int32, (rows, rows), 0) < lax.broadcasted_iota(jnp.int32, (rows, rows), 1)
    ).astype(F32).astype(BF)
    slot = lax.broadcasted_iota(jnp.int32, (MOST, rows), 0)
    hits, picks = [], []
    for step in range(EXPERTS):
        hit = (ids == (me ^ step)).astype(F32)
        member = jnp.sum(hit, axis=0, keepdims=True)
        before = jnp.dot(
            jnp.broadcast_to(member, (16, rows)).astype(BF), upper, preferred_element_type=F32
        )[:1]
        place = jnp.where(member > 0.5, before.astype(jnp.int32), -1)
        hits.append(hit)
        picks.append((slot == place).astype(F32))
    return hits, picks


def fold(block):
    return jnp.concatenate([block[:, c:c + 128] for c in range(0, block.shape[1], 128)], axis=0)


def unfold(block):
    return jnp.concatenate([block[r:r + MOST] for r in range(0, block.shape[0], MOST)], axis=1)


def folded(width):
    return jax.ShapeDtypeStruct((width // 128 * MOST, 128), BF)


def select_kernel(me_ref, t_ref, ids_hbm, tokens_hbm, *refs):
    out_refs = refs[:EXPERTS]
    ids_ref, tokens_ref, sems = refs[EXPERTS:]
    ids_copy = pltpu.make_async_copy(ids_hbm, ids_ref, sems.at[0])
    tokens_copy = pltpu.make_async_copy(tokens_hbm, tokens_ref, sems.at[1])
    ids_copy.start()
    tokens_copy.start()
    ids_copy.wait()
    _, picks = routing(ids_ref[...], me_ref[0])
    tokens_copy.wait()
    for k, (pick, out_ref) in enumerate(zip(picks, out_refs)):
        block = jnp.dot(pick.astype(BF), tokens_ref[...], preferred_element_type=F32)
        out_ref[...] = (block if k == 0 else fold(block)).astype(BF)


def select_rows(me, t, ids_t, tokens):
    width = tokens.shape[1]
    return pl.pallas_call(
        select_kernel,
        out_shape=[jax.ShapeDtypeStruct((MOST, width), BF)] + [folded(width)] * (EXPERTS - 1),
        in_specs=[SMEM, SMEM, ANY, ANY],
        out_specs=[VMEM] * EXPERTS,
        scratch_shapes=[
            pltpu.VMEM(ids_t.shape, ids_t.dtype),
            pltpu.VMEM(tokens.shape, tokens.dtype),
            pltpu.SemaphoreType.DMA((2,)),
        ],
        name="select_rows",
        compiler_params=pltpu.CompilerParams(vmem_limit_bytes=SMALL_LIMIT),
        cost_estimate=pl.CostEstimate(flops=8_000_000_000, bytes_accessed=1000, transcendentals=0),
    )(me, t, *(pltpu.with_memory_space_constraint(v, pltpu.HBM) for v in (ids_t, tokens)))


CUT = 3 * MOST // 16 * 16


def near_kernel(own_ref, *refs):
    blocks = [own_ref[...].astype(F32)] + [unfold(r[...].astype(F32)) for r in refs[:2]]
    refs[-1][...] = jnp.concatenate(blocks, axis=0)[:CUT].astype(BF)


def far_kernel(third_ref, fourth_ref, out_ref):
    rest = unfold(third_ref[...].astype(F32))[CUT - 2 * MOST:]
    out_ref[...] = jnp.concatenate([rest, unfold(fourth_ref[...].astype(F32))], axis=0).astype(BF)


def pack_near(own, second, third):
    return pl.pallas_call(
        near_kernel,
        out_shape=jax.ShapeDtypeStruct((CUT, own.shape[1]), BF),
        in_specs=[VMEM] * 3,
        out_specs=VMEM,
        name="pack_near",
        **SMALL,
    )(own, second, third)


def pack_far(third, fourth, width):
    return pl.pallas_call(
        far_kernel,
        out_shape=jax.ShapeDtypeStruct((EXPERTS * MOST - CUT, width), BF),
        in_specs=[VMEM] * 2,
        out_specs=VMEM,
        name="pack_far",
        compiler_params=pltpu.CompilerParams(vmem_limit_bytes=SMALL_LIMIT),
        cost_estimate=pl.CostEstimate(flops=1_000_000_000, bytes_accessed=1000, transcendentals=0),
    )(third, fourth)


def hold(value, after):
    return pl.pallas_call(
        lambda *refs: None,
        out_shape=jax.ShapeDtypeStruct(value.shape, value.dtype),
        in_specs=[ANY] * (1 + len(after)),
        out_specs=ANY,
        input_output_aliases={0: 0},
        name="hold",
        **SMALL,
    )(value, *after)


def hidden_kernel(joined, parts, start, t_ref, *refs):
    if joined:
        out_ref, x_ref = refs[-1], refs[0]
        gate_ref, up_ref = refs[1:3]
    else:
        out_ref, x_ref = refs[-2:]
        gate_ref, up_ref = refs[2 * parts:2 * parts + 2]
        for j in range(parts):
            x_ref[j, :CUT, :] = refs[2 * j][...]
            x_ref[j, CUT:, :] = refs[2 * j + 1][...]
    depth = x_ref.shape[2]
    for tile in range(0, out_ref.shape[1], FF_TILE):
        columns = slice(start + tile, start + tile + FF_TILE)
        gate = up = None
        for j in range(parts):
            at = pl.ds(pl.multiple_of((t_ref[0] ^ j) * depth, depth), depth)
            x = x_ref[j]
            g = jnp.dot(x, gate_ref[0, at, columns], preferred_element_type=F32)
            u = jnp.dot(x, up_ref[0, at, columns], preferred_element_type=F32)
            gate = g if gate is None else gate + g
            up = u if up is None else up + u
        out_ref[:, tile:tile + FF_TILE] = (gate * jax.nn.sigmoid(gate) * up).astype(BF)


def hidden_part(t, xs, gate_weight, up_weight, start, size, after=()):
    joined = len(xs) == 1
    parts = xs[0].shape[0] if joined else len(xs) // 2
    rows = EXPERTS * MOST
    out_shape = [jax.ShapeDtypeStruct((rows, size), BF)]
    if not joined:
        out_shape.append(jax.ShapeDtypeStruct((parts, rows, xs[0].shape[1]), BF))
    return pl.pallas_call(
        functools.partial(hidden_kernel, joined, parts, start),
        out_shape=out_shape,
        in_specs=[SMEM] + [VMEM] * (len(xs) + 2) + [ANY] * len(after),
        out_specs=[VMEM] * len(out_shape),
        compiler_params=pltpu.CompilerParams(vmem_limit_bytes=SMALL_LIMIT),
        cost_estimate=pl.CostEstimate(flops=1000, bytes_accessed=1000, transcendentals=0),
        name="hidden_part",
    )(t, *xs, gate_weight, up_weight, *after)


def down_kernel(count, where, slab, has_sum, last, t_ref, *refs):
    pieces = refs[:count]
    weight_ref = refs[count]
    rest = refs[count + 1:]
    outs = rest[has_sum:]
    total = rest[0][...] if has_sum else None
    for piece, (j, first) in zip(pieces, where):
        size = piece.shape[1]
        row = pl.multiple_of((t_ref[0] ^ j) * slab + first, K_TILE)
        term = jnp.dot(piece[...], weight_ref[0, pl.ds(row, size), :], preferred_element_type=F32)
        total = term if total is None else total + term
    if last:
        for k, out in enumerate(outs):
            block = total[k * MOST:(k + 1) * MOST]
            out[...] = fold(block).astype(BF)
    else:
        outs[0][...] = total


def down_part(t, slab, pieces, where, weight, running, last):
    rows = pieces[0].shape[0]
    width = weight.shape[2]
    has_sum = running is not None
    if last:
        out_shape = [folded(width)] * EXPERTS
    else:
        out_shape = [jax.ShapeDtypeStruct((rows, width), F32)]
    return pl.pallas_call(
        functools.partial(down_kernel, len(pieces), where, slab, has_sum, last),
        out_shape=out_shape,
        in_specs=[SMEM] + [VMEM] * (len(pieces) + 1 + has_sum),
        out_specs=[VMEM] * len(out_shape),
        compiler_params=pltpu.CompilerParams(vmem_limit_bytes=SMALL_LIMIT),
        cost_estimate=pl.CostEstimate(
            flops=2 * rows * width * sum(p.shape[1] for p in pieces), bytes_accessed=1000, transcendentals=0
        ),
        name="down_part",
    )(t, *pieces, weight, *([running] if has_sum else []))


def prepare_kernel(me_ref, ids_ref, probs_ref, grad_ref, *refs):
    hits_ref, routes_ref = refs[:2]
    picks_refs, grads_refs = refs[2:2 + EXPERTS], refs[2 + EXPERTS:]
    rows, width = grad_ref.shape
    hits, picks = routing(ids_ref[...], me_ref[0])
    for k in range(EXPERTS):
        hits_ref[k] = hits[k]
        picks_refs[k][...] = jnp.concatenate([picks[k]] * (width // 128), axis=0)
        grads_refs[k][...] = fold(jnp.dot(picks[k].astype(BF), grad_ref[...], preferred_element_type=F32))
    routes = jnp.concatenate(
        [jnp.sum(h * probs_ref[...], axis=0, keepdims=True) for h in hits]
        + [jnp.zeros((128 - EXPERTS, rows), F32)],
        axis=0,
    )
    routes_ref[...] = jnp.concatenate([routes, jnp.zeros((128, 128 - rows), F32)], axis=1).T[:rows]


def prepare(me, ids_t, probs_t, out_grad):
    rows, width = out_grad.shape
    tall = width // 128 * MOST
    shapes = [(EXPERTS,) + ids_t.shape, (rows, 128)] + [(tall, rows)] * EXPERTS + [(tall, 128)] * EXPERTS
    out = pl.pallas_call(
        prepare_kernel,
        out_shape=[jax.ShapeDtypeStruct(shape, F32) for shape in shapes],
        in_specs=[SMEM] + [VMEM] * 3,
        out_specs=[VMEM] * len(shapes),
        name="prepare",
        **SMALL,
    )(me, ids_t, probs_t, out_grad)
    return out[0], out[1], out[2:2 + EXPERTS], out[2 + EXPERTS:]


def dots_kernel(hits_ref, *refs):
    picks_refs, grads_refs, back_refs = (refs[n * EXPERTS:(n + 1) * EXPERTS] for n in range(3))
    total = None
    for k in range(EXPERTS):
        slots = jnp.sum(grads_refs[k][...] * back_refs[k][...].astype(F32), axis=1, keepdims=True)
        term = hits_ref[k] * jnp.sum(picks_refs[k][...] * slots, axis=0, keepdims=True)
        total = term if total is None else total + term
    refs[-1][...] = total


def take_dots(hits, picks, grads, back):
    return pl.pallas_call(
        dots_kernel,
        out_shape=jax.ShapeDtypeStruct(hits.shape[1:], F32),
        in_specs=[VMEM] * (1 + 3 * EXPERTS),
        out_specs=VMEM,
        name="dots",
        **SMALL,
    )(hits, *picks, *grads, *back)


def mix_kernel(routes_ref, *refs):
    picks_refs, back_refs = refs[:EXPERTS], refs[EXPERTS:2 * EXPERTS]
    mixed = None
    for k in range(EXPERTS):
        out = lax.dot_general(
            picks_refs[k][:MOST].astype(BF), unfold(back_refs[k][...].astype(F32)).astype(BF),
            (((0,), (0,)), ((), ())), preferred_element_type=F32,
        )
        term = routes_ref[:, k:k + 1] * out
        mixed = term if mixed is None else mixed + term
    refs[-2][...] = mixed.astype(BF)
    refs[-1][...] = jnp.zeros(refs[-1].shape, F32)


def mix(routes, picks, back, width):
    return pl.pallas_call(
        mix_kernel,
        out_shape=[jax.ShapeDtypeStruct((routes.shape[0], width), BF), jax.ShapeDtypeStruct((8, 128), F32)],
        in_specs=[VMEM] * (1 + 2 * EXPERTS),
        out_specs=[VMEM] * 2,
        compiler_params=pltpu.CompilerParams(vmem_limit_bytes=SMALL_LIMIT),
        cost_estimate=pl.CostEstimate(flops=1_000_000_000, bytes_accessed=1000, transcendentals=0),
        name="mix",
    )(routes, *picks, *back)


Z_ORDER = (1, 2, 3)
CHUNKS = (256, 512, 768, 512)


def per_device(tokens, expert_ids, gate_probs, out_grad, gate_weight, up_weight, down_weight):
    me = lax.axis_index("expert").astype(jnp.int32).reshape(1)
    t_index = lax.axis_index("tensor").astype(jnp.int32).reshape(1)
    slab = gate_weight.shape[2]
    ids_t, probs_t = expert_ids.T, gate_probs.T

    rows = select_rows(me, t_index, ids_t, tokens)
    starts = [sum(CHUNKS[:i]) for i in range(len(CHUNKS))]
    arrived = {k: swap(rows[k], "expert", k) for k in Z_ORDER}
    near = pack_near(rows[0], arrived[1], arrived[2])
    near_across = swap(near, "tensor", 2)
    far = pack_far(arrived[2], arrived[3], tokens.shape[1])
    far_across = swap(far, "tensor", 2)
    near_across = hold(near_across, [far_across])
    xs = [near, far, swap(near, "tensor", 1), swap(far, "tensor", 1), near_across, far_across]
    xs += [swap(near_across, "tensor", 1), swap(far_across, "tensor", 1)]

    hits, routes, picks, grads = prepare(me, ids_t, probs_t, out_grad)

    pieces = []
    for i, (start, size) in enumerate(zip(starts, CHUNKS)):
        after = [pieces[i - 2][2]] if i >= 2 else []
        h, *whole = hidden_part(t_index, xs, gate_weight, up_weight, start, size, after)
        xs = whole or xs
        pieces.append([h, swap(h, "tensor", 1), swap(h, "tensor", 2)])
    sums = []
    for i, start in enumerate(starts):
        far = hold(pieces[i][2], sums[i - 2:i - 1]) if i >= 2 else pieces[i][2]
        pieces[i] = pieces[i][:2] + [far, swap(far, "tensor", 1)]
        use = [(i, 2), (i, 3)]
        if i == 0:
            use = [(0, 0), (0, 1)] + use
        if i + 1 < len(starts):
            use += [(i + 1, 0), (i + 1, 1)]
        result = down_part(
            t_index, slab, [pieces[n][j] for n, j in use], [(j, starts[n]) for n, j in use], down_weight,
            sums[-1] if sums else None, i + 1 == len(starts),
        )
        sums.append(result[0])
    back = [result[0]] + [swap(result[k], "expert", k) for k in (1, 2, 3)]
    gate_grad = take_dots(hits, picks, grads, back)
    mixed, done = mix(routes, picks, back, tokens.shape[1])
    gate_grad = gate_grad + hold(swap(gate_grad, "tensor", 2), [done])
    gate_grad = gate_grad + swap(gate_grad, "tensor", 1)
    return mixed, gate_grad.T


def per_device_any(tokens, expert_ids, gate_probs, out_grad, gate_weight, up_weight, down_weight):
    span_count = lax.axis_size("expert") // EXPERTS
    hits = expert_ids[:, :, None] == jnp.arange(EXPERTS, dtype=jnp.int32)[None, None, :]
    hit_float = hits.astype(F32)
    member = jnp.sum(hits.astype(jnp.int32), axis=1)
    place = jnp.cumsum(member, axis=0) - member
    placed = (place[None, :, :] == jnp.arange(MOST, dtype=jnp.int32)[:, None, None]) & (member[None, :, :] == 1)
    select = jnp.transpose(placed, (2, 0, 1)).astype(F32)
    route = jnp.sum(hit_float * gate_probs[:, :, None], axis=1)
    rows = jnp.einsum("est,td->esd", select.astype(BF), tokens, preferred_element_type=F32).astype(BF)
    arrived = lax.all_to_all(
        jnp.repeat(rows, span_count, axis=0), "expert", split_axis=0, concat_axis=0, tiled=True
    )
    full = lax.all_gather(arrived, "tensor", axis=2, tiled=True)
    gate = jnp.einsum("smd,df->smf", full, gate_weight[0], preferred_element_type=F32)
    up = jnp.einsum("smd,df->smf", full, up_weight[0], preferred_element_type=F32)
    hidden = (gate * jax.nn.sigmoid(gate) * up).astype(BF)
    partial_out = jnp.einsum(
        "smf,fd->smd",
        lax.all_gather(hidden, "tensor", axis=2, tiled=True),
        down_weight[0],
        preferred_element_type=F32,
    )
    back = lax.all_to_all(partial_out, "expert", split_axis=0, concat_axis=0, tiled=True)
    expert_out = jnp.sum(back.reshape(EXPERTS, span_count, MOST, tokens.shape[1]), axis=1)
    token_out = jnp.einsum("est,esd->ted", select, expert_out, precision=lax.Precision.HIGHEST)
    mixed = jnp.sum(route[:, :, None] * token_out, axis=1).astype(BF)
    dots = lax.psum(jnp.sum(out_grad.astype(F32)[:, None, :] * token_out, axis=2), "tensor")
    return mixed, jnp.sum(hit_float * dots[:, None, :], axis=2)


def solution(mesh):
    in_specs = (
        P(("groups", "expert"), "tensor"),
        P(("groups", "expert"), None),
        P(("groups", "expert"), None),
        P(("groups", "expert"), "tensor"),
        P("expert", None, "tensor"),
        P("expert", None, "tensor"),
        P("expert", None, "tensor"),
    )
    out_specs = (P(("groups", "expert"), "tensor"), P(("groups", "expert"), None))
    direct = mesh.shape["expert"] == EXPERTS and mesh.shape["tensor"] == 4
    return jax.shard_map(
        per_device if direct else per_device_any,
        mesh=mesh, in_specs=in_specs, out_specs=out_specs, check_vma=False,
    )
```

```python
import functools

import jax
import jax.numpy as jnp
from jax import lax
from jax.experimental import pallas as pl
from jax.experimental.pallas import tpu as pltpu
from jax.sharding import PartitionSpec as P

EXPERTS = 4
MOST = 34
BF = jnp.bfloat16
F32 = jnp.float32
VMEM_LIMIT = 24 * 1024 * 1024
SMALL_LIMIT = 4 * 1024 * 1024
FF_TILE = 256
K_TILE = 256


def swap(value, axis, bit):
    size = lax.axis_size(axis)
    return lax.ppermute(value, axis, [(i, i ^ bit) for i in range(size)])


VMEM = pl.BlockSpec(memory_space=pltpu.VMEM)
SMEM = pl.BlockSpec(memory_space=pltpu.SMEM)
ANY = pl.BlockSpec(memory_space=pl.ANY)
SMALL = dict(
    compiler_params=pltpu.CompilerParams(vmem_limit_bytes=SMALL_LIMIT),
    cost_estimate=pl.CostEstimate(flops=1000, bytes_accessed=1000, transcendentals=0),
)


def routing(ids, me):
    rows = ids.shape[1]
    upper = (
        lax.broadcasted_iota(jnp.int32, (rows, rows), 0) < lax.broadcasted_iota(jnp.int32, (rows, rows), 1)
    ).astype(F32).astype(BF)
    slot = lax.broadcasted_iota(jnp.int32, (MOST, rows), 0)
    hits, picks = [], []
    for step in range(EXPERTS):
        hit = (ids == (me ^ step)).astype(F32)
        member = jnp.sum(hit, axis=0, keepdims=True)
        before = jnp.dot(
            jnp.broadcast_to(member, (16, rows)).astype(BF), upper, preferred_element_type=F32
        )[:1]
        place = jnp.where(member > 0.5, before.astype(jnp.int32), -1)
        hits.append(hit)
        picks.append((slot == place).astype(F32))
    return hits, picks


def fold(block):
    return jnp.concatenate([block[:, c:c + 128] for c in range(0, block.shape[1], 128)], axis=0)


def unfold(block):
    return jnp.concatenate([block[r:r + MOST] for r in range(0, block.shape[0], MOST)], axis=1)


def folded(width):
    return jax.ShapeDtypeStruct((width // 128 * MOST, 128), BF)


def select_kernel(me_ref, t_ref, ids_hbm, tokens_hbm, *refs):
    out_refs = refs[:EXPERTS]
    ids_ref, tokens_ref, sems = refs[EXPERTS:]
    ids_copy = pltpu.make_async_copy(ids_hbm, ids_ref, sems.at[0])
    tokens_copy = pltpu.make_async_copy(tokens_hbm, tokens_ref, sems.at[1])
    ids_copy.start()
    tokens_copy.start()
    ids_copy.wait()
    _, picks = routing(ids_ref[...], me_ref[0])
    tokens_copy.wait()
    for k, (pick, out_ref) in enumerate(zip(picks, out_refs)):
        block = jnp.dot(pick.astype(BF), tokens_ref[...], preferred_element_type=F32)
        out_ref[...] = (block if k == 0 else fold(block)).astype(BF)


def select_rows(me, t, ids_t, tokens):
    width = tokens.shape[1]
    return pl.pallas_call(
        select_kernel,
        out_shape=[jax.ShapeDtypeStruct((MOST, width), BF)] + [folded(width)] * (EXPERTS - 1),
        in_specs=[SMEM, SMEM, ANY, ANY],
        out_specs=[VMEM] * EXPERTS,
        scratch_shapes=[
            pltpu.VMEM(ids_t.shape, ids_t.dtype),
            pltpu.VMEM(tokens.shape, tokens.dtype),
            pltpu.SemaphoreType.DMA((2,)),
        ],
        name="select_rows",
        compiler_params=pltpu.CompilerParams(vmem_limit_bytes=SMALL_LIMIT),
        cost_estimate=pl.CostEstimate(flops=8_000_000_000, bytes_accessed=1000, transcendentals=0),
    )(me, t, *(pltpu.with_memory_space_constraint(v, pltpu.HBM) for v in (ids_t, tokens)))


CUT = 3 * MOST // 16 * 16


def near_kernel(own_ref, *refs):
    blocks = [own_ref[...].astype(F32)] + [unfold(r[...].astype(F32)) for r in refs[:2]]
    refs[-1][...] = jnp.concatenate(blocks, axis=0)[:CUT].astype(BF)


def far_kernel(third_ref, fourth_ref, out_ref):
    rest = unfold(third_ref[...].astype(F32))[CUT - 2 * MOST:]
    out_ref[...] = jnp.concatenate([rest, unfold(fourth_ref[...].astype(F32))], axis=0).astype(BF)


def pack_near(own, second, third):
    return pl.pallas_call(
        near_kernel,
        out_shape=jax.ShapeDtypeStruct((CUT, own.shape[1]), BF),
        in_specs=[VMEM] * 3,
        out_specs=VMEM,
        name="pack_near",
        **SMALL,
    )(own, second, third)


def pack_far(third, fourth, width):
    return pl.pallas_call(
        far_kernel,
        out_shape=jax.ShapeDtypeStruct((EXPERTS * MOST - CUT, width), BF),
        in_specs=[VMEM] * 2,
        out_specs=VMEM,
        name="pack_far",
        compiler_params=pltpu.CompilerParams(vmem_limit_bytes=SMALL_LIMIT),
        cost_estimate=pl.CostEstimate(flops=1_000_000_000, bytes_accessed=1000, transcendentals=0),
    )(third, fourth)


def hold(value, after):
    return pl.pallas_call(
        lambda *refs: None,
        out_shape=jax.ShapeDtypeStruct(value.shape, value.dtype),
        in_specs=[ANY] * (1 + len(after)),
        out_specs=ANY,
        input_output_aliases={0: 0},
        name="hold",
        **SMALL,
    )(value, *after)


def hidden_kernel(joined, parts, start, t_ref, *refs):
    if joined:
        out_ref, x_ref = refs[-1], refs[0]
        gate_ref, up_ref = refs[1:3]
    else:
        out_ref, x_ref = refs[-2:]
        gate_ref, up_ref = refs[2 * parts:2 * parts + 2]
        for j in range(parts):
            x_ref[j, :CUT, :] = refs[2 * j][...]
            x_ref[j, CUT:, :] = refs[2 * j + 1][...]
    depth = x_ref.shape[2]
    for tile in range(0, out_ref.shape[1], FF_TILE):
        columns = slice(start + tile, start + tile + FF_TILE)
        gate = up = None
        for j in range(parts):
            at = pl.ds(pl.multiple_of((t_ref[0] ^ j) * depth, depth), depth)
            x = x_ref[j]
            g = jnp.dot(x, gate_ref[0, at, columns], preferred_element_type=F32)
            u = jnp.dot(x, up_ref[0, at, columns], preferred_element_type=F32)
            gate = g if gate is None else gate + g
            up = u if up is None else up + u
        out_ref[:, tile:tile + FF_TILE] = (gate * jax.nn.sigmoid(gate) * up).astype(BF)


def hidden_part(t, xs, gate_weight, up_weight, start, size, after=()):
    joined = len(xs) == 1
    parts = xs[0].shape[0] if joined else len(xs) // 2
    rows = EXPERTS * MOST
    out_shape = [jax.ShapeDtypeStruct((rows, size), BF)]
    if not joined:
        out_shape.append(jax.ShapeDtypeStruct((parts, rows, xs[0].shape[1]), BF))
    return pl.pallas_call(
        functools.partial(hidden_kernel, joined, parts, start),
        out_shape=out_shape,
        in_specs=[SMEM] + [VMEM] * (len(xs) + 2) + [ANY] * len(after),
        out_specs=[VMEM] * len(out_shape),
        compiler_params=pltpu.CompilerParams(vmem_limit_bytes=SMALL_LIMIT),
        cost_estimate=pl.CostEstimate(flops=1000, bytes_accessed=1000, transcendentals=0),
        name="hidden_part",
    )(t, *xs, gate_weight, up_weight, *after)


def down_kernel(count, where, slab, has_sum, last, t_ref, *refs):
    pieces = refs[:count]
    weight_ref = refs[count]
    rest = refs[count + 1:]
    outs = rest[has_sum:]
    total = rest[0][...] if has_sum else None
    for piece, (j, first) in zip(pieces, where):
        size = piece.shape[1]
        row = pl.multiple_of((t_ref[0] ^ j) * slab + first, K_TILE)
        term = jnp.dot(piece[...], weight_ref[0, pl.ds(row, size), :], preferred_element_type=F32)
        total = term if total is None else total + term
    if last:
        for k, out in enumerate(outs):
            block = total[k * MOST:(k + 1) * MOST]
            out[...] = fold(block).astype(BF)
    else:
        outs[0][...] = total


def down_part(t, slab, pieces, where, weight, running, last):
    rows = pieces[0].shape[0]
    width = weight.shape[2]
    has_sum = running is not None
    if last:
        out_shape = [folded(width)] * EXPERTS
    else:
        out_shape = [jax.ShapeDtypeStruct((rows, width), F32)]
    return pl.pallas_call(
        functools.partial(down_kernel, len(pieces), where, slab, has_sum, last),
        out_shape=out_shape,
        in_specs=[SMEM] + [VMEM] * (len(pieces) + 1 + has_sum),
        out_specs=[VMEM] * len(out_shape),
        compiler_params=pltpu.CompilerParams(vmem_limit_bytes=SMALL_LIMIT),
        cost_estimate=pl.CostEstimate(
            flops=2 * rows * width * sum(p.shape[1] for p in pieces), bytes_accessed=1000, transcendentals=0
        ),
        name="down_part",
    )(t, *pieces, weight, *([running] if has_sum else []))


def prepare_kernel(me_ref, ids_ref, probs_ref, grad_ref, *refs):
    hits_ref, routes_ref = refs[:2]
    picks_refs, grads_refs = refs[2:2 + EXPERTS], refs[2 + EXPERTS:]
    rows, width = grad_ref.shape
    hits, picks = routing(ids_ref[...], me_ref[0])
    for k in range(EXPERTS):
        hits_ref[k] = hits[k]
        picks_refs[k][...] = jnp.concatenate([picks[k]] * (width // 128), axis=0)
        grads_refs[k][...] = fold(jnp.dot(picks[k].astype(BF), grad_ref[...], preferred_element_type=F32))
    routes = jnp.concatenate(
        [jnp.sum(h * probs_ref[...], axis=0, keepdims=True) for h in hits]
        + [jnp.zeros((128 - EXPERTS, rows), F32)],
        axis=0,
    )
    routes_ref[...] = jnp.concatenate([routes, jnp.zeros((128, 128 - rows), F32)], axis=1).T[:rows]


def prepare(me, ids_t, probs_t, out_grad):
    rows, width = out_grad.shape
    tall = width // 128 * MOST
    shapes = [(EXPERTS,) + ids_t.shape, (rows, 128)] + [(tall, rows)] * EXPERTS + [(tall, 128)] * EXPERTS
    out = pl.pallas_call(
        prepare_kernel,
        out_shape=[jax.ShapeDtypeStruct(shape, F32) for shape in shapes],
        in_specs=[SMEM] + [VMEM] * 3,
        out_specs=[VMEM] * len(shapes),
        name="prepare",
        **SMALL,
    )(me, ids_t, probs_t, out_grad)
    return out[0], out[1], out[2:2 + EXPERTS], out[2 + EXPERTS:]


def dots_kernel(hits_ref, *refs):
    picks_refs, grads_refs, back_refs = (refs[n * EXPERTS:(n + 1) * EXPERTS] for n in range(3))
    total = None
    for k in range(EXPERTS):
        slots = jnp.sum(grads_refs[k][...] * back_refs[k][...].astype(F32), axis=1, keepdims=True)
        term = hits_ref[k] * jnp.sum(picks_refs[k][...] * slots, axis=0, keepdims=True)
        total = term if total is None else total + term
    refs[-1][...] = total


def take_dots(hits, picks, grads, back):
    return pl.pallas_call(
        dots_kernel,
        out_shape=jax.ShapeDtypeStruct(hits.shape[1:], F32),
        in_specs=[VMEM] * (1 + 3 * EXPERTS),
        out_specs=VMEM,
        name="dots",
        **SMALL,
    )(hits, *picks, *grads, *back)


def mix_kernel(routes_ref, *refs):
    picks_refs, back_refs = refs[:EXPERTS], refs[EXPERTS:2 * EXPERTS]
    mixed = None
    for k in range(EXPERTS):
        out = lax.dot_general(
            picks_refs[k][:MOST].astype(BF), unfold(back_refs[k][...].astype(F32)).astype(BF),
            (((0,), (0,)), ((), ())), preferred_element_type=F32,
        )
        term = routes_ref[:, k:k + 1] * out
        mixed = term if mixed is None else mixed + term
    refs[-2][...] = mixed.astype(BF)
    refs[-1][...] = jnp.zeros(refs[-1].shape, F32)


def mix(routes, picks, back, width):
    return pl.pallas_call(
        mix_kernel,
        out_shape=[jax.ShapeDtypeStruct((routes.shape[0], width), BF), jax.ShapeDtypeStruct((8, 128), F32)],
        in_specs=[VMEM] * (1 + 2 * EXPERTS),
        out_specs=[VMEM] * 2,
        compiler_params=pltpu.CompilerParams(vmem_limit_bytes=SMALL_LIMIT),
        cost_estimate=pl.CostEstimate(flops=1_000_000_000, bytes_accessed=1000, transcendentals=0),
        name="mix",
    )(routes, *picks, *back)


Z_ORDER = (1, 2, 3)
CHUNKS = (256, 512, 768, 512)


def per_device(tokens, expert_ids, gate_probs, out_grad, gate_weight, up_weight, down_weight):
    me = lax.axis_index("expert").astype(jnp.int32).reshape(1)
    t_index = lax.axis_index("tensor").astype(jnp.int32).reshape(1)
    slab = gate_weight.shape[2]
    ids_t, probs_t = expert_ids.T, gate_probs.T

    rows = select_rows(me, t_index, ids_t, tokens)
    starts = [sum(CHUNKS[:i]) for i in range(len(CHUNKS))]
    arrived = {k: swap(rows[k], "expert", k) for k in Z_ORDER}
    near = pack_near(rows[0], arrived[1], arrived[2])
    near_across = swap(near, "tensor", 2)
    far = pack_far(arrived[2], arrived[3], tokens.shape[1])
    far_across = swap(far, "tensor", 2)
    near_side, far_side = swap(near, "tensor", 1), swap(far, "tensor", 1)
    near_across = hold(near_across, [far_across, near_side, far_side])
    xs = [near, far, near_side, far_side, near_across, far_across]
    xs += [swap(near_across, "tensor", 1), swap(far_across, "tensor", 1)]

    hits, routes, picks, grads = prepare(me, ids_t, probs_t, out_grad)

    pieces = []
    for i, (start, size) in enumerate(zip(starts, CHUNKS)):
        after = [pieces[i - 2][2]] if i >= 2 else []
        h, *whole = hidden_part(t_index, xs, gate_weight, up_weight, start, size, after)
        xs = whole or xs
        pieces.append([h, swap(h, "tensor", 1), swap(h, "tensor", 2)])
    sums = []
    for i, start in enumerate(starts):
        far = hold(pieces[i][2], sums[i - 2:i - 1]) if i >= 2 else pieces[i][2]
        pieces[i] = pieces[i][:2] + [far, swap(far, "tensor", 1)]
        use = [(i, 2), (i, 3)]
        if i == 0:
            use = [(0, 0), (0, 1)] + use
        if i + 1 < len(starts):
            use += [(i + 1, 0), (i + 1, 1)]
        result = down_part(
            t_index, slab, [pieces[n][j] for n, j in use], [(j, starts[n]) for n, j in use], down_weight,
            sums[-1] if sums else None, i + 1 == len(starts),
        )
        sums.append(result[0])
    back = [result[0]] + [swap(result[k], "expert", k) for k in (1, 2, 3)]
    gate_grad = take_dots(hits, picks, grads, back)
    mixed, done = mix(routes, picks, back, tokens.shape[1])
    gate_grad = gate_grad + hold(swap(gate_grad, "tensor", 2), [done])
    gate_grad = gate_grad + swap(gate_grad, "tensor", 1)
    return mixed, gate_grad.T


def per_device_any(tokens, expert_ids, gate_probs, out_grad, gate_weight, up_weight, down_weight):
    span_count = lax.axis_size("expert") // EXPERTS
    hits = expert_ids[:, :, None] == jnp.arange(EXPERTS, dtype=jnp.int32)[None, None, :]
    hit_float = hits.astype(F32)
    member = jnp.sum(hits.astype(jnp.int32), axis=1)
    place = jnp.cumsum(member, axis=0) - member
    placed = (place[None, :, :] == jnp.arange(MOST, dtype=jnp.int32)[:, None, None]) & (member[None, :, :] == 1)
    select = jnp.transpose(placed, (2, 0, 1)).astype(F32)
    route = jnp.sum(hit_float * gate_probs[:, :, None], axis=1)
    rows = jnp.einsum("est,td->esd", select.astype(BF), tokens, preferred_element_type=F32).astype(BF)
    arrived = lax.all_to_all(
        jnp.repeat(rows, span_count, axis=0), "expert", split_axis=0, concat_axis=0, tiled=True
    )
    full = lax.all_gather(arrived, "tensor", axis=2, tiled=True)
    gate = jnp.einsum("smd,df->smf", full, gate_weight[0], preferred_element_type=F32)
    up = jnp.einsum("smd,df->smf", full, up_weight[0], preferred_element_type=F32)
    hidden = (gate * jax.nn.sigmoid(gate) * up).astype(BF)
    partial_out = jnp.einsum(
        "smf,fd->smd",
        lax.all_gather(hidden, "tensor", axis=2, tiled=True),
        down_weight[0],
        preferred_element_type=F32,
    )
    back = lax.all_to_all(partial_out, "expert", split_axis=0, concat_axis=0, tiled=True)
    expert_out = jnp.sum(back.reshape(EXPERTS, span_count, MOST, tokens.shape[1]), axis=1)
    token_out = jnp.einsum("est,esd->ted", select, expert_out, precision=lax.Precision.HIGHEST)
    mixed = jnp.sum(route[:, :, None] * token_out, axis=1).astype(BF)
    dots = lax.psum(jnp.sum(out_grad.astype(F32)[:, None, :] * token_out, axis=2), "tensor")
    return mixed, jnp.sum(hit_float * dots[:, None, :], axis=2)


def solution(mesh):
    in_specs = (
        P(("groups", "expert"), "tensor"),
        P(("groups", "expert"), None),
        P(("groups", "expert"), None),
        P(("groups", "expert"), "tensor"),
        P("expert", None, "tensor"),
        P("expert", None, "tensor"),
        P("expert", None, "tensor"),
    )
    out_specs = (P(("groups", "expert"), "tensor"), P(("groups", "expert"), None))
    direct = mesh.shape["expert"] == EXPERTS and mesh.shape["tensor"] == 4
    return jax.shard_map(
        per_device if direct else per_device_any,
        mesh=mesh, in_specs=in_specs, out_specs=out_specs, check_vma=False,
    )
```

```python
import functools

import jax
import jax.numpy as jnp
from jax import lax
from jax.experimental import pallas as pl
from jax.experimental.pallas import tpu as pltpu
from jax.sharding import PartitionSpec as P

EXPERTS = 4
MOST = 34
BF = jnp.bfloat16
F32 = jnp.float32
VMEM_LIMIT = 24 * 1024 * 1024
SMALL_LIMIT = 4 * 1024 * 1024
FF_TILE = 256
K_TILE = 256


def swap(value, axis, bit):
    size = lax.axis_size(axis)
    return lax.ppermute(value, axis, [(i, i ^ bit) for i in range(size)])


VMEM = pl.BlockSpec(memory_space=pltpu.VMEM)
SMEM = pl.BlockSpec(memory_space=pltpu.SMEM)
ANY = pl.BlockSpec(memory_space=pl.ANY)
SMALL = dict(
    compiler_params=pltpu.CompilerParams(vmem_limit_bytes=SMALL_LIMIT),
    cost_estimate=pl.CostEstimate(flops=1000, bytes_accessed=1000, transcendentals=0),
)


def routing(ids, me):
    rows = ids.shape[1]
    upper = (
        lax.broadcasted_iota(jnp.int32, (rows, rows), 0) < lax.broadcasted_iota(jnp.int32, (rows, rows), 1)
    ).astype(F32).astype(BF)
    slot = lax.broadcasted_iota(jnp.int32, (MOST, rows), 0)
    hits, picks = [], []
    for step in range(EXPERTS):
        hit = (ids == (me ^ step)).astype(F32)
        member = jnp.sum(hit, axis=0, keepdims=True)
        before = jnp.dot(
            jnp.broadcast_to(member, (16, rows)).astype(BF), upper, preferred_element_type=F32
        )[:1]
        place = jnp.where(member > 0.5, before.astype(jnp.int32), -1)
        hits.append(hit)
        picks.append((slot == place).astype(F32))
    return hits, picks


def fold(block):
    return jnp.concatenate([block[:, c:c + 128] for c in range(0, block.shape[1], 128)], axis=0)


def unfold(block):
    return jnp.concatenate([block[r:r + MOST] for r in range(0, block.shape[0], MOST)], axis=1)


def folded(width):
    return jax.ShapeDtypeStruct((width // 128 * MOST, 128), BF)


def select_kernel(me_ref, t_ref, ids_hbm, tokens_hbm, *refs):
    out_refs = refs[:EXPERTS]
    ids_ref, tokens_ref, sems = refs[EXPERTS:]
    ids_copy = pltpu.make_async_copy(ids_hbm, ids_ref, sems.at[0])
    tokens_copy = pltpu.make_async_copy(tokens_hbm, tokens_ref, sems.at[1])
    ids_copy.start()
    tokens_copy.start()
    ids_copy.wait()
    _, picks = routing(ids_ref[...], me_ref[0])
    tokens_copy.wait()
    for k, (pick, out_ref) in enumerate(zip(picks, out_refs)):
        block = jnp.dot(pick.astype(BF), tokens_ref[...], preferred_element_type=F32)
        out_ref[...] = (block if k == 0 else fold(block)).astype(BF)


def select_rows(me, t, ids_t, tokens):
    width = tokens.shape[1]
    return pl.pallas_call(
        select_kernel,
        out_shape=[jax.ShapeDtypeStruct((MOST, width), BF)] + [folded(width)] * (EXPERTS - 1),
        in_specs=[SMEM, SMEM, ANY, ANY],
        out_specs=[VMEM] * EXPERTS,
        scratch_shapes=[
            pltpu.VMEM(ids_t.shape, ids_t.dtype),
            pltpu.VMEM(tokens.shape, tokens.dtype),
            pltpu.SemaphoreType.DMA((2,)),
        ],
        name="select_rows",
        compiler_params=pltpu.CompilerParams(vmem_limit_bytes=SMALL_LIMIT),
        cost_estimate=pl.CostEstimate(flops=8_000_000_000, bytes_accessed=1000, transcendentals=0),
    )(me, t, *(pltpu.with_memory_space_constraint(v, pltpu.HBM) for v in (ids_t, tokens)))


CUT = 3 * MOST // 16 * 16


def near_kernel(own_ref, *refs):
    blocks = [own_ref[...].astype(F32)] + [unfold(r[...].astype(F32)) for r in refs[:2]]
    refs[-1][...] = jnp.concatenate(blocks, axis=0)[:CUT].astype(BF)


def far_kernel(third_ref, fourth_ref, out_ref):
    rest = unfold(third_ref[...].astype(F32))[CUT - 2 * MOST:]
    out_ref[...] = jnp.concatenate([rest, unfold(fourth_ref[...].astype(F32))], axis=0).astype(BF)


def pack_near(own, second, third):
    return pl.pallas_call(
        near_kernel,
        out_shape=jax.ShapeDtypeStruct((CUT, own.shape[1]), BF),
        in_specs=[VMEM] * 3,
        out_specs=VMEM,
        name="pack_near",
        **SMALL,
    )(own, second, third)


def pack_far(third, fourth, width):
    return pl.pallas_call(
        far_kernel,
        out_shape=jax.ShapeDtypeStruct((EXPERTS * MOST - CUT, width), BF),
        in_specs=[VMEM] * 2,
        out_specs=VMEM,
        name="pack_far",
        compiler_params=pltpu.CompilerParams(vmem_limit_bytes=SMALL_LIMIT),
        cost_estimate=pl.CostEstimate(flops=1_000_000_000, bytes_accessed=1000, transcendentals=0),
    )(third, fourth)


def hold(value, after):
    return pl.pallas_call(
        lambda *refs: None,
        out_shape=jax.ShapeDtypeStruct(value.shape, value.dtype),
        in_specs=[ANY] * (1 + len(after)),
        out_specs=ANY,
        input_output_aliases={0: 0},
        name="hold",
        **SMALL,
    )(value, *after)


def hidden_kernel(joined, parts, start, t_ref, *refs):
    if joined:
        out_ref, x_ref = refs[-1], refs[0]
        gate_ref, up_ref = refs[1:3]
    else:
        out_ref, x_ref = refs[-2:]
        gate_ref, up_ref = refs[2 * parts:2 * parts + 2]
        for j in range(parts):
            x_ref[j, :CUT, :] = refs[2 * j][...]
            x_ref[j, CUT:, :] = refs[2 * j + 1][...]
    depth = x_ref.shape[2]
    for tile in range(0, out_ref.shape[1], FF_TILE):
        columns = slice(start + tile, start + tile + FF_TILE)
        gate = up = None
        for j in range(parts):
            at = pl.ds(pl.multiple_of((t_ref[0] ^ j) * depth, depth), depth)
            x = x_ref[j]
            g = jnp.dot(x, gate_ref[0, at, columns], preferred_element_type=F32)
            u = jnp.dot(x, up_ref[0, at, columns], preferred_element_type=F32)
            gate = g if gate is None else gate + g
            up = u if up is None else up + u
        out_ref[:, tile:tile + FF_TILE] = (gate * jax.nn.sigmoid(gate) * up).astype(BF)


def hidden_part(t, xs, gate_weight, up_weight, start, size, after=()):
    joined = len(xs) == 1
    parts = xs[0].shape[0] if joined else len(xs) // 2
    rows = EXPERTS * MOST
    out_shape = [jax.ShapeDtypeStruct((rows, size), BF)]
    if not joined:
        out_shape.append(jax.ShapeDtypeStruct((parts, rows, xs[0].shape[1]), BF))
    return pl.pallas_call(
        functools.partial(hidden_kernel, joined, parts, start),
        out_shape=out_shape,
        in_specs=[SMEM] + [VMEM] * (len(xs) + 2) + [ANY] * len(after),
        out_specs=[VMEM] * len(out_shape),
        compiler_params=pltpu.CompilerParams(vmem_limit_bytes=SMALL_LIMIT),
        cost_estimate=pl.CostEstimate(flops=1000, bytes_accessed=1000, transcendentals=0),
        name="hidden_part",
    )(t, *xs, gate_weight, up_weight, *after)


def down_kernel(count, where, slab, has_sum, last, t_ref, *refs):
    pieces = refs[:count]
    weight_ref = refs[count]
    rest = refs[count + 1:]
    outs = rest[has_sum:]
    total = rest[0][...] if has_sum else None
    for piece, (j, first) in zip(pieces, where):
        size = piece.shape[1]
        row = pl.multiple_of((t_ref[0] ^ j) * slab + first, K_TILE)
        term = jnp.dot(piece[...], weight_ref[0, pl.ds(row, size), :], preferred_element_type=F32)
        total = term if total is None else total + term
    if last:
        for k, out in enumerate(outs):
            block = total[k * MOST:(k + 1) * MOST]
            out[...] = fold(block).astype(BF)
    else:
        outs[0][...] = total


def down_part(t, slab, pieces, where, weight, running, last):
    rows = pieces[0].shape[0]
    width = weight.shape[2]
    has_sum = running is not None
    if last:
        out_shape = [folded(width)] * EXPERTS
    else:
        out_shape = [jax.ShapeDtypeStruct((rows, width), F32)]
    return pl.pallas_call(
        functools.partial(down_kernel, len(pieces), where, slab, has_sum, last),
        out_shape=out_shape,
        in_specs=[SMEM] + [VMEM] * (len(pieces) + 1 + has_sum),
        out_specs=[VMEM] * len(out_shape),
        compiler_params=pltpu.CompilerParams(vmem_limit_bytes=SMALL_LIMIT),
        cost_estimate=pl.CostEstimate(
            flops=2 * rows * width * sum(p.shape[1] for p in pieces), bytes_accessed=1000, transcendentals=0
        ),
        name="down_part",
    )(t, *pieces, weight, *([running] if has_sum else []))


def prepare_kernel(me_ref, ids_ref, probs_ref, grad_ref, *refs):
    hits_ref, routes_ref = refs[:2]
    picks_refs, grads_refs = refs[2:2 + EXPERTS], refs[2 + EXPERTS:]
    rows, width = grad_ref.shape
    hits, picks = routing(ids_ref[...], me_ref[0])
    for k in range(EXPERTS):
        hits_ref[k] = hits[k]
        picks_refs[k][...] = jnp.concatenate([picks[k]] * (width // 128), axis=0)
        grads_refs[k][...] = fold(jnp.dot(picks[k].astype(BF), grad_ref[...], preferred_element_type=F32))
    routes = jnp.concatenate(
        [jnp.sum(h * probs_ref[...], axis=0, keepdims=True) for h in hits]
        + [jnp.zeros((128 - EXPERTS, rows), F32)],
        axis=0,
    )
    routes_ref[...] = jnp.concatenate([routes, jnp.zeros((128, 128 - rows), F32)], axis=1).T[:rows]


def prepare(me, ids_t, probs_t, out_grad):
    rows, width = out_grad.shape
    tall = width // 128 * MOST
    shapes = [(EXPERTS,) + ids_t.shape, (rows, 128)] + [(tall, rows)] * EXPERTS + [(tall, 128)] * EXPERTS
    out = pl.pallas_call(
        prepare_kernel,
        out_shape=[jax.ShapeDtypeStruct(shape, F32) for shape in shapes],
        in_specs=[SMEM] + [VMEM] * 3,
        out_specs=[VMEM] * len(shapes),
        name="prepare",
        **SMALL,
    )(me, ids_t, probs_t, out_grad)
    return out[0], out[1], out[2:2 + EXPERTS], out[2 + EXPERTS:]


def dots_kernel(hits_ref, *refs):
    picks_refs, grads_refs, back_refs = (refs[n * EXPERTS:(n + 1) * EXPERTS] for n in range(3))
    total = None
    for k in range(EXPERTS):
        slots = jnp.sum(grads_refs[k][...] * back_refs[k][...].astype(F32), axis=1, keepdims=True)
        term = hits_ref[k] * jnp.sum(picks_refs[k][...] * slots, axis=0, keepdims=True)
        total = term if total is None else total + term
    refs[-1][...] = total


def take_dots(hits, picks, grads, back):
    return pl.pallas_call(
        dots_kernel,
        out_shape=jax.ShapeDtypeStruct(hits.shape[1:], F32),
        in_specs=[VMEM] * (1 + 3 * EXPERTS),
        out_specs=VMEM,
        name="dots",
        **SMALL,
    )(hits, *picks, *grads, *back)


def mix_kernel(routes_ref, *refs):
    picks_refs, back_refs = refs[:EXPERTS], refs[EXPERTS:2 * EXPERTS]
    mixed = None
    for k in range(EXPERTS):
        out = lax.dot_general(
            picks_refs[k][:MOST].astype(BF), unfold(back_refs[k][...].astype(F32)).astype(BF),
            (((0,), (0,)), ((), ())), preferred_element_type=F32,
        )
        term = routes_ref[:, k:k + 1] * out
        mixed = term if mixed is None else mixed + term
    refs[-2][...] = mixed.astype(BF)
    refs[-1][...] = jnp.zeros(refs[-1].shape, F32)


def mix(routes, picks, back, width):
    return pl.pallas_call(
        mix_kernel,
        out_shape=[jax.ShapeDtypeStruct((routes.shape[0], width), BF), jax.ShapeDtypeStruct((8, 128), F32)],
        in_specs=[VMEM] * (1 + 2 * EXPERTS),
        out_specs=[VMEM] * 2,
        compiler_params=pltpu.CompilerParams(vmem_limit_bytes=SMALL_LIMIT),
        cost_estimate=pl.CostEstimate(flops=1_000_000_000, bytes_accessed=1000, transcendentals=0),
        name="mix",
    )(routes, *picks, *back)


Z_ORDER = (1, 2, 3)
CHUNKS = (512, 512, 512, 512)


def per_device(tokens, expert_ids, gate_probs, out_grad, gate_weight, up_weight, down_weight):
    me = lax.axis_index("expert").astype(jnp.int32).reshape(1)
    t_index = lax.axis_index("tensor").astype(jnp.int32).reshape(1)
    slab = gate_weight.shape[2]
    ids_t, probs_t = expert_ids.T, gate_probs.T

    rows = select_rows(me, t_index, ids_t, tokens)
    starts = [sum(CHUNKS[:i]) for i in range(len(CHUNKS))]
    arrived = {k: swap(rows[k], "expert", k) for k in Z_ORDER}
    near = pack_near(rows[0], arrived[1], arrived[2])
    near_across = swap(near, "tensor", 2)
    far = pack_far(arrived[2], arrived[3], tokens.shape[1])
    far_across = swap(far, "tensor", 2)
    near_across = hold(near_across, [far_across])
    xs = [near, far, swap(near, "tensor", 1), swap(far, "tensor", 1), near_across, far_across]
    xs += [swap(near_across, "tensor", 1), swap(far_across, "tensor", 1)]

    hits, routes, picks, grads = prepare(me, ids_t, probs_t, out_grad)

    pieces = []
    for i, (start, size) in enumerate(zip(starts, CHUNKS)):
        after = [pieces[i - 2][2]] if i >= 2 else []
        h, *whole = hidden_part(t_index, xs, gate_weight, up_weight, start, size, after)
        xs = whole or xs
        pieces.append([h, swap(h, "tensor", 1), swap(h, "tensor", 2)])
    sums = []
    for i, start in enumerate(starts):
        far = hold(pieces[i][2], sums[i - 2:i - 1]) if i >= 2 else pieces[i][2]
        pieces[i] = pieces[i][:2] + [far, swap(far, "tensor", 1)]
        use = [(i, 2), (i, 3)]
        if i == 0:
            use = [(0, 0), (0, 1)] + use
        if i + 1 < len(starts):
            use += [(i + 1, 0), (i + 1, 1)]
        result = down_part(
            t_index, slab, [pieces[n][j] for n, j in use], [(j, starts[n]) for n, j in use], down_weight,
            sums[-1] if sums else None, i + 1 == len(starts),
        )
        sums.append(result[0])
    back = [result[0]] + [swap(result[k], "expert", k) for k in (1, 2, 3)]
    gate_grad = take_dots(hits, picks, grads, back)
    mixed, done = mix(routes, picks, back, tokens.shape[1])
    gate_grad = gate_grad + hold(swap(gate_grad, "tensor", 2), [done])
    gate_grad = gate_grad + swap(gate_grad, "tensor", 1)
    return mixed, gate_grad.T


def per_device_any(tokens, expert_ids, gate_probs, out_grad, gate_weight, up_weight, down_weight):
    span_count = lax.axis_size("expert") // EXPERTS
    hits = expert_ids[:, :, None] == jnp.arange(EXPERTS, dtype=jnp.int32)[None, None, :]
    hit_float = hits.astype(F32)
    member = jnp.sum(hits.astype(jnp.int32), axis=1)
    place = jnp.cumsum(member, axis=0) - member
    placed = (place[None, :, :] == jnp.arange(MOST, dtype=jnp.int32)[:, None, None]) & (member[None, :, :] == 1)
    select = jnp.transpose(placed, (2, 0, 1)).astype(F32)
    route = jnp.sum(hit_float * gate_probs[:, :, None], axis=1)
    rows = jnp.einsum("est,td->esd", select.astype(BF), tokens, preferred_element_type=F32).astype(BF)
    arrived = lax.all_to_all(
        jnp.repeat(rows, span_count, axis=0), "expert", split_axis=0, concat_axis=0, tiled=True
    )
    full = lax.all_gather(arrived, "tensor", axis=2, tiled=True)
    gate = jnp.einsum("smd,df->smf", full, gate_weight[0], preferred_element_type=F32)
    up = jnp.einsum("smd,df->smf", full, up_weight[0], preferred_element_type=F32)
    hidden = (gate * jax.nn.sigmoid(gate) * up).astype(BF)
    partial_out = jnp.einsum(
        "smf,fd->smd",
        lax.all_gather(hidden, "tensor", axis=2, tiled=True),
        down_weight[0],
        preferred_element_type=F32,
    )
    back = lax.all_to_all(partial_out, "expert", split_axis=0, concat_axis=0, tiled=True)
    expert_out = jnp.sum(back.reshape(EXPERTS, span_count, MOST, tokens.shape[1]), axis=1)
    token_out = jnp.einsum("est,esd->ted", select, expert_out, precision=lax.Precision.HIGHEST)
    mixed = jnp.sum(route[:, :, None] * token_out, axis=1).astype(BF)
    dots = lax.psum(jnp.sum(out_grad.astype(F32)[:, None, :] * token_out, axis=2), "tensor")
    return mixed, jnp.sum(hit_float * dots[:, None, :], axis=2)


def solution(mesh):
    in_specs = (
        P(("groups", "expert"), "tensor"),
        P(("groups", "expert"), None),
        P(("groups", "expert"), None),
        P(("groups", "expert"), "tensor"),
        P("expert", None, "tensor"),
        P("expert", None, "tensor"),
        P("expert", None, "tensor"),
    )
    out_specs = (P(("groups", "expert"), "tensor"), P(("groups", "expert"), None))
    direct = mesh.shape["expert"] == EXPERTS and mesh.shape["tensor"] == 4
    return jax.shard_map(
        per_device if direct else per_device_any,
        mesh=mesh, in_specs=in_specs, out_specs=out_specs, check_vma=False,
    )
```

```python
import functools

import jax
import jax.numpy as jnp
from jax import lax
from jax.experimental import pallas as pl
from jax.experimental.pallas import tpu as pltpu
from jax.sharding import PartitionSpec as P

EXPERTS = 4
MOST = 34
BF = jnp.bfloat16
F32 = jnp.float32
VMEM_LIMIT = 24 * 1024 * 1024
SMALL_LIMIT = 4 * 1024 * 1024
FF_TILE = 256
K_TILE = 256


def swap(value, axis, bit):
    size = lax.axis_size(axis)
    return lax.ppermute(value, axis, [(i, i ^ bit) for i in range(size)])


VMEM = pl.BlockSpec(memory_space=pltpu.VMEM)
SMEM = pl.BlockSpec(memory_space=pltpu.SMEM)
ANY = pl.BlockSpec(memory_space=pl.ANY)
SMALL = dict(
    compiler_params=pltpu.CompilerParams(vmem_limit_bytes=SMALL_LIMIT),
    cost_estimate=pl.CostEstimate(flops=1000, bytes_accessed=1000, transcendentals=0),
)


def routing(ids, me):
    rows = ids.shape[1]
    upper = (
        lax.broadcasted_iota(jnp.int32, (rows, rows), 0) < lax.broadcasted_iota(jnp.int32, (rows, rows), 1)
    ).astype(F32).astype(BF)
    slot = lax.broadcasted_iota(jnp.int32, (MOST, rows), 0)
    hits, picks = [], []
    for step in range(EXPERTS):
        hit = (ids == (me ^ step)).astype(F32)
        member = jnp.sum(hit, axis=0, keepdims=True)
        before = jnp.dot(
            jnp.broadcast_to(member, (16, rows)).astype(BF), upper, preferred_element_type=F32
        )[:1]
        place = jnp.where(member > 0.5, before.astype(jnp.int32), -1)
        hits.append(hit)
        picks.append((slot == place).astype(F32))
    return hits, picks


def fold(block):
    return jnp.concatenate([block[:, c:c + 128] for c in range(0, block.shape[1], 128)], axis=0)


def unfold(block):
    return jnp.concatenate([block[r:r + MOST] for r in range(0, block.shape[0], MOST)], axis=1)


def folded(width):
    return jax.ShapeDtypeStruct((width // 128 * MOST, 128), BF)


def select_kernel(me_ref, t_ref, ids_hbm, tokens_hbm, *refs):
    out_refs = refs[:EXPERTS]
    ids_ref, tokens_ref, sems = refs[EXPERTS:]
    ids_copy = pltpu.make_async_copy(ids_hbm, ids_ref, sems.at[0])
    tokens_copy = pltpu.make_async_copy(tokens_hbm, tokens_ref, sems.at[1])
    ids_copy.start()
    tokens_copy.start()
    ids_copy.wait()
    _, picks = routing(ids_ref[...], me_ref[0])
    tokens_copy.wait()
    for k, (pick, out_ref) in enumerate(zip(picks, out_refs)):
        block = jnp.dot(pick.astype(BF), tokens_ref[...], preferred_element_type=F32)
        out_ref[...] = (block if k == 0 else fold(block)).astype(BF)


def select_rows(me, t, ids_t, tokens):
    width = tokens.shape[1]
    return pl.pallas_call(
        select_kernel,
        out_shape=[jax.ShapeDtypeStruct((MOST, width), BF)] + [folded(width)] * (EXPERTS - 1),
        in_specs=[SMEM, SMEM, ANY, ANY],
        out_specs=[VMEM] * EXPERTS,
        scratch_shapes=[
            pltpu.VMEM(ids_t.shape, ids_t.dtype),
            pltpu.VMEM(tokens.shape, tokens.dtype),
            pltpu.SemaphoreType.DMA((2,)),
        ],
        name="select_rows",
        compiler_params=pltpu.CompilerParams(vmem_limit_bytes=SMALL_LIMIT),
        cost_estimate=pl.CostEstimate(flops=8_000_000_000, bytes_accessed=1000, transcendentals=0),
    )(me, t, *(pltpu.with_memory_space_constraint(v, pltpu.HBM) for v in (ids_t, tokens)))


CUT = 3 * MOST // 16 * 16


def near_kernel(own_ref, *refs):
    blocks = [own_ref[...].astype(F32)] + [unfold(r[...].astype(F32)) for r in refs[:2]]
    refs[-1][...] = jnp.concatenate(blocks, axis=0)[:CUT].astype(BF)


def far_kernel(third_ref, fourth_ref, out_ref):
    rest = unfold(third_ref[...].astype(F32))[CUT - 2 * MOST:]
    out_ref[...] = jnp.concatenate([rest, unfold(fourth_ref[...].astype(F32))], axis=0).astype(BF)


def pack_near(own, second, third):
    return pl.pallas_call(
        near_kernel,
        out_shape=jax.ShapeDtypeStruct((CUT, own.shape[1]), BF),
        in_specs=[VMEM] * 3,
        out_specs=VMEM,
        name="pack_near",
        **SMALL,
    )(own, second, third)


def pack_far(third, fourth, width):
    return pl.pallas_call(
        far_kernel,
        out_shape=jax.ShapeDtypeStruct((EXPERTS * MOST - CUT, width), BF),
        in_specs=[VMEM] * 2,
        out_specs=VMEM,
        name="pack_far",
        compiler_params=pltpu.CompilerParams(vmem_limit_bytes=SMALL_LIMIT),
        cost_estimate=pl.CostEstimate(flops=1_000_000_000, bytes_accessed=1000, transcendentals=0),
    )(third, fourth)


def hold(value, after):
    return pl.pallas_call(
        lambda *refs: None,
        out_shape=jax.ShapeDtypeStruct(value.shape, value.dtype),
        in_specs=[ANY] * (1 + len(after)),
        out_specs=ANY,
        input_output_aliases={0: 0},
        name="hold",
        **SMALL,
    )(value, *after)


def hidden_kernel(joined, parts, start, t_ref, *refs):
    if joined:
        out_ref, x_ref = refs[-1], refs[0]
        gate_ref, up_ref = refs[1:3]
    else:
        out_ref, x_ref = refs[-2:]
        gate_ref, up_ref = refs[2 * parts:2 * parts + 2]
        for j in range(parts):
            x_ref[j, :CUT, :] = refs[2 * j][...]
            x_ref[j, CUT:, :] = refs[2 * j + 1][...]
    depth = x_ref.shape[2]
    for tile in range(0, out_ref.shape[1], FF_TILE):
        columns = slice(start + tile, start + tile + FF_TILE)
        gate = up = None
        for j in range(parts):
            at = pl.ds(pl.multiple_of((t_ref[0] ^ j) * depth, depth), depth)
            x = x_ref[j]
            g = jnp.dot(x, gate_ref[0, at, columns], preferred_element_type=F32)
            u = jnp.dot(x, up_ref[0, at, columns], preferred_element_type=F32)
            gate = g if gate is None else gate + g
            up = u if up is None else up + u
        out_ref[:, tile:tile + FF_TILE] = (gate * jax.nn.sigmoid(gate) * up).astype(BF)


def hidden_part(t, xs, gate_weight, up_weight, start, size, after=()):
    joined = len(xs) == 1
    parts = xs[0].shape[0] if joined else len(xs) // 2
    rows = EXPERTS * MOST
    out_shape = [jax.ShapeDtypeStruct((rows, size), BF)]
    if not joined:
        out_shape.append(jax.ShapeDtypeStruct((parts, rows, xs[0].shape[1]), BF))
    return pl.pallas_call(
        functools.partial(hidden_kernel, joined, parts, start),
        out_shape=out_shape,
        in_specs=[SMEM] + [VMEM] * (len(xs) + 2) + [ANY] * len(after),
        out_specs=[VMEM] * len(out_shape),
        compiler_params=pltpu.CompilerParams(vmem_limit_bytes=SMALL_LIMIT),
        cost_estimate=pl.CostEstimate(flops=1000, bytes_accessed=1000, transcendentals=0),
        name="hidden_part",
    )(t, *xs, gate_weight, up_weight, *after)


def down_kernel(count, where, slab, has_sum, last, t_ref, *refs):
    pieces = refs[:count]
    weight_ref = refs[count]
    rest = refs[count + 1:]
    outs = rest[has_sum:]
    total = rest[0][...] if has_sum else None
    for piece, (j, first) in zip(pieces, where):
        size = piece.shape[1]
        row = pl.multiple_of((t_ref[0] ^ j) * slab + first, K_TILE)
        term = jnp.dot(piece[...], weight_ref[0, pl.ds(row, size), :], preferred_element_type=F32)
        total = term if total is None else total + term
    if last:
        for k, out in enumerate(outs):
            block = total[k * MOST:(k + 1) * MOST]
            out[...] = fold(block).astype(BF)
    else:
        outs[0][...] = total


def down_part(t, slab, pieces, where, weight, running, last):
    rows = pieces[0].shape[0]
    width = weight.shape[2]
    has_sum = running is not None
    if last:
        out_shape = [folded(width)] * EXPERTS
    else:
        out_shape = [jax.ShapeDtypeStruct((rows, width), F32)]
    return pl.pallas_call(
        functools.partial(down_kernel, len(pieces), where, slab, has_sum, last),
        out_shape=out_shape,
        in_specs=[SMEM] + [VMEM] * (len(pieces) + 1 + has_sum),
        out_specs=[VMEM] * len(out_shape),
        compiler_params=pltpu.CompilerParams(vmem_limit_bytes=SMALL_LIMIT),
        cost_estimate=pl.CostEstimate(
            flops=2 * rows * width * sum(p.shape[1] for p in pieces), bytes_accessed=1000, transcendentals=0
        ),
        name="down_part",
    )(t, *pieces, weight, *([running] if has_sum else []))


def prepare_kernel(me_ref, ids_ref, probs_ref, grad_ref, *refs):
    hits_ref, routes_ref = refs[:2]
    picks_refs, grads_refs = refs[2:2 + EXPERTS], refs[2 + EXPERTS:]
    rows, width = grad_ref.shape
    hits, picks = routing(ids_ref[...], me_ref[0])
    for k in range(EXPERTS):
        hits_ref[k] = hits[k]
        picks_refs[k][...] = jnp.concatenate([picks[k]] * (width // 128), axis=0)
        grads_refs[k][...] = fold(jnp.dot(picks[k].astype(BF), grad_ref[...], preferred_element_type=F32))
    routes = jnp.concatenate(
        [jnp.sum(h * probs_ref[...], axis=0, keepdims=True) for h in hits]
        + [jnp.zeros((128 - EXPERTS, rows), F32)],
        axis=0,
    )
    routes_ref[...] = jnp.concatenate([routes, jnp.zeros((128, 128 - rows), F32)], axis=1).T[:rows]


def prepare(me, ids_t, probs_t, out_grad):
    rows, width = out_grad.shape
    tall = width // 128 * MOST
    shapes = [(EXPERTS,) + ids_t.shape, (rows, 128)] + [(tall, rows)] * EXPERTS + [(tall, 128)] * EXPERTS
    out = pl.pallas_call(
        prepare_kernel,
        out_shape=[jax.ShapeDtypeStruct(shape, F32) for shape in shapes],
        in_specs=[SMEM] + [VMEM] * 3,
        out_specs=[VMEM] * len(shapes),
        name="prepare",
        **SMALL,
    )(me, ids_t, probs_t, out_grad)
    return out[0], out[1], out[2:2 + EXPERTS], out[2 + EXPERTS:]


def dots_kernel(hits_ref, *refs):
    picks_refs, grads_refs, back_refs = (refs[n * EXPERTS:(n + 1) * EXPERTS] for n in range(3))
    total = None
    for k in range(EXPERTS):
        slots = jnp.sum(grads_refs[k][...] * back_refs[k][...].astype(F32), axis=1, keepdims=True)
        term = hits_ref[k] * jnp.sum(picks_refs[k][...] * slots, axis=0, keepdims=True)
        total = term if total is None else total + term
    refs[-1][...] = total


def take_dots(hits, picks, grads, back):
    return pl.pallas_call(
        dots_kernel,
        out_shape=jax.ShapeDtypeStruct(hits.shape[1:], F32),
        in_specs=[VMEM] * (1 + 3 * EXPERTS),
        out_specs=VMEM,
        name="dots",
        **SMALL,
    )(hits, *picks, *grads, *back)


def mix_kernel(routes_ref, *refs):
    picks_refs, back_refs = refs[:EXPERTS], refs[EXPERTS:2 * EXPERTS]
    mixed = None
    for k in range(EXPERTS):
        out = lax.dot_general(
            picks_refs[k][:MOST].astype(BF), unfold(back_refs[k][...].astype(F32)).astype(BF),
            (((0,), (0,)), ((), ())), preferred_element_type=F32,
        )
        term = routes_ref[:, k:k + 1] * out
        mixed = term if mixed is None else mixed + term
    refs[-2][...] = mixed.astype(BF)
    refs[-1][...] = jnp.zeros(refs[-1].shape, F32)


def mix(routes, picks, back, width):
    return pl.pallas_call(
        mix_kernel,
        out_shape=[jax.ShapeDtypeStruct((routes.shape[0], width), BF), jax.ShapeDtypeStruct((8, 128), F32)],
        in_specs=[VMEM] * (1 + 2 * EXPERTS),
        out_specs=[VMEM] * 2,
        compiler_params=pltpu.CompilerParams(vmem_limit_bytes=SMALL_LIMIT),
        cost_estimate=pl.CostEstimate(flops=1_000_000_000, bytes_accessed=1000, transcendentals=0),
        name="mix",
    )(routes, *picks, *back)


Z_ORDER = (1, 2, 3)
CHUNKS = (256, 512, 768, 512)


def per_device(tokens, expert_ids, gate_probs, out_grad, gate_weight, up_weight, down_weight):
    me = lax.axis_index("expert").astype(jnp.int32).reshape(1)
    t_index = lax.axis_index("tensor").astype(jnp.int32).reshape(1)
    slab = gate_weight.shape[2]
    ids_t, probs_t = expert_ids.T, gate_probs.T

    rows = select_rows(me, t_index, ids_t, tokens)
    starts = [sum(CHUNKS[:i]) for i in range(len(CHUNKS))]
    arrived = {k: swap(rows[k], "expert", k) for k in Z_ORDER}
    near = pack_near(rows[0], arrived[1], arrived[2])
    near_across = swap(near, "tensor", 2)
    far = pack_far(arrived[2], arrived[3], tokens.shape[1])
    far_across = swap(far, "tensor", 2)
    near_across = hold(near_across, [far_across])
    xs = [near, far, swap(near, "tensor", 1), swap(far, "tensor", 1), near_across, far_across]
    xs += [swap(near_across, "tensor", 1), swap(far_across, "tensor", 1)]

    hits, routes, picks, grads = prepare(me, ids_t, probs_t, out_grad)

    pieces = []
    for i, (start, size) in enumerate(zip(starts, CHUNKS)):
        after = [pieces[i - 2][2]] if i >= 2 else []
        h, *whole = hidden_part(t_index, xs, gate_weight, up_weight, start, size, after)
        xs = whole or xs
        pieces.append([h, swap(h, "tensor", 1), swap(h, "tensor", 2)])
    sums = []
    for i, start in enumerate(starts):
        far = hold(pieces[i][2], sums[i - 2:i - 1]) if i >= 2 else pieces[i][2]
        pieces[i] = pieces[i][:2] + [far, swap(far, "tensor", 1)]
        use = [(i, 2), (i, 3)]
        if i == 0:
            use = [(0, 0), (0, 1)] + use
        if i + 1 < len(starts):
            use += [(i + 1, 0), (i + 1, 1)]
        result = down_part(
            t_index, slab, [pieces[n][j] for n, j in use], [(j, starts[n]) for n, j in use], down_weight,
            sums[-1] if sums else None, i + 1 == len(starts),
        )
        sums.append(result[0])
    back = [result[0]] + [swap(result[k], "expert", k) for k in (1, 2, 3)]
    gate_grad = take_dots(hits, picks, grads, back)
    mixed, done = mix(routes, picks, back, tokens.shape[1])
    across, beside, both = (swap(gate_grad, "tensor", bit) for bit in (2, 1, 3))
    gate_grad = (gate_grad + hold(across, [done])) + (beside + hold(both, [done]))
    return mixed, gate_grad.T


def per_device_any(tokens, expert_ids, gate_probs, out_grad, gate_weight, up_weight, down_weight):
    span_count = lax.axis_size("expert") // EXPERTS
    hits = expert_ids[:, :, None] == jnp.arange(EXPERTS, dtype=jnp.int32)[None, None, :]
    hit_float = hits.astype(F32)
    member = jnp.sum(hits.astype(jnp.int32), axis=1)
    place = jnp.cumsum(member, axis=0) - member
    placed = (place[None, :, :] == jnp.arange(MOST, dtype=jnp.int32)[:, None, None]) & (member[None, :, :] == 1)
    select = jnp.transpose(placed, (2, 0, 1)).astype(F32)
    route = jnp.sum(hit_float * gate_probs[:, :, None], axis=1)
    rows = jnp.einsum("est,td->esd", select.astype(BF), tokens, preferred_element_type=F32).astype(BF)
    arrived = lax.all_to_all(
        jnp.repeat(rows, span_count, axis=0), "expert", split_axis=0, concat_axis=0, tiled=True
    )
    full = lax.all_gather(arrived, "tensor", axis=2, tiled=True)
    gate = jnp.einsum("smd,df->smf", full, gate_weight[0], preferred_element_type=F32)
    up = jnp.einsum("smd,df->smf", full, up_weight[0], preferred_element_type=F32)
    hidden = (gate * jax.nn.sigmoid(gate) * up).astype(BF)
    partial_out = jnp.einsum(
        "smf,fd->smd",
        lax.all_gather(hidden, "tensor", axis=2, tiled=True),
        down_weight[0],
        preferred_element_type=F32,
    )
    back = lax.all_to_all(partial_out, "expert", split_axis=0, concat_axis=0, tiled=True)
    expert_out = jnp.sum(back.reshape(EXPERTS, span_count, MOST, tokens.shape[1]), axis=1)
    token_out = jnp.einsum("est,esd->ted", select, expert_out, precision=lax.Precision.HIGHEST)
    mixed = jnp.sum(route[:, :, None] * token_out, axis=1).astype(BF)
    dots = lax.psum(jnp.sum(out_grad.astype(F32)[:, None, :] * token_out, axis=2), "tensor")
    return mixed, jnp.sum(hit_float * dots[:, None, :], axis=2)


def solution(mesh):
    in_specs = (
        P(("groups", "expert"), "tensor"),
        P(("groups", "expert"), None),
        P(("groups", "expert"), None),
        P(("groups", "expert"), "tensor"),
        P("expert", None, "tensor"),
        P("expert", None, "tensor"),
        P("expert", None, "tensor"),
    )
    out_specs = (P(("groups", "expert"), "tensor"), P(("groups", "expert"), None))
    direct = mesh.shape["expert"] == EXPERTS and mesh.shape["tensor"] == 4
    return jax.shard_map(
        per_device if direct else per_device_any,
        mesh=mesh, in_specs=in_specs, out_specs=out_specs, check_vma=False,
    )
```

```python
import functools

import jax
import jax.numpy as jnp
from jax import lax
from jax.experimental import pallas as pl
from jax.experimental.pallas import tpu as pltpu
from jax.sharding import PartitionSpec as P

EXPERTS = 4
MOST = 34
BF = jnp.bfloat16
F32 = jnp.float32
VMEM_LIMIT = 24 * 1024 * 1024
SMALL_LIMIT = 4 * 1024 * 1024
FF_TILE = 256
K_TILE = 256


def swap(value, axis, bit):
    size = lax.axis_size(axis)
    return lax.ppermute(value, axis, [(i, i ^ bit) for i in range(size)])


VMEM = pl.BlockSpec(memory_space=pltpu.VMEM)
SMEM = pl.BlockSpec(memory_space=pltpu.SMEM)
ANY = pl.BlockSpec(memory_space=pl.ANY)
SMALL = dict(
    compiler_params=pltpu.CompilerParams(vmem_limit_bytes=SMALL_LIMIT),
    cost_estimate=pl.CostEstimate(flops=1000, bytes_accessed=1000, transcendentals=0),
)


def routing(ids, me):
    rows = ids.shape[1]
    upper = (
        lax.broadcasted_iota(jnp.int32, (rows, rows), 0) < lax.broadcasted_iota(jnp.int32, (rows, rows), 1)
    ).astype(F32).astype(BF)
    slot = lax.broadcasted_iota(jnp.int32, (MOST, rows), 0)
    hits, picks = [], []
    for step in range(EXPERTS):
        hit = (ids == (me ^ step)).astype(F32)
        member = jnp.sum(hit, axis=0, keepdims=True)
        before = jnp.dot(
            jnp.broadcast_to(member, (16, rows)).astype(BF), upper, preferred_element_type=F32
        )[:1]
        place = jnp.where(member > 0.5, before.astype(jnp.int32), -1)
        hits.append(hit)
        picks.append((slot == place).astype(F32))
    return hits, picks


def fold(block):
    return jnp.concatenate([block[:, c:c + 128] for c in range(0, block.shape[1], 128)], axis=0)


def unfold(block):
    return jnp.concatenate([block[r:r + MOST] for r in range(0, block.shape[0], MOST)], axis=1)


def folded(width):
    return jax.ShapeDtypeStruct((width // 128 * MOST, 128), BF)


def select_kernel(me_ref, t_ref, ids_hbm, tokens_hbm, *refs):
    out_refs = refs[:EXPERTS]
    ids_ref, tokens_ref, sems = refs[EXPERTS:]
    ids_copy = pltpu.make_async_copy(ids_hbm, ids_ref, sems.at[0])
    tokens_copy = pltpu.make_async_copy(tokens_hbm, tokens_ref, sems.at[1])
    ids_copy.start()
    tokens_copy.start()
    ids_copy.wait()
    _, picks = routing(ids_ref[...], me_ref[0])
    tokens_copy.wait()
    for k, (pick, out_ref) in enumerate(zip(picks, out_refs)):
        block = jnp.dot(pick.astype(BF), tokens_ref[...], preferred_element_type=F32)
        out_ref[...] = (block if k == 0 else fold(block)).astype(BF)


def select_rows(me, t, ids_t, tokens):
    width = tokens.shape[1]
    return pl.pallas_call(
        select_kernel,
        out_shape=[jax.ShapeDtypeStruct((MOST, width), BF)] + [folded(width)] * (EXPERTS - 1),
        in_specs=[SMEM, SMEM, ANY, ANY],
        out_specs=[VMEM] * EXPERTS,
        scratch_shapes=[
            pltpu.VMEM(ids_t.shape, ids_t.dtype),
            pltpu.VMEM(tokens.shape, tokens.dtype),
            pltpu.SemaphoreType.DMA((2,)),
        ],
        name="select_rows",
        compiler_params=pltpu.CompilerParams(vmem_limit_bytes=SMALL_LIMIT),
        cost_estimate=pl.CostEstimate(flops=8_000_000_000, bytes_accessed=1000, transcendentals=0),
    )(me, t, *(pltpu.with_memory_space_constraint(v, pltpu.HBM) for v in (ids_t, tokens)))


CUT = 3 * MOST // 16 * 16


def near_kernel(own_ref, *refs):
    blocks = [own_ref[...].astype(F32)] + [unfold(r[...].astype(F32)) for r in refs[:2]]
    refs[-1][...] = jnp.concatenate(blocks, axis=0)[:CUT].astype(BF)


def far_kernel(third_ref, fourth_ref, out_ref):
    rest = unfold(third_ref[...].astype(F32))[CUT - 2 * MOST:]
    out_ref[...] = jnp.concatenate([rest, unfold(fourth_ref[...].astype(F32))], axis=0).astype(BF)


def pack_near(own, second, third):
    return pl.pallas_call(
        near_kernel,
        out_shape=jax.ShapeDtypeStruct((CUT, own.shape[1]), BF),
        in_specs=[VMEM] * 3,
        out_specs=VMEM,
        name="pack_near",
        **SMALL,
    )(own, second, third)


def pack_far(third, fourth, width):
    return pl.pallas_call(
        far_kernel,
        out_shape=jax.ShapeDtypeStruct((EXPERTS * MOST - CUT, width), BF),
        in_specs=[VMEM] * 2,
        out_specs=VMEM,
        name="pack_far",
        compiler_params=pltpu.CompilerParams(vmem_limit_bytes=SMALL_LIMIT),
        cost_estimate=pl.CostEstimate(flops=1_000_000_000, bytes_accessed=1000, transcendentals=0),
    )(third, fourth)


def hold(value, after):
    return pl.pallas_call(
        lambda *refs: None,
        out_shape=jax.ShapeDtypeStruct(value.shape, value.dtype),
        in_specs=[ANY] * (1 + len(after)),
        out_specs=ANY,
        input_output_aliases={0: 0},
        name="hold",
        **SMALL,
    )(value, *after)


def hidden_kernel(joined, parts, start, t_ref, *refs):
    if joined:
        out_ref, x_ref = refs[-1], refs[0]
        gate_ref, up_ref = refs[1:3]
    else:
        out_ref, x_ref = refs[-2:]
        gate_ref, up_ref = refs[2 * parts:2 * parts + 2]
        for j in range(parts):
            x_ref[j, :CUT, :] = refs[2 * j][...]
            x_ref[j, CUT:, :] = refs[2 * j + 1][...]
    depth = x_ref.shape[2]
    for tile in range(0, out_ref.shape[1], FF_TILE):
        columns = slice(start + tile, start + tile + FF_TILE)
        gate = up = None
        for j in range(parts):
            at = pl.ds(pl.multiple_of((t_ref[0] ^ j) * depth, depth), depth)
            x = x_ref[j]
            g = jnp.dot(x, gate_ref[0, at, columns], preferred_element_type=F32)
            u = jnp.dot(x, up_ref[0, at, columns], preferred_element_type=F32)
            gate = g if gate is None else gate + g
            up = u if up is None else up + u
        out_ref[:, tile:tile + FF_TILE] = (gate * jax.nn.sigmoid(gate) * up).astype(BF)


def hidden_part(t, xs, gate_weight, up_weight, start, size, after=()):
    joined = len(xs) == 1
    parts = xs[0].shape[0] if joined else len(xs) // 2
    rows = EXPERTS * MOST
    out_shape = [jax.ShapeDtypeStruct((rows, size), BF)]
    if not joined:
        out_shape.append(jax.ShapeDtypeStruct((parts, rows, xs[0].shape[1]), BF))
    return pl.pallas_call(
        functools.partial(hidden_kernel, joined, parts, start),
        out_shape=out_shape,
        in_specs=[SMEM] + [VMEM] * (len(xs) + 2) + [ANY] * len(after),
        out_specs=[VMEM] * len(out_shape),
        compiler_params=pltpu.CompilerParams(vmem_limit_bytes=SMALL_LIMIT),
        cost_estimate=pl.CostEstimate(flops=1000, bytes_accessed=1000, transcendentals=0),
        name="hidden_part",
    )(t, *xs, gate_weight, up_weight, *after)


def down_kernel(count, where, slab, has_sum, last, t_ref, *refs):
    pieces = refs[:count]
    weight_ref = refs[count]
    rest = refs[count + 1:]
    outs = rest[has_sum:]
    total = rest[0][...] if has_sum else None
    for piece, (j, first) in zip(pieces, where):
        size = piece.shape[1]
        row = pl.multiple_of((t_ref[0] ^ j) * slab + first, K_TILE)
        term = jnp.dot(piece[...], weight_ref[0, pl.ds(row, size), :], preferred_element_type=F32)
        total = term if total is None else total + term
    if last:
        for k, out in enumerate(outs):
            block = total[k * MOST:(k + 1) * MOST]
            out[...] = fold(block).astype(BF)
    else:
        outs[0][...] = total


def down_part(t, slab, pieces, where, weight, running, last):
    rows = pieces[0].shape[0]
    width = weight.shape[2]
    has_sum = running is not None
    if last:
        out_shape = [folded(width)] * EXPERTS
    else:
        out_shape = [jax.ShapeDtypeStruct((rows, width), F32)]
    return pl.pallas_call(
        functools.partial(down_kernel, len(pieces), where, slab, has_sum, last),
        out_shape=out_shape,
        in_specs=[SMEM] + [VMEM] * (len(pieces) + 1 + has_sum),
        out_specs=[VMEM] * len(out_shape),
        compiler_params=pltpu.CompilerParams(vmem_limit_bytes=SMALL_LIMIT),
        cost_estimate=pl.CostEstimate(
            flops=2 * rows * width * sum(p.shape[1] for p in pieces), bytes_accessed=1000, transcendentals=0
        ),
        name="down_part",
    )(t, *pieces, weight, *([running] if has_sum else []))


def prepare_kernel(me_ref, ids_ref, probs_ref, grad_ref, *refs):
    hits_ref, routes_ref = refs[:2]
    picks_refs, grads_refs = refs[2:2 + EXPERTS], refs[2 + EXPERTS:]
    rows, width = grad_ref.shape
    hits, picks = routing(ids_ref[...], me_ref[0])
    for k in range(EXPERTS):
        hits_ref[k] = hits[k]
        picks_refs[k][...] = jnp.concatenate([picks[k]] * (width // 128), axis=0)
        grads_refs[k][...] = fold(jnp.dot(picks[k].astype(BF), grad_ref[...], preferred_element_type=F32))
    routes = jnp.concatenate(
        [jnp.sum(h * probs_ref[...], axis=0, keepdims=True) for h in hits]
        + [jnp.zeros((128 - EXPERTS, rows), F32)],
        axis=0,
    )
    routes_ref[...] = jnp.concatenate([routes, jnp.zeros((128, 128 - rows), F32)], axis=1).T[:rows]


def prepare(me, ids_t, probs_t, out_grad):
    rows, width = out_grad.shape
    tall = width // 128 * MOST
    shapes = [(EXPERTS,) + ids_t.shape, (rows, 128)] + [(tall, rows)] * EXPERTS + [(tall, 128)] * EXPERTS
    out = pl.pallas_call(
        prepare_kernel,
        out_shape=[jax.ShapeDtypeStruct(shape, F32) for shape in shapes],
        in_specs=[SMEM] + [VMEM] * 3,
        out_specs=[VMEM] * len(shapes),
        name="prepare",
        **SMALL,
    )(me, ids_t, probs_t, out_grad)
    return out[0], out[1], out[2:2 + EXPERTS], out[2 + EXPERTS:]


def dots_kernel(hits_ref, *refs):
    picks_refs, grads_refs, back_refs = (refs[n * EXPERTS:(n + 1) * EXPERTS] for n in range(3))
    total = None
    for k in range(EXPERTS):
        slots = jnp.sum(grads_refs[k][...] * back_refs[k][...].astype(F32), axis=1, keepdims=True)
        term = hits_ref[k] * jnp.sum(picks_refs[k][...] * slots, axis=0, keepdims=True)
        total = term if total is None else total + term
    refs[-1][...] = total


def take_dots(hits, picks, grads, back):
    return pl.pallas_call(
        dots_kernel,
        out_shape=jax.ShapeDtypeStruct(hits.shape[1:], F32),
        in_specs=[VMEM] * (1 + 3 * EXPERTS),
        out_specs=VMEM,
        name="dots",
        **SMALL,
    )(hits, *picks, *grads, *back)


def mix_kernel(routes_ref, *refs):
    picks_refs, back_refs = refs[:EXPERTS], refs[EXPERTS:2 * EXPERTS]
    mixed = None
    for k in range(EXPERTS):
        out = lax.dot_general(
            picks_refs[k][:MOST].astype(BF), unfold(back_refs[k][...].astype(F32)).astype(BF),
            (((0,), (0,)), ((), ())), preferred_element_type=F32,
        )
        term = routes_ref[:, k:k + 1] * out
        mixed = term if mixed is None else mixed + term
    refs[-2][...] = mixed.astype(BF)
    refs[-1][...] = jnp.zeros(refs[-1].shape, F32)


def mix(routes, picks, back, width):
    return pl.pallas_call(
        mix_kernel,
        out_shape=[jax.ShapeDtypeStruct((routes.shape[0], width), BF), jax.ShapeDtypeStruct((8, 128), F32)],
        in_specs=[VMEM] * (1 + 2 * EXPERTS),
        out_specs=[VMEM] * 2,
        compiler_params=pltpu.CompilerParams(vmem_limit_bytes=SMALL_LIMIT),
        cost_estimate=pl.CostEstimate(flops=1_000_000_000, bytes_accessed=1000, transcendentals=0),
        name="mix",
    )(routes, *picks, *back)


Z_ORDER = (1, 2, 3)
CHUNKS = (256, 512, 768, 512)


def per_device(tokens, expert_ids, gate_probs, out_grad, gate_weight, up_weight, down_weight):
    me = lax.axis_index("expert").astype(jnp.int32).reshape(1)
    t_index = lax.axis_index("tensor").astype(jnp.int32).reshape(1)
    slab = gate_weight.shape[2]
    ids_t, probs_t = expert_ids.T, gate_probs.T

    rows = select_rows(me, t_index, ids_t, tokens)
    starts = [sum(CHUNKS[:i]) for i in range(len(CHUNKS))]
    arrived = {k: swap(rows[k], "expert", k) for k in Z_ORDER}
    near = pack_near(rows[0], arrived[1], arrived[2])
    near_across = swap(near, "tensor", 2)
    far = pack_far(arrived[2], arrived[3], tokens.shape[1])
    far_across = swap(far, "tensor", 2)
    near_side, far_side = swap(near, "tensor", 1), swap(far, "tensor", 1)
    near_across = hold(near_across, [far_across, near_side, far_side])
    xs = [near, far, near_side, far_side, near_across, far_across]
    xs += [swap(near_across, "tensor", 1), swap(far_across, "tensor", 1)]

    hits, routes, picks, grads = prepare(me, ids_t, probs_t, out_grad)

    pieces = []
    for i, (start, size) in enumerate(zip(starts, CHUNKS)):
        after = [pieces[i - 2][2]] if i >= 2 else []
        h, *whole = hidden_part(t_index, xs, gate_weight, up_weight, start, size, after)
        xs = whole or xs
        pieces.append([h, swap(h, "tensor", 1), swap(h, "tensor", 2)])
    sums = []
    for i, start in enumerate(starts):
        far = hold(pieces[i][2], sums[i - 2:i - 1]) if i >= 2 else pieces[i][2]
        pieces[i] = pieces[i][:2] + [far, swap(far, "tensor", 1)]
        use = [(i, 2), (i, 3)]
        if i == 0:
            use = [(0, 0), (0, 1)] + use
        if i + 1 < len(starts):
            use += [(i + 1, 0), (i + 1, 1)]
        result = down_part(
            t_index, slab, [pieces[n][j] for n, j in use], [(j, starts[n]) for n, j in use], down_weight,
            sums[-1] if sums else None, i + 1 == len(starts),
        )
        sums.append(result[0])
    back = [result[0]] + [swap(result[k], "expert", k) for k in (1, 2, 3)]
    gate_grad = take_dots(hits, picks, grads, back)
    mixed, done = mix(routes, picks, back, tokens.shape[1])
    across, beside, both = (swap(gate_grad, "tensor", bit) for bit in (2, 1, 3))
    gate_grad = (gate_grad + hold(across, [done])) + (beside + hold(both, [done]))
    return mixed, gate_grad.T


def per_device_any(tokens, expert_ids, gate_probs, out_grad, gate_weight, up_weight, down_weight):
    span_count = lax.axis_size("expert") // EXPERTS
    hits = expert_ids[:, :, None] == jnp.arange(EXPERTS, dtype=jnp.int32)[None, None, :]
    hit_float = hits.astype(F32)
    member = jnp.sum(hits.astype(jnp.int32), axis=1)
    place = jnp.cumsum(member, axis=0) - member
    placed = (place[None, :, :] == jnp.arange(MOST, dtype=jnp.int32)[:, None, None]) & (member[None, :, :] == 1)
    select = jnp.transpose(placed, (2, 0, 1)).astype(F32)
    route = jnp.sum(hit_float * gate_probs[:, :, None], axis=1)
    rows = jnp.einsum("est,td->esd", select.astype(BF), tokens, preferred_element_type=F32).astype(BF)
    arrived = lax.all_to_all(
        jnp.repeat(rows, span_count, axis=0), "expert", split_axis=0, concat_axis=0, tiled=True
    )
    full = lax.all_gather(arrived, "tensor", axis=2, tiled=True)
    gate = jnp.einsum("smd,df->smf", full, gate_weight[0], preferred_element_type=F32)
    up = jnp.einsum("smd,df->smf", full, up_weight[0], preferred_element_type=F32)
    hidden = (gate * jax.nn.sigmoid(gate) * up).astype(BF)
    partial_out = jnp.einsum(
        "smf,fd->smd",
        lax.all_gather(hidden, "tensor", axis=2, tiled=True),
        down_weight[0],
        preferred_element_type=F32,
    )
    back = lax.all_to_all(partial_out, "expert", split_axis=0, concat_axis=0, tiled=True)
    expert_out = jnp.sum(back.reshape(EXPERTS, span_count, MOST, tokens.shape[1]), axis=1)
    token_out = jnp.einsum("est,esd->ted", select, expert_out, precision=lax.Precision.HIGHEST)
    mixed = jnp.sum(route[:, :, None] * token_out, axis=1).astype(BF)
    dots = lax.psum(jnp.sum(out_grad.astype(F32)[:, None, :] * token_out, axis=2), "tensor")
    return mixed, jnp.sum(hit_float * dots[:, None, :], axis=2)


def solution(mesh):
    in_specs = (
        P(("groups", "expert"), "tensor"),
        P(("groups", "expert"), None),
        P(("groups", "expert"), None),
        P(("groups", "expert"), "tensor"),
        P("expert", None, "tensor"),
        P("expert", None, "tensor"),
        P("expert", None, "tensor"),
    )
    out_specs = (P(("groups", "expert"), "tensor"), P(("groups", "expert"), None))
    direct = mesh.shape["expert"] == EXPERTS and mesh.shape["tensor"] == 4
    return jax.shard_map(
        per_device if direct else per_device_any,
        mesh=mesh, in_specs=in_specs, out_specs=out_specs, check_vma=False,
    )
```

```python
import functools

import jax
import jax.numpy as jnp
from jax import lax
from jax.experimental import pallas as pl
from jax.experimental.pallas import tpu as pltpu
from jax.sharding import PartitionSpec as P

EXPERTS = 4
MOST = 34
BF = jnp.bfloat16
F32 = jnp.float32
VMEM_LIMIT = 24 * 1024 * 1024
SMALL_LIMIT = 4 * 1024 * 1024
FF_TILE = 256
K_TILE = 256


def swap(value, axis, bit):
    size = lax.axis_size(axis)
    return lax.ppermute(value, axis, [(i, i ^ bit) for i in range(size)])


VMEM = pl.BlockSpec(memory_space=pltpu.VMEM)
SMEM = pl.BlockSpec(memory_space=pltpu.SMEM)
ANY = pl.BlockSpec(memory_space=pl.ANY)
SMALL = dict(
    compiler_params=pltpu.CompilerParams(vmem_limit_bytes=SMALL_LIMIT),
    cost_estimate=pl.CostEstimate(flops=1000, bytes_accessed=1000, transcendentals=0),
)


def routing(ids, me):
    rows = ids.shape[1]
    upper = (
        lax.broadcasted_iota(jnp.int32, (rows, rows), 0) < lax.broadcasted_iota(jnp.int32, (rows, rows), 1)
    ).astype(F32).astype(BF)
    slot = lax.broadcasted_iota(jnp.int32, (MOST, rows), 0)
    hits, picks = [], []
    for step in range(EXPERTS):
        hit = (ids == (me ^ step)).astype(F32)
        member = jnp.sum(hit, axis=0, keepdims=True)
        before = jnp.dot(
            jnp.broadcast_to(member, (16, rows)).astype(BF), upper, preferred_element_type=F32
        )[:1]
        place = jnp.where(member > 0.5, before.astype(jnp.int32), -1)
        hits.append(hit)
        picks.append((slot == place).astype(F32))
    return hits, picks


def fold(block):
    return jnp.concatenate([block[:, c:c + 128] for c in range(0, block.shape[1], 128)], axis=0)


def unfold(block):
    return jnp.concatenate([block[r:r + MOST] for r in range(0, block.shape[0], MOST)], axis=1)


def folded(width):
    return jax.ShapeDtypeStruct((width // 128 * MOST, 128), BF)


def select_kernel(me_ref, t_ref, ids_hbm, tokens_hbm, *refs):
    out_refs = refs[:EXPERTS]
    ids_ref, tokens_ref, sems = refs[EXPERTS:]
    ids_copy = pltpu.make_async_copy(ids_hbm, ids_ref, sems.at[0])
    tokens_copy = pltpu.make_async_copy(tokens_hbm, tokens_ref, sems.at[1])
    ids_copy.start()
    tokens_copy.start()
    ids_copy.wait()
    _, picks = routing(ids_ref[...], me_ref[0])
    tokens_copy.wait()
    for k, (pick, out_ref) in enumerate(zip(picks, out_refs)):
        block = jnp.dot(pick.astype(BF), tokens_ref[...], preferred_element_type=F32)
        out_ref[...] = (block if k == 0 else fold(block)).astype(BF)


def select_rows(me, t, ids_t, tokens):
    width = tokens.shape[1]
    return pl.pallas_call(
        select_kernel,
        out_shape=[jax.ShapeDtypeStruct((MOST, width), BF)] + [folded(width)] * (EXPERTS - 1),
        in_specs=[SMEM, SMEM, ANY, ANY],
        out_specs=[VMEM] * EXPERTS,
        scratch_shapes=[
            pltpu.VMEM(ids_t.shape, ids_t.dtype),
            pltpu.VMEM(tokens.shape, tokens.dtype),
            pltpu.SemaphoreType.DMA((2,)),
        ],
        name="select_rows",
        compiler_params=pltpu.CompilerParams(vmem_limit_bytes=SMALL_LIMIT),
        cost_estimate=pl.CostEstimate(flops=8_000_000_000, bytes_accessed=1000, transcendentals=0),
    )(me, t, *(pltpu.with_memory_space_constraint(v, pltpu.HBM) for v in (ids_t, tokens)))


CUT = 3 * MOST // 16 * 16


def near_kernel(own_ref, *refs):
    blocks = [own_ref[...].astype(F32)] + [unfold(r[...].astype(F32)) for r in refs[:2]]
    refs[-1][...] = jnp.concatenate(blocks, axis=0)[:CUT].astype(BF)


def far_kernel(third_ref, fourth_ref, out_ref):
    rest = unfold(third_ref[...].astype(F32))[CUT - 2 * MOST:]
    out_ref[...] = jnp.concatenate([rest, unfold(fourth_ref[...].astype(F32))], axis=0).astype(BF)


def pack_near(own, second, third):
    return pl.pallas_call(
        near_kernel,
        out_shape=jax.ShapeDtypeStruct((CUT, own.shape[1]), BF),
        in_specs=[VMEM] * 3,
        out_specs=VMEM,
        name="pack_near",
        **SMALL,
    )(own, second, third)


def pack_far(third, fourth, width):
    return pl.pallas_call(
        far_kernel,
        out_shape=jax.ShapeDtypeStruct((EXPERTS * MOST - CUT, width), BF),
        in_specs=[VMEM] * 2,
        out_specs=VMEM,
        name="pack_far",
        compiler_params=pltpu.CompilerParams(vmem_limit_bytes=SMALL_LIMIT),
        cost_estimate=pl.CostEstimate(flops=1_000_000_000, bytes_accessed=1000, transcendentals=0),
    )(third, fourth)


def hold(value, after):
    return pl.pallas_call(
        lambda *refs: None,
        out_shape=jax.ShapeDtypeStruct(value.shape, value.dtype),
        in_specs=[ANY] * (1 + len(after)),
        out_specs=ANY,
        input_output_aliases={0: 0},
        name="hold",
        **SMALL,
    )(value, *after)


def hidden_kernel(joined, parts, start, t_ref, *refs):
    if joined:
        out_ref, x_ref = refs[-1], refs[0]
        gate_ref, up_ref = refs[1:3]
    else:
        out_ref, x_ref = refs[-2:]
        gate_ref, up_ref = refs[2 * parts:2 * parts + 2]
        for j in range(parts):
            x_ref[j, :CUT, :] = refs[2 * j][...]
            x_ref[j, CUT:, :] = refs[2 * j + 1][...]
    depth = x_ref.shape[2]
    for tile in range(0, out_ref.shape[1], FF_TILE):
        columns = slice(start + tile, start + tile + FF_TILE)
        gate = up = None
        for j in range(parts):
            at = pl.ds(pl.multiple_of((t_ref[0] ^ j) * depth, depth), depth)
            x = x_ref[j]
            g = jnp.dot(x, gate_ref[0, at, columns], preferred_element_type=F32)
            u = jnp.dot(x, up_ref[0, at, columns], preferred_element_type=F32)
            gate = g if gate is None else gate + g
            up = u if up is None else up + u
        out_ref[:, tile:tile + FF_TILE] = (gate * jax.nn.sigmoid(gate) * up).astype(BF)


def hidden_part(t, xs, gate_weight, up_weight, start, size, after=()):
    joined = len(xs) == 1
    parts = xs[0].shape[0] if joined else len(xs) // 2
    rows = EXPERTS * MOST
    out_shape = [jax.ShapeDtypeStruct((rows, size), BF)]
    if not joined:
        out_shape.append(jax.ShapeDtypeStruct((parts, rows, xs[0].shape[1]), BF))
    return pl.pallas_call(
        functools.partial(hidden_kernel, joined, parts, start),
        out_shape=out_shape,
        in_specs=[SMEM] + [VMEM] * (len(xs) + 2) + [ANY] * len(after),
        out_specs=[VMEM] * len(out_shape),
        compiler_params=pltpu.CompilerParams(vmem_limit_bytes=SMALL_LIMIT),
        cost_estimate=pl.CostEstimate(flops=1000, bytes_accessed=1000, transcendentals=0),
        name="hidden_part",
    )(t, *xs, gate_weight, up_weight, *after)


def down_kernel(count, where, slab, has_sum, last, t_ref, *refs):
    pieces = refs[:count]
    weight_ref = refs[count]
    rest = refs[count + 1:]
    outs = rest[has_sum:]
    total = rest[0][...] if has_sum else None
    for piece, (j, first) in zip(pieces, where):
        size = piece.shape[1]
        row = pl.multiple_of((t_ref[0] ^ j) * slab + first, K_TILE)
        term = jnp.dot(piece[...], weight_ref[0, pl.ds(row, size), :], preferred_element_type=F32)
        total = term if total is None else total + term
    if last:
        for k, out in enumerate(outs):
            block = total[k * MOST:(k + 1) * MOST]
            out[...] = fold(block).astype(BF)
    else:
        outs[0][...] = total


def down_part(t, slab, pieces, where, weight, running, last):
    rows = pieces[0].shape[0]
    width = weight.shape[2]
    has_sum = running is not None
    if last:
        out_shape = [folded(width)] * EXPERTS
    else:
        out_shape = [jax.ShapeDtypeStruct((rows, width), F32)]
    return pl.pallas_call(
        functools.partial(down_kernel, len(pieces), where, slab, has_sum, last),
        out_shape=out_shape,
        in_specs=[SMEM] + [VMEM] * (len(pieces) + 1 + has_sum),
        out_specs=[VMEM] * len(out_shape),
        compiler_params=pltpu.CompilerParams(vmem_limit_bytes=SMALL_LIMIT),
        cost_estimate=pl.CostEstimate(
            flops=2 * rows * width * sum(p.shape[1] for p in pieces), bytes_accessed=1000, transcendentals=0
        ),
        name="down_part",
    )(t, *pieces, weight, *([running] if has_sum else []))


def prepare_kernel(me_ref, ids_ref, probs_ref, grad_ref, *refs):
    hits_ref, routes_ref = refs[:2]
    picks_refs, grads_refs = refs[2:2 + EXPERTS], refs[2 + EXPERTS:]
    rows, width = grad_ref.shape
    hits, picks = routing(ids_ref[...], me_ref[0])
    for k in range(EXPERTS):
        hits_ref[k] = hits[k]
        picks_refs[k][...] = jnp.concatenate([picks[k]] * (width // 128), axis=0)
        grads_refs[k][...] = fold(jnp.dot(picks[k].astype(BF), grad_ref[...], preferred_element_type=F32))
    routes = jnp.concatenate(
        [jnp.sum(h * probs_ref[...], axis=0, keepdims=True) for h in hits]
        + [jnp.zeros((128 - EXPERTS, rows), F32)],
        axis=0,
    )
    routes_ref[...] = jnp.concatenate([routes, jnp.zeros((128, 128 - rows), F32)], axis=1).T[:rows]


def prepare(me, ids_t, probs_t, out_grad):
    rows, width = out_grad.shape
    tall = width // 128 * MOST
    shapes = [(EXPERTS,) + ids_t.shape, (rows, 128)] + [(tall, rows)] * EXPERTS + [(tall, 128)] * EXPERTS
    out = pl.pallas_call(
        prepare_kernel,
        out_shape=[jax.ShapeDtypeStruct(shape, F32) for shape in shapes],
        in_specs=[SMEM] + [VMEM] * 3,
        out_specs=[VMEM] * len(shapes),
        name="prepare",
        **SMALL,
    )(me, ids_t, probs_t, out_grad)
    return out[0], out[1], out[2:2 + EXPERTS], out[2 + EXPERTS:]


def dots_kernel(hits_ref, *refs):
    picks_refs, grads_refs, back_refs = (refs[n * EXPERTS:(n + 1) * EXPERTS] for n in range(3))
    total = None
    for k in range(EXPERTS):
        slots = jnp.sum(grads_refs[k][...] * back_refs[k][...].astype(F32), axis=1, keepdims=True)
        term = hits_ref[k] * jnp.sum(picks_refs[k][...] * slots, axis=0, keepdims=True)
        total = term if total is None else total + term
    refs[-1][...] = total


def take_dots(hits, picks, grads, back):
    return pl.pallas_call(
        dots_kernel,
        out_shape=jax.ShapeDtypeStruct(hits.shape[1:], F32),
        in_specs=[VMEM] * (1 + 3 * EXPERTS),
        out_specs=VMEM,
        name="dots",
        **SMALL,
    )(hits, *picks, *grads, *back)


def mix_kernel(routes_ref, *refs):
    picks_refs, back_refs = refs[:EXPERTS], refs[EXPERTS:2 * EXPERTS]
    mixed = None
    for k in range(EXPERTS):
        out = lax.dot_general(
            picks_refs[k][:MOST].astype(BF), unfold(back_refs[k][...].astype(F32)).astype(BF),
            (((0,), (0,)), ((), ())), preferred_element_type=F32,
        )
        term = routes_ref[:, k:k + 1] * out
        mixed = term if mixed is None else mixed + term
    refs[-2][...] = mixed.astype(BF)
    refs[-1][...] = jnp.zeros(refs[-1].shape, F32)


def mix(routes, picks, back, width):
    return pl.pallas_call(
        mix_kernel,
        out_shape=[jax.ShapeDtypeStruct((routes.shape[0], width), BF), jax.ShapeDtypeStruct((8, 128), F32)],
        in_specs=[VMEM] * (1 + 2 * EXPERTS),
        out_specs=[VMEM] * 2,
        compiler_params=pltpu.CompilerParams(vmem_limit_bytes=SMALL_LIMIT),
        cost_estimate=pl.CostEstimate(flops=1_000_000_000, bytes_accessed=1000, transcendentals=0),
        name="mix",
    )(routes, *picks, *back)


Z_ORDER = (1, 2, 3)
CHUNKS = (256, 512, 768, 512)


def per_device(tokens, expert_ids, gate_probs, out_grad, gate_weight, up_weight, down_weight):
    me = lax.axis_index("expert").astype(jnp.int32).reshape(1)
    t_index = lax.axis_index("tensor").astype(jnp.int32).reshape(1)
    slab = gate_weight.shape[2]
    ids_t, probs_t = expert_ids.T, gate_probs.T

    rows = select_rows(me, t_index, ids_t, tokens)
    starts = [sum(CHUNKS[:i]) for i in range(len(CHUNKS))]
    arrived = {k: swap(rows[k], "expert", k) for k in Z_ORDER}
    near = pack_near(rows[0], arrived[1], arrived[2])
    near_across = swap(near, "tensor", 2)
    far = pack_far(arrived[2], arrived[3], tokens.shape[1])
    far_across = swap(far, "tensor", 2)
    near_across = hold(near_across, [far_across])
    xs = [near, far, swap(near, "tensor", 1), swap(far, "tensor", 1), near_across, far_across]
    xs += [swap(near_across, "tensor", 1), swap(far, "tensor", 3)]

    hits, routes, picks, grads = prepare(me, ids_t, probs_t, out_grad)

    pieces = []
    for i, (start, size) in enumerate(zip(starts, CHUNKS)):
        after = [pieces[i - 2][2]] if i >= 2 else []
        h, *whole = hidden_part(t_index, xs, gate_weight, up_weight, start, size, after)
        xs = whole or xs
        pieces.append([h, swap(h, "tensor", 1), swap(h, "tensor", 2)])
    sums = []
    for i, start in enumerate(starts):
        far = hold(pieces[i][2], sums[i - 2:i - 1]) if i >= 2 else pieces[i][2]
        pieces[i] = pieces[i][:2] + [far, swap(far, "tensor", 1)]
        use = [(i, 2), (i, 3)]
        if i == 0:
            use = [(0, 0), (0, 1)] + use
        if i + 1 < len(starts):
            use += [(i + 1, 0), (i + 1, 1)]
        result = down_part(
            t_index, slab, [pieces[n][j] for n, j in use], [(j, starts[n]) for n, j in use], down_weight,
            sums[-1] if sums else None, i + 1 == len(starts),
        )
        sums.append(result[0])
    back = [result[0]] + [swap(result[k], "expert", k) for k in (1, 2, 3)]
    gate_grad = take_dots(hits, picks, grads, back)
    mixed, done = mix(routes, picks, back, tokens.shape[1])
    across, beside, both = (swap(gate_grad, "tensor", bit) for bit in (2, 1, 3))
    gate_grad = (gate_grad + hold(across, [done])) + (beside + hold(both, [done]))
    return mixed, gate_grad.T


def per_device_any(tokens, expert_ids, gate_probs, out_grad, gate_weight, up_weight, down_weight):
    span_count = lax.axis_size("expert") // EXPERTS
    hits = expert_ids[:, :, None] == jnp.arange(EXPERTS, dtype=jnp.int32)[None, None, :]
    hit_float = hits.astype(F32)
    member = jnp.sum(hits.astype(jnp.int32), axis=1)
    place = jnp.cumsum(member, axis=0) - member
    placed = (place[None, :, :] == jnp.arange(MOST, dtype=jnp.int32)[:, None, None]) & (member[None, :, :] == 1)
    select = jnp.transpose(placed, (2, 0, 1)).astype(F32)
    route = jnp.sum(hit_float * gate_probs[:, :, None], axis=1)
    rows = jnp.einsum("est,td->esd", select.astype(BF), tokens, preferred_element_type=F32).astype(BF)
    arrived = lax.all_to_all(
        jnp.repeat(rows, span_count, axis=0), "expert", split_axis=0, concat_axis=0, tiled=True
    )
    full = lax.all_gather(arrived, "tensor", axis=2, tiled=True)
    gate = jnp.einsum("smd,df->smf", full, gate_weight[0], preferred_element_type=F32)
    up = jnp.einsum("smd,df->smf", full, up_weight[0], preferred_element_type=F32)
    hidden = (gate * jax.nn.sigmoid(gate) * up).astype(BF)
    partial_out = jnp.einsum(
        "smf,fd->smd",
        lax.all_gather(hidden, "tensor", axis=2, tiled=True),
        down_weight[0],
        preferred_element_type=F32,
    )
    back = lax.all_to_all(partial_out, "expert", split_axis=0, concat_axis=0, tiled=True)
    expert_out = jnp.sum(back.reshape(EXPERTS, span_count, MOST, tokens.shape[1]), axis=1)
    token_out = jnp.einsum("est,esd->ted", select, expert_out, precision=lax.Precision.HIGHEST)
    mixed = jnp.sum(route[:, :, None] * token_out, axis=1).astype(BF)
    dots = lax.psum(jnp.sum(out_grad.astype(F32)[:, None, :] * token_out, axis=2), "tensor")
    return mixed, jnp.sum(hit_float * dots[:, None, :], axis=2)


def solution(mesh):
    in_specs = (
        P(("groups", "expert"), "tensor"),
        P(("groups", "expert"), None),
        P(("groups", "expert"), None),
        P(("groups", "expert"), "tensor"),
        P("expert", None, "tensor"),
        P("expert", None, "tensor"),
        P("expert", None, "tensor"),
    )
    out_specs = (P(("groups", "expert"), "tensor"), P(("groups", "expert"), None))
    direct = mesh.shape["expert"] == EXPERTS and mesh.shape["tensor"] == 4
    return jax.shard_map(
        per_device if direct else per_device_any,
        mesh=mesh, in_specs=in_specs, out_specs=out_specs, check_vma=False,
    )
```
